32 devices in a mesh: row: 16 (over z, y, x), head: 2 (over core).
Axes of the slice: x: 2, y: 2, z: 4, core: 2. Of those that a mesh axis runs over, the one named last changes fastest.
Arguments:
- memory: float32 [16384, 172], P('row'), may hold values from -4 to 4
- sources: int32 [16, 1024], P('row'), may hold values from 0 to 1023, each once within a row
- dest_ids: int32 [16384], P('row'), may hold values from 0 to 16383
- neighbours: int32 [16384, 10], P('row'), may hold values from 0 to 16383
- delta_t: float32 [16384], P('row'), may hold values from 0.25 to 4
- nbr_delta: float32 [16384, 10], P('row'), may hold values from 0.25 to 4
- edge_feat: bfloat16 [16384, 172], P('row'), may hold values from -6 to 6
- window_count: int32 [16], P('row'), may hold values from 1 to 1024, as said below
- message_weight: float32 [688, 516], P(None, 'head'), may hold values from -0.21875 to 0.21875
- message_weight_moment: float32 [688, 516], P(None, 'head'), may hold values from -0.0009765625 to 0.0009765625
- message_weight_square: float32 [688, 516], P(None, 'head'), may hold values from 6.1035155e-10 to 6.1035155e-09
- state_weight: float32 [172, 516], P(None, 'head'), may hold values from -0.4375 to 0.4375
- state_weight_moment: float32 [172, 516], P(None, 'head'), may hold values from -0.0009765625 to 0.0009765625
- state_weight_square: float32 [172, 516], P(None, 'head'), may hold values from 6.1035155e-10 to 6.1035155e-09
- gate_bias: float32 [2, 516], P(None, 'head'), may hold values from -1.75 to 1.75
- gate_bias_moment: float32 [2, 516], P(None, 'head'), may hold values from -0.0009765625 to 0.0009765625
- gate_bias_square: float32 [2, 516], P(None, 'head'), may hold values from 6.1035155e-10 to 6.1035155e-09
- time_param: float32 [2, 172], replicated, may hold values from 0.1 to 3
- time_param_moment: float32 [2, 172], replicated, may hold values from -0.0009765625 to 0.0009765625
- time_param_square: float32 [2, 172], replicated, may hold values from 6.1035155e-10 to 6.1035155e-09
- attend_weight: float32 [3, 344, 172], P(None, None, 'head'), may hold values from -0.625 to 0.625
- attend_weight_moment: float32 [3, 344, 172], P(None, None, 'head'), may hold values from -0.0009765625 to 0.0009765625
- attend_weight_square: float32 [3, 344, 172], P(None, None, 'head'), may hold values from 6.1035155e-10 to 6.1035155e-09
- dense_first: float32 [2, 172, 172], P(None, 'head'), may hold values from -0.3125 to 0.3125
- dense_first_moment: float32 [2, 172, 172], P(None, 'head'), may hold values from -0.0009765625 to 0.0009765625
- dense_first_square: float32 [2, 172, 172], P(None, 'head'), may hold values from 6.1035155e-10 to 6.1035155e-09
- dense_second: float32 [172, 172], P(None, 'head'), may hold values from -0.4375 to 0.4375
- dense_second_moment: float32 [172, 172], P(None, 'head'), may hold values from -0.0009765625 to 0.0009765625
- dense_second_square: float32 [172, 172], P(None, 'head'), may hold values from 6.1035155e-10 to 6.1035155e-09
- target_weight: float32 [172, 172], replicated, may hold values from -0.4375 to 0.4375
- target_weight_moment: float32 [172, 172], replicated, may hold values from -0.0009765625 to 0.0009765625
- target_weight_square: float32 [172, 172], replicated, may hold values from 6.1035155e-10 to 6.1035155e-09
Outputs:
- new_memory: float32 [16384, 172], P('row', 'head')
- loss_sum: float32 [], replicated
- live_rows: float32 [], replicated
- message_weight_new: float32 [688, 516], P(None, 'head')
- message_weight_moment_new: float32 [688, 516], P(None, 'head')
- message_weight_square_new: float32 [688, 516], P(None, 'head')
- state_weight_new: float32 [172, 516], P(None, 'head')
- state_weight_moment_new: float32 [172, 516], P(None, 'head')
- state_weight_square_new: float32 [172, 516], P(None, 'head')
- gate_bias_new: float32 [2, 516], P(None, 'head')
- gate_bias_moment_new: float32 [2, 516], P(None, 'head')
- gate_bias_square_new: float32 [2, 516], P(None, 'head')
- time_param_new: float32 [2, 172], replicated
- time_param_moment_new: float32 [2, 172], replicated
- time_param_square_new: float32 [2, 172], replicated
- attend_weight_new: float32 [3, 344, 172], P(None, None, 'head')
- attend_weight_moment_new: float32 [3, 344, 172], P(None, None, 'head')
- attend_weight_square_new: float32 [3, 344, 172], P(None, None, 'head')
- dense_first_new: float32 [2, 172, 172], P(None, 'head')
- dense_first_moment_new: float32 [2, 172, 172], P(None, 'head')
- dense_first_square_new: float32 [2, 172, 172], P(None, 'head')
- dense_second_new: float32 [172, 172], P(None, 'head')
- dense_second_moment_new: float32 [172, 172], P(None, 'head')
- dense_second_square_new: float32 [172, 172], P(None, 'head')
- target_weight_new: float32 [172, 172], replicated
- target_weight_moment_new: float32 [172, 172], replicated
- target_weight_square_new: float32 [172, 172], replicated
The draws below stay inside these ranges and needn't reach their ends.
Inputs may be any that keep to these rules, and one draw needn't show every extreme that they name: Each row of sources holds every number of 0 to 1023 once. The events of row block b that count are its first window_count[b]; the last block's are all of them.
All inputs are finite; a program needn't handle non-finite values.
Results may differ from the reference program's by a relative error of at most 0.0022.
The reference program's roundings to bfloat16 on the way count: a program that leaves them out, or rounds other values in their place, can miss the bound.
Values may be sent and summed in bfloat16 or wider, within the bound.
No kernel may reach another device: no remote copies, remote signals or barrier semaphores. Data moves between devices by JAX's collectives and lax.ppermute only.
A program may use at most 256 MiB of HBM per device.

```python
import math
import jax
import jax.numpy as jnp
from jax import lax

D = 172
NB = 10
EV_DEV = 1024
EVENTS = 16384
STEP = 10
N_ROW = 16


def draw_window_count(key, part):
    key = jax.random.fold_in(key, 7)
    places = jnp.arange(N_ROW, dtype=jnp.int32)
    base_count = EV_DEV // 3 + 2 * EV_DEV // 3 * places // max(N_ROW - 1, 1)
    jitter = jax.random.randint(key, (N_ROW,), 0, EV_DEV // 8 + 1)
    counts = jnp.maximum(base_count - jitter, 1)
    return jnp.where(places == N_ROW - 1, EV_DEV, counts).astype(jnp.int32)


def touch_ends(values, key, smallest, high):
    spot = [jax.random.randint(jax.random.fold_in(key, axis), (), 0, length) for axis, length in enumerate(values.shape)]
    main_axis = values.shape.index(max(values.shape))
    neighbour = spot[:main_axis] + [(spot[main_axis] + 1) % values.shape[main_axis]] + spot[main_axis + 1:]
    return values.at[tuple(spot)].set(smallest).at[tuple(neighbour)].set(high)


def block_levels(stream_key, dims, cuts, least, top_value):
    def one(axis_at, parts):
        heights = jax.random.uniform(jax.random.fold_in(jax.random.fold_in(stream_key, 6), axis_at), (parts,), jnp.float32, least / len(cuts), top_value / len(cuts))
        return jnp.repeat(jnp.exp(heights), dims[axis_at] // parts).reshape((-1,) + (1,) * (len(dims) - axis_at - 1))

    factor_of = one(*cuts[0])
    for cut in cuts[1:]:
        factor_of = factor_of * one(*cut)
    return factor_of


def normal_values(rng, dims, scale, limit, shards=(), kind=jnp.bfloat16):
    result = jax.random.normal(rng, dims, jnp.float32) * scale
    if len(shards) > 0:
        result = block_levels(rng, dims, shards, -0.22, 0.18) * result
    return jnp.clip(result, min=-limit, max=limit).astype(kind)


def setup_inputs(seed: int = 0) -> dict:
    seeds = jax.random.split(jax.random.key(seed), 33)
    memory = normal_values(seeds[0], (EVENTS, D), 0.7, 4.0, ((0, 16),), jnp.float32)
    sources = jax.vmap(lambda own: jax.random.permutation(own, EV_DEV))(jax.random.split(seeds[1], N_ROW)).reshape((N_ROW, EV_DEV)).astype(jnp.int32)
    dest_ids = touch_ends(jax.random.randint(seeds[2], (EVENTS,), 0, EVENTS), jax.random.fold_in(seeds[2], 1), 0, EVENTS - 1).astype(jnp.int32)
    neighbours = touch_ends(jax.random.randint(seeds[3], (EVENTS, NB), 0, EVENTS), jax.random.fold_in(seeds[3], 1), 0, EVENTS - 1).astype(jnp.int32)
    delta_t = jnp.clip(jnp.exp(math.log(4.0) - 2.7725887 * jax.random.uniform(seeds[4], (EVENTS,), jnp.float32) ** block_levels(seeds[4], (EVENTS,), ((0, 16),), -0.2, 0.2)), 0.25, 4.0)
    nbr_delta = jnp.clip(jnp.exp(math.log(4.0) - 2.7725887 * jax.random.uniform(seeds[5], (EVENTS, NB), jnp.float32) ** block_levels(seeds[5], (EVENTS, NB), ((0, 16),), -0.2, 0.2)), 0.25, 4.0)
    edge_feat = normal_values(seeds[6], (EVENTS, D), 1.0, 6.0, ((0, 16),))
    window_count = draw_window_count(jax.random.fold_in(seeds[32], 71), 0)
    message_weight = normal_values(seeds[8], (4 * D, 3 * D), (4 * D) ** -0.5, 0.21875, ((1, 2),), jnp.float32)
    message_weight_moment = normal_values(seeds[9], (4 * D, 3 * D), (0.02 * (EV_DEV * N_ROW) ** -0.5), 0.0009765625, ((1, 2),), jnp.float32)
    message_weight_square = jnp.clip(jnp.exp(math.log(6.103515470812226e-09) - 2.3025851 * jax.random.uniform(seeds[10], (4 * D, 3 * D), jnp.float32) ** block_levels(seeds[10], (4 * D, 3 * D), ((1, 2),), -0.2, 0.2)), 6.103515470812226e-10, 6.103515470812226e-09)
    state_weight = normal_values(seeds[11], (D, 3 * D), D ** -0.5, 0.4375, ((1, 2),), jnp.float32)
    state_weight_moment = normal_values(seeds[12], (D, 3 * D), (0.02 * (EV_DEV * N_ROW) ** -0.5), 0.0009765625, ((1, 2),), jnp.float32)
    state_weight_square = jnp.clip(jnp.exp(math.log(6.103515470812226e-09) - 2.3025851 * jax.random.uniform(seeds[13], (D, 3 * D), jnp.float32) ** block_levels(seeds[13], (D, 3 * D), ((1, 2),), -0.2, 0.2)), 6.103515470812226e-10, 6.103515470812226e-09)
    gate_bias = normal_values(seeds[14], (2, 3 * D), 0.3, 1.75, ((1, 2),), jnp.float32)
    gate_bias_moment = normal_values(seeds[15], (2, 3 * D), (0.02 * (EV_DEV * N_ROW) ** -0.5), 0.0009765625, ((1, 2),), jnp.float32)
    gate_bias_square = jnp.clip(jnp.exp(math.log(6.103515470812226e-09) - 2.3025851 * jax.random.uniform(seeds[16], (2, 3 * D), jnp.float32) ** block_levels(seeds[16], (2, 3 * D), ((1, 2),), -0.2, 0.2)), 6.103515470812226e-10, 6.103515470812226e-09)
    time_param = jnp.clip(jnp.exp(jax.random.uniform(seeds[17], (2, D), jnp.float32, math.log(0.1), math.log(3.0))), 0.1, 3.0)
    time_param_moment = normal_values(seeds[18], (2, D), (0.02 * (EV_DEV * N_ROW) ** -0.5), 0.0009765625, (), jnp.float32)
    time_param_square = jnp.clip(jnp.exp(jax.random.uniform(seeds[19], (2, D), jnp.float32, math.log(6.103515470812226e-10), math.log(6.103515470812226e-09))), 6.103515470812226e-10, 6.103515470812226e-09)
    attend_weight = normal_values(seeds[20], (3, 2 * D, D), (D // 2) ** -0.5, 0.625, ((2, 2),), jnp.float32)
    attend_weight_moment = normal_values(seeds[21], (3, 2 * D, D), (0.02 * (EV_DEV * N_ROW) ** -0.5), 0.0009765625, ((2, 2),), jnp.float32)
    attend_weight_square = jnp.clip(jnp.exp(math.log(6.103515470812226e-09) - 2.3025851 * jax.random.uniform(seeds[22], (3, 2 * D, D), jnp.float32) ** block_levels(seeds[22], (3, 2 * D, D), ((2, 2),), -0.2, 0.2)), 6.103515470812226e-10, 6.103515470812226e-09)
    dense_first = normal_values(seeds[23], (2, D, D), (2 * D) ** -0.5, 0.3125, ((1, 2),), jnp.float32)
    dense_first_moment = normal_values(seeds[24], (2, D, D), (0.02 * (EV_DEV * N_ROW) ** -0.5), 0.0009765625, ((1, 2),), jnp.float32)
    dense_first_square = jnp.clip(jnp.exp(math.log(6.103515470812226e-09) - 2.3025851 * jax.random.uniform(seeds[25], (2, D, D), jnp.float32) ** block_levels(seeds[25], (2, D, D), ((1, 2),), -0.2, 0.2)), 6.103515470812226e-10, 6.103515470812226e-09)
    dense_second = normal_values(seeds[26], (D, D), D ** -0.5, 0.4375, ((1, 2),), jnp.float32)
    dense_second_moment = normal_values(seeds[27], (D, D), (0.02 * (EV_DEV * N_ROW) ** -0.5), 0.0009765625, ((1, 2),), jnp.float32)
    dense_second_square = jnp.clip(jnp.exp(math.log(6.103515470812226e-09) - 2.3025851 * jax.random.uniform(seeds[28], (D, D), jnp.float32) ** block_levels(seeds[28], (D, D), ((1, 2),), -0.2, 0.2)), 6.103515470812226e-10, 6.103515470812226e-09)
    target_weight = normal_values(seeds[29], (D, D), D ** -0.5, 0.4375, (), jnp.float32)
    target_weight_moment = normal_values(seeds[30], (D, D), (0.02 * (EV_DEV * N_ROW) ** -0.5), 0.0009765625, (), jnp.float32)
    target_weight_square = jnp.clip(jnp.exp(jax.random.uniform(seeds[31], (D, D), jnp.float32, math.log(6.103515470812226e-10), math.log(6.103515470812226e-09))), 6.103515470812226e-10, 6.103515470812226e-09)
    return dict(memory=memory, sources=sources, dest_ids=dest_ids, neighbours=neighbours, delta_t=delta_t, nbr_delta=nbr_delta, edge_feat=edge_feat, window_count=window_count, message_weight=message_weight, message_weight_moment=message_weight_moment, message_weight_square=message_weight_square, state_weight=state_weight, state_weight_moment=state_weight_moment, state_weight_square=state_weight_square, gate_bias=gate_bias, gate_bias_moment=gate_bias_moment, gate_bias_square=gate_bias_square, time_param=time_param, time_param_moment=time_param_moment, time_param_square=time_param_square, attend_weight=attend_weight, attend_weight_moment=attend_weight_moment, attend_weight_square=attend_weight_square, dense_first=dense_first, dense_first_moment=dense_first_moment, dense_first_square=dense_first_square, dense_second=dense_second, dense_second_moment=dense_second_moment, dense_second_square=dense_second_square, target_weight=target_weight, target_weight_moment=target_weight_moment, target_weight_square=target_weight_square)


@jax.custom_vjp
def low(v):
    return lax.optimization_barrier(v.astype(jnp.bfloat16)).astype(jnp.float32)

@jax.custom_vjp
def low_back(v):
    return v

def low_keep(v):
    return (low(v), None)

def low_pass(kept, grad):
    return (grad,)

def back_keep(v):
    return (v, None)

def back_low(kept, grad):
    return (low(grad),)
low.defvjp(low_keep, low_pass)
low_back.defvjp(back_keep, back_low)
LOGIT_SCALE = 0.25
BETA_ONE = 0.9
BETA_TWO = 0.999
RATE = 0.05
EPSILON = 1e-08
HIGHEST = lax.Precision.HIGHEST

def matmul(left_side, right_side):
    return jnp.dot(left_side, right_side, precision=HIGHEST)

def encode(times, time_param):
    return jnp.cos(times[..., None] * time_param[0] + time_param[1])

def adam_step(master, moment, square, gradient):
    moment_new = BETA_ONE * moment + (1.0 - BETA_ONE) * gradient
    square_new = BETA_TWO * square + (1.0 - BETA_TWO) * gradient * gradient
    master_new = master - RATE * (moment_new / (1.0 - BETA_ONE ** STEP)) / (jnp.sqrt(square_new / (1.0 - BETA_TWO ** STEP)) + EPSILON)
    return (master_new, moment_new, square_new)

def event_block(params, memory_low, block_in):
    message_weight, state_weight, gate_bias, time_param, attend_weight, dense_first, dense_second, target_weight = params
    source_state, dest_ids, neighbours, delta_t, nbr_delta, edge_feat = block_in
    rows_here, model_width = source_state.shape
    head_size = model_width // 2
    source_low = low(source_state)
    dest_state = memory_low[dest_ids]
    message = jnp.concatenate([source_low, dest_state, low(encode(delta_t, time_param)), edge_feat], 1)
    gate_in = low_back(matmul(message, low(message_weight)) + gate_bias[0]).reshape(rows_here, 2, 3, head_size)
    gate_state = low_back(matmul(source_low, low(state_weight)) + gate_bias[1]).reshape(rows_here, 2, 3, head_size)
    reset_gate = jax.nn.sigmoid(gate_in[:, :, 0] + gate_state[:, :, 0])
    update = jax.nn.sigmoid(gate_in[:, :, 1] + gate_state[:, :, 1])
    candidate = jnp.tanh(gate_in[:, :, 2] + reset_gate * gate_state[:, :, 2])
    fresh_state = ((1.0 - update) * candidate + update * source_state.reshape(rows_here, 2, head_size)).reshape(rows_here, model_width)
    fresh_low = low(fresh_state)
    zero_code = jnp.broadcast_to(low(jnp.cos(time_param[1])), (rows_here, model_width))
    query_in = jnp.concatenate([fresh_low, zero_code], 1)
    queries = low_back(matmul(query_in, low(attend_weight[0]))).reshape(rows_here, 2, head_size)
    nbr_in = jnp.concatenate([memory_low[neighbours], low(encode(nbr_delta, time_param))], 2)
    key_vecs = low_back(jnp.einsum('bjc,cd->bjd', nbr_in, low(attend_weight[1]), precision=HIGHEST))
    value_vecs = low_back(jnp.einsum('bjc,cd->bjd', nbr_in, low(attend_weight[2]), precision=HIGHEST))
    key_vecs = key_vecs.reshape(rows_here, NB, 2, head_size)
    value_vecs = value_vecs.reshape(rows_here, NB, 2, head_size)
    scores = jnp.einsum('bhd,bjhd->bhj', queries, key_vecs, precision=HIGHEST) / math.sqrt(head_size)
    attn_probs = jax.nn.softmax(scores, axis=-1)
    attended = jnp.einsum('bhj,bjhd->bhd', attn_probs, value_vecs, precision=HIGHEST).reshape(rows_here, model_width)
    hidden = low_back(matmul(low(attended), low(dense_first[0])) + matmul(fresh_low, low(dense_first[1])))
    mixed_low = low(jax.nn.silu(hidden))
    embedding = low_back(low(matmul(mixed_low, low(dense_second))))
    dest_key = low(matmul(dest_state, low(target_weight)))
    return (fresh_state, embedding, dest_key)

def forward(params, memory, global_rows, dest_ids, neighbours, delta_t, nbr_delta, edge_feat, live_float):
    model_width = memory.shape[1]
    memory_low = low(memory)

    def shaped(array):
        return array.reshape((N_ROW, EV_DEV) + array.shape[1:])

    def one_block(block_in):
        return event_block(params, memory_low, block_in)
    block_all = (shaped(memory[global_rows]), shaped(dest_ids), shaped(neighbours), shaped(delta_t), shaped(nbr_delta), shaped(edge_feat))
    fresh_state, embedding, dest_key = lax.map(jax.checkpoint(one_block), block_all)
    dest_key = dest_key.reshape(EVENTS, model_width)

    def loss_rows(block_in):
        embed_rows, row_start, weight_rows = block_in
        logits = low_back(LOGIT_SCALE * matmul(embed_rows, dest_key.T))
        log_total = jax.nn.logsumexp(logits, axis=1)
        positions = row_start + jnp.arange(embed_rows.shape[0], dtype=jnp.int32)
        target = jnp.take_along_axis(logits, positions[:, None], axis=1)[:, 0]
        return jnp.sum((log_total - target) * weight_rows)
    starts = jnp.arange(N_ROW, dtype=jnp.int32) * EV_DEV
    pieces = lax.map(jax.checkpoint(loss_rows), (embedding, starts, shaped(live_float)))
    return (jnp.sum(pieces), fresh_state.reshape(EVENTS, model_width))

def reference(memory, sources, dest_ids, neighbours, delta_t, nbr_delta, edge_feat, window_count, message_weight, message_weight_moment, message_weight_square, state_weight, state_weight_moment, state_weight_square, gate_bias, gate_bias_moment, gate_bias_square, time_param, time_param_moment, time_param_square, attend_weight, attend_weight_moment, attend_weight_square, dense_first, dense_first_moment, dense_first_square, dense_second, dense_second_moment, dense_second_square, target_weight, target_weight_moment, target_weight_square):
    live_mask = (jnp.arange(EV_DEV, dtype=jnp.int32)[None, :] < window_count[:, None]).reshape(EVENTS)
    live_float = live_mask.astype(jnp.float32)
    live_rows = jnp.sum(live_float)
    global_rows = (jnp.arange(N_ROW, dtype=jnp.int32)[:, None] * EV_DEV + sources).reshape(EVENTS)
    params = (message_weight, state_weight, gate_bias, time_param, attend_weight, dense_first, dense_second, target_weight)
    edge_wide = edge_feat.astype(jnp.float32)

    def objective(weights):
        loss_sum, fresh_state = forward(weights, memory, global_rows, dest_ids, neighbours, delta_t, nbr_delta, edge_wide, live_float)
        return (loss_sum / live_rows, (loss_sum, fresh_state))
    objective_value, pullback, aux_pair = jax.vjp(objective, params, has_aux=True)
    loss_sum, fresh_state = aux_pair
    gradients = pullback(jnp.ones_like(objective_value))[0]
    old_rows = memory[global_rows]
    new_memory = memory.at[global_rows].set(jnp.where(live_mask[:, None], fresh_state, old_rows))
    moments = (message_weight_moment, state_weight_moment, gate_bias_moment, time_param_moment, attend_weight_moment, dense_first_moment, dense_second_moment, target_weight_moment)
    squares = (message_weight_square, state_weight_square, gate_bias_square, time_param_square, attend_weight_square, dense_first_square, dense_second_square, target_weight_square)
    updated = []
    for master, moment, square, gradient in zip(params, moments, squares, gradients):
        updated.extend(adam_step(master, moment, square, gradient))
    return (new_memory, loss_sum, live_rows, updated[0], updated[1], updated[2], updated[3], updated[4], updated[5], updated[6], updated[7], updated[8], updated[9], updated[10], updated[11], updated[12], updated[13], updated[14], updated[15], updated[16], updated[17], updated[18], updated[19], updated[20], updated[21], updated[22], updated[23])
```

```python
import functools
import math

import jax
import jax.numpy as jnp
from jax import lax
from jax.experimental import pallas as pl
from jax.experimental.pallas import tpu as pltpu
from jax.sharding import PartitionSpec as P

STEP = 10
LOGIT_SCALE = 0.25
BETA_ONE = 0.9
BETA_TWO = 0.999
RATE = 0.05
EPSILON = 1e-08
BF = jnp.bfloat16
F32 = jnp.float32
PLANE = 4
PAD = 88
LO_BASE = 256
VMEM_LIMIT = 58 * 2**20
VMEM_WHOLE = 62 * 2**20
TABLE_ROWS_MAX = 16384


def nn(a, b):
    return jnp.dot(a, b, preferred_element_type=F32)


def nt(a, b):
    return lax.dot_general(a, b, (((1,), (1,)), ((), ())), preferred_element_type=F32)


def tn(a, b):
    return lax.dot_general(a, b, (((0,), (0,)), ((), ())), preferred_element_type=F32)


def split3(x):
    first = x.astype(BF)
    rest = x - first.astype(F32)
    second = rest.astype(BF)
    third = (rest - second.astype(F32)).astype(BF)
    return first, second, third


def sin_cos(x):
    turns = jnp.floor(x * (1.0 / math.pi) + 0.5)
    r = ((x - turns * 3.140625) - turns * 0.0009679794311523438) + turns * 3.2584135922775204e-07
    sign = 1.0 - 2.0 * (turns - 2.0 * jnp.floor(turns * 0.5))
    r2 = r * r
    s = SIN[4]
    for k in (3, 2, 1, 0):
        s = s * r2 + SIN[k]
    c = COS[5]
    for k in (4, 3, 2, 1, 0):
        c = c * r2 + COS[k]
    return sign * (r * s), sign * c


SIN = (
    0.9999999956301436,
    -0.16666657831257647,
    0.008333047252581481,
    -0.00019808792312667284,
    2.6045791061554316e-06,
)
COS = (
    0.9999999997746029,
    -0.49999999344091517,
    0.0416666357232742,
    -0.0013888354556677485,
    2.4759808628775167e-05,
    -2.604520000579671e-07,
)


def vmem_call(kernel, out_shape, in_spaces, scratch=(), limit=VMEM_LIMIT, flops=0, nbytes=0):
    spaces = {"s": pltpu.SMEM, "v": pltpu.VMEM, "a": pl.ANY}
    return pl.pallas_call(
        kernel,
        out_shape=out_shape,
        in_specs=[pl.BlockSpec(memory_space=spaces[s]) for s in in_spaces],
        out_specs=jax.tree.map(lambda _: pl.BlockSpec(memory_space=pltpu.VMEM), out_shape),
        scratch_shapes=list(scratch),
        compiler_params=pltpu.CompilerParams(vmem_limit_bytes=limit),
        cost_estimate=pl.CostEstimate(flops=flops, bytes_accessed=nbytes, transcendentals=0),
    )


def shape(*dims, dtype=F32):
    return jax.ShapeDtypeStruct(dims, dtype)


def codes_kernel(mem, src, delta, ndelta, tcol, srct, code_d, sin_d, code_n, sin_n):
    model_width, rows = mem.shape
    events = src.shape[1]
    nbrs = ndelta.shape[0]
    pick = (lax.broadcasted_iota(jnp.int32, (rows, events), 0) == src[...]).astype(BF)
    parts = split3(mem[...])
    srct[...] = nn(parts[0], pick) + nn(parts[1], pick) + nn(parts[2], pick)
    freq, phase = tcol[:, 0:1], tcol[:, 1:2]
    sin_v, cos_v = sin_cos(delta[...] * freq + phase)
    code_d[...] = cos_v.astype(BF)
    sin_d[...] = sin_v

    def body(j, carry):
        cols = pl.ds(pl.multiple_of(j * events, events), events)
        s, c = sin_cos(ndelta[pl.ds(j, 1), :] * freq + phase)
        code_n[:, cols] = c.astype(BF)
        sin_n[:, cols] = s
        return carry

    lax.fori_loop(0, nbrs, body, 0)


def weights_kernel(
    meta, mw, mw_o, sw, sw_o, aw, aw_o, df, df_o, ds, ds_o, tw,
    o_m, o_s, o_q, o_kvm, o_kvc, o_kvct, o_f, o_ft, o_d, o_dt, o_tt,
):
    head = meta[1]
    width = tw.shape[0]
    units = width // 2

    def put(h, mw, sw, aw, df, ds):
        o_m[h] = mw[...].astype(BF)
        o_s[h] = sw[...].T.astype(BF)
        o_q[h] = aw[0].astype(BF)
        zero = jnp.zeros((PAD - units, 2 * width), F32)
        pair = jnp.concatenate([aw[1], zero, aw[2], zero], 0)
        wide = jnp.concatenate(
            [pair[:, :width], jnp.zeros((2 * PAD, 256 - width), F32)], 1
        )
        rows = pl.ds(pl.multiple_of(h * 2 * PAD, 2 * PAD), 2 * PAD)
        o_kvm[rows] = wide.astype(BF)
        code = pair[:, width:]
        o_kvc[rows] = code.astype(BF)
        o_kvct[h] = code.T.astype(BF)
        for i in range(2):
            o_f[i, h] = df[i].astype(BF)
            o_ft[i, h] = df[i].T.astype(BF)
        o_d[h] = ds[...].astype(BF)
        o_dt[h] = ds[...].T.astype(BF)

    put(head, mw, sw, aw, df, ds)
    put(1 - head, mw_o, sw_o, aw_o, df_o, ds_o)
    o_tt[...] = tw[...].T.astype(BF)


def chunk_rows(mem_a, mem_b, c, planes, meta, events):
    lo = lax.rem(c, PLANE)
    rest = lax.div(c, PLANE)
    hi = lax.rem(rest, planes)
    half = lax.div(rest, planes)
    first = mem_a[half, lo, hi]
    second = mem_b[half, hi, lo]
    row = meta[0] ^ (hi * PLANE + lo)
    base = row * (2 * events) + (meta[1] ^ half) * events
    return jnp.concatenate([first, second], 0), base, half


def step_kernel(
    planes, use_table,
    meta, idx, mem_a, mem_b, srct, code_d, sin_d, code_n, sin_n, edge, delta, ndelta, tcol, bias,
    w_m, w_s, w_q, w_kvm, w_kvc, w_kvct, w_f, w_ft, w_d, w_dt, w_tt, gathered_in, wcount,
    o_fresh, o_pack,
    near, msg, qin, emb, keyt, count, stat, scores, probs, fresh_s, att_s, gates, acc_m, tgrad,
):
    width, events = srct.shape
    units = width // 2
    nbrs = ndelta.shape[0]
    chunks = 2 * planes * PLANE
    lookups = (nbrs + 1) * events
    scale = 1.0 / math.sqrt(units)
    row_pos, head = meta[0], meta[1]
    hi_rows = count.shape[0]

    count[...] = jnp.zeros_like(count)
    stat[...] = jnp.zeros_like(stat)
    target_t = w_tt[...]

    def per_chunk(c, table):
        x, base, half = chunk_rows(mem_a, mem_b, c, planes, meta, events)
        wide = x.astype(F32)
        if use_table:
            keyt[c] = nn(target_t, x[:width]).astype(BF)
        id_hi = wide[width : width + 1].astype(jnp.int32)
        id_lo = wide[width + 1 : width + 2].astype(jnp.int32)
        hot_hi = (lax.broadcasted_iota(jnp.int32, (hi_rows, events), 0) == id_hi).astype(BF)
        hot_lo = (lax.broadcasted_iota(jnp.int32, (LO_BASE, events), 0) == id_lo).astype(BF)
        count[...] += nt(hot_hi, hot_lo)
        here = (wide[width + 2 : width + 3] * LO_BASE + wide[width + 3 : width + 4])[:, :128]
        stat[0:1, :] += jnp.where(half == 0, here, 0.0)
        if table is not None:
            turned = wide.T
            table[pl.ds(pl.multiple_of(2 * base, 2), events, stride=2), :] = turned[:, :128]
            table[pl.ds(2 * base + 1, events, stride=2), :] = jnp.concatenate(
                [turned[:, 128:], jnp.zeros((events, 256 - wide.shape[0]), F32)], 1
            )

    def gather_rows(table, gathered):
        lax.fori_loop(0, chunks, lambda c, s: (per_chunk(c, table), s)[1], 0)
        unroll = 32

        def body(i, carry):
            for u in range(unroll):
                k = i * unroll + u
                gathered[pl.ds(pl.multiple_of(2 * k, 2), 2), :] = table[
                    pl.ds(pl.multiple_of(idx[k], 2), 2), :
                ]
            return carry

        lax.fori_loop(0, lookups // unroll, body, 0)
        for j in range(nbrs + 1):
            low = gathered[pl.ds(2 * j * events, events, stride=2), :]
            high = gathered[pl.ds(2 * j * events + 1, events, stride=2), :]
            near[pl.ds(j * events, events), :] = jnp.concatenate([low, high], 1).astype(BF)

    if use_table:
        pl.run_scoped(
            gather_rows,
            pltpu.VMEM((2 * chunks * events, 128), F32),
            pltpu.VMEM((2 * lookups, 128), F32),
        )
    else:
        lax.fori_loop(0, chunks, lambda c, s: (per_chunk(c, None), s)[1], 0)
        near = gathered_in
    count[...] = jnp.where(count[...] > 0.5, jnp.log(jnp.maximum(count[...], 1.0)), -1e30)
    live_rows = stat[0:1, 0:1]

    def rest(kvt, pair):
        dest = near[pl.ds(nbrs * events, events), :]
        dest_t = dest.astype(F32).T[:width]
        msg[0:width] = srct[...]
        msg[width : 2 * width] = dest_t
        msg[2 * width : 3 * width] = code_d[...].astype(F32)
        msg[3 * width : 4 * width] = edge[...].astype(F32)
        message = msg[...].astype(BF)
        src_low = srct[...].astype(BF)
        dest_key = nn(target_t, dest_t.astype(BF)).astype(BF)

        def gate_values(h):
            gate_in = nn(w_m[h], message) + bias[h, :, 0:1]
            gate_state = nn(w_s[h], src_low) + bias[h, :, 1:2]
            reset = jax.nn.sigmoid(gate_in[:units] + gate_state[:units])
            update = jax.nn.sigmoid(
                gate_in[units : 2 * units] + gate_state[units : 2 * units]
            )
            state_c = gate_state[2 * units :]
            candidate = jnp.tanh(gate_in[2 * units :] + reset * state_c)
            return reset, update, candidate, state_c

        for h in range(2):
            reset, update, candidate, state_c = gate_values(h)
            for k, v in enumerate((reset, update, candidate, state_c)):
                gates[h, k] = v
            fresh = (1.0 - update) * candidate + update * srct[h * units : (h + 1) * units]
            o_fresh[h] = fresh
            qin[h * units : (h + 1) * units] = fresh
        _, zero_cos = sin_cos(tcol[...])
        zero_sin, _ = sin_cos(tcol[...])
        qin[width : 2 * width] = jnp.broadcast_to(zero_cos[:, 1:2], (width, events))
        query_in = qin[...].astype(BF)
        fresh_low = query_in[:width]

        def project(j, carry):
            cols = pl.ds(pl.multiple_of(j * events, events), events)
            kvt[:, cols] = nt(w_kvm[...], near[cols, :]) + nn(w_kvc[...], code_n[:, cols])
            return carry

        lax.fori_loop(0, nbrs, project, 0)
        attended_low = []
        for h in range(2):
            key_at, value_at = h * 2 * PAD, h * 2 * PAD + PAD
            queries = nn(w_q[h], query_in)
            fresh_s[h, :units] = queries
            for j in range(nbrs):
                cols = pl.ds(j * events, events)
                scores[j : j + 1] = (
                    jnp.sum(queries * kvt[key_at : key_at + units, cols], 0, keepdims=True) * scale
                )
            score = scores[0:nbrs]
            grown = jnp.exp(score - jnp.max(score, 0, keepdims=True))
            prob = grown / jnp.sum(grown, 0, keepdims=True)
            probs[h, 0:nbrs] = prob
            total = jnp.zeros((units, events), F32)
            for j in range(nbrs):
                cols = pl.ds(j * events, events)
                total = total + prob[j : j + 1] * kvt[value_at : value_at + units, cols]
            att_s[h, :units] = total
            attended_low.append(total.astype(BF))
        fresh_lows = [qin[h * units : (h + 1) * units].astype(BF) for h in range(2)]
        hidden = (nn(w_ft[0, 0], attended_low[0]) + nn(w_ft[0, 1], attended_low[1])) + (
            nn(w_ft[1, 0], fresh_lows[0]) + nn(w_ft[1, 1], fresh_lows[1])
        )
        sigmoid_h = jax.nn.sigmoid(hidden)
        mixed_low = (hidden * sigmoid_h).astype(BF)
        emb_halves = [nn(w_dt[h], mixed_low) for h in range(2)]
        emb[0:units] = emb_halves[0]
        emb[units:width] = emb_halves[1]
        emb_low = emb[...].astype(BF)
        emb_rows = (LOGIT_SCALE * emb_low.astype(F32)).T.astype(BF)
        own_logit = LOGIT_SCALE * jnp.sum(
            emb_low.astype(F32) * dest_key.astype(F32), 0, keepdims=True
        )

        group = 4 if use_table else 2

        def soft_section(logits, acc, top, total):
            top[...] = jnp.full_like(top, -1e30)
            total[...] = jnp.zeros_like(total)
            acc[...] = jnp.zeros_like(acc)

            def body(g, carry):
                parts = []
                for s in range(group):
                    c = g * group + s
                    x, base, _ = chunk_rows(mem_a, mem_b, c, planes, meta, events)
                    parts.append(x)
                    at = lax.div(base, LO_BASE)
                    shift = jnp.concatenate(
                        [count[pl.ds(at + k, 1), :] for k in range(events // LO_BASE)], 1
                    )
                    keys = keyt[c] if use_table else nn(target_t, x[:width]).astype(BF)
                    logits[:, s * events : (s + 1) * events] = nn(emb_rows, keys) + shift
                old = top[:, 0:1]
                new = jnp.maximum(old, jnp.max(logits[...], 1, keepdims=True))
                grown = jnp.exp(logits[...] - new)
                fade = jnp.exp(old - new)
                total[...] = total[...] * fade + jnp.sum(grown, 1, keepdims=True)
                top[...] = jnp.broadcast_to(new, top.shape)
                low = grown.astype(BF)
                more = nt(low[:, 0:events], parts[0])
                for s in range(1, group):
                    more = more + nt(low[:, s * events : (s + 1) * events], parts[s])
                acc[...] = acc[...] * fade + more
                return carry

            lax.fori_loop(0, chunks // group, body, 0)
            acc_m[...] = (acc[...] / total[:, 0:1]).T
            stat[8:16, :] = jnp.zeros((8, 128), F32)
            probs[2] = jnp.broadcast_to(top[:, 0:1] + jnp.log(total[:, 0:1]), (events, 128)).T[:16]

        pl.run_scoped(
            soft_section,
            pltpu.VMEM((events, group * events), F32),
            pltpu.VMEM((events, mem_a.shape[3] + mem_b.shape[3]), F32),
            pltpu.VMEM((events, 128), F32),
            pltpu.VMEM((events, 128), F32),
        )
        log_total = probs[2, 0:1]
        position = lax.broadcasted_iota(jnp.int32, (1, events), 1) + head * events
        live = (position < wcount[0]).astype(F32)
        loss = jnp.sum((log_total - own_logit) * live, 1, keepdims=True)
        weight = live / live_rows
        own_prob = jnp.exp(own_logit - log_total)
        own_grad = ((own_prob - 1.0) * weight).astype(BF).astype(F32) - own_prob * weight
        mean_mem = acc_m[:width]
        spread = weight * mean_mem + own_grad * dest_t
        parts = split3(spread)
        target_grad = LOGIT_SCALE * (nt(parts[0], emb_low) + nt(parts[1], emb_low) + nt(parts[2], emb_low))
        parts = split3(mean_mem)
        mean_key = nn(target_t, parts[0]) + nn(target_t, parts[1]) + nn(target_t, parts[2])
        emb_grad = LOGIT_SCALE * (weight * mean_key + own_grad * dest_key.astype(F32))

        o_pack[...] = jnp.zeros_like(o_pack)
        row_qk, row_vf, row_sd, row_t, row_b = pack_rows(units)

        def slot(h):
            return h ^ head

        emb_grad_low = [emb_grad[h * units : (h + 1) * units].astype(BF) for h in range(2)]
        mixed_grad = nn(w_d[0], emb_grad_low[0]) + nn(w_d[1], emb_grad_low[1])
        hidden_grad = (mixed_grad * sigmoid_h * (1.0 + hidden * (1.0 - sigmoid_h))).astype(BF)
        for h in range(2):
            second = nt(mixed_low, emb_grad_low[h])
            place = slot(h)
            o_pack[place, row_sd : row_sd + units, 3 * units : 4 * units] = second[:units]
            o_pack[place, row_sd : row_sd + units, 7 * units : 8 * units] = second[units:]
            for i, v in enumerate((attended_low[h], fresh_lows[h])):
                o_pack[place, row_vf : row_vf + units, (2 + i) * width : (3 + i) * width] = nt(
                    v, hidden_grad
                )
            quarter = units // 2
            for k in range(2):
                o_pack[place, row_t : row_t + quarter, k * width : (k + 1) * width] = target_grad[
                    h * units + k * quarter : h * units + (k + 1) * quarter
                ]

        tgrad[...] = jnp.zeros_like(tgrad)
        query_lows = []
        prob_terms = []
        att_grads = []
        for h in range(2):
            value_at = h * 2 * PAD + PAD
            att_grad = nn(w_f[0, h], hidden_grad)
            prob = probs[h, 0:nbrs]
            for j in range(nbrs):
                cols = pl.ds(j * events, events)
                scores[j : j + 1] = jnp.sum(
                    att_grad * kvt[value_at : value_at + units, cols], 0, keepdims=True
                )
            prob_grad = scores[0:nbrs]
            prob_terms.append(prob * (prob_grad - jnp.sum(prob * prob_grad, 0, keepdims=True)))
            att_grads.append(att_grad)
            total = jnp.zeros((units, events), F32)
            key_at = h * 2 * PAD
            for j in range(nbrs):
                cols = pl.ds(j * events, events)
                total = total + prob_terms[h][j : j + 1] * kvt[key_at : key_at + units, cols]
            query_lows.append((total * scale).astype(BF))
        fill = jnp.zeros((PAD - units, events), F32)
        for j in range(nbrs):
            cols = pl.ds(j * events, events)
            pieces = []
            for h in range(2):
                pieces += [
                    (prob_terms[h][j : j + 1] * scale) * fresh_s[h, :units], fill,
                    probs[h, j : j + 1] * att_grads[h], fill,
                ]
            pair_j = jnp.concatenate(pieces, 0).astype(BF)
            pair[:, cols] = pair_j
            code_grad = nn(w_kvct[0], pair_j[: 2 * PAD]) + nn(w_kvct[1], pair_j[2 * PAD :])
            slope = sin_n[:, cols] * code_grad
            tgrad[1, :width] -= slope
            tgrad[0, :width] -= slope * ndelta[j : j + 1]
        near_grad = nn(pair[...], near[pl.ds(0, nbrs * events), :])
        code_wgrad = nt(pair[...], code_n[...])
        for h in range(2):
            place = slot(h)
            base = h * 2 * PAD
            query_grad = nt(query_lows[h], query_in)
            o_pack[place, row_qk : row_qk + units, 0 : 2 * width] = query_grad
            for k, (row, lane) in enumerate(((row_qk, 2 * width), (row_vf, 0))):
                at = base + k * PAD
                o_pack[place, row : row + units, lane : lane + width] = near_grad[
                    at : at + units, :width
                ]
                o_pack[place, row : row + units, lane + width : lane + 2 * width] = code_wgrad[
                    at : at + units
                ]
        query_in_grad = tn(w_q[0], query_lows[0]) + tn(w_q[1], query_lows[1])
        zero_term = zero_sin[:, 1:2] * query_in_grad[width:]
        tgrad[1, :width] -= zero_term

        code_dt_grad = jnp.zeros((width, events), F32)
        ones = jnp.ones((8, events), BF)
        for h in range(2):
            place = slot(h)
            reset, update, candidate, state_c = (gates[h, k] for k in range(4))
            fresh_grad = nn(w_f[1, h], hidden_grad) + query_in_grad[h * units : (h + 1) * units]
            own_state = srct[h * units : (h + 1) * units]
            candidate_pre = fresh_grad * (1.0 - update) * (1.0 - candidate * candidate)
            update_pre = fresh_grad * (own_state - candidate) * update * (1.0 - update)
            reset_pre = candidate_pre * state_c * reset * (1.0 - reset)
            in_grad = jnp.concatenate([reset_pre, update_pre, candidate_pre], 0).astype(BF)
            state_grad = jnp.concatenate([reset_pre, update_pre, candidate_pre * reset], 0).astype(BF)
            o_pack[place, 0 : 3 * units, :] = nt(in_grad, message)
            state_w = nt(src_low, state_grad)
            o_pack[place, row_sd : row_sd + units, 0 : 3 * units] = state_w[:units]
            o_pack[place, row_sd : row_sd + units, 4 * units : 7 * units] = state_w[units:]
            o_pack[place, row_b : row_b + 1, 0 : 3 * units] = nt(ones, in_grad)[0:1]
            o_pack[place, row_b + 1 : row_b + 2, 0 : 3 * units] = nt(ones, state_grad)[0:1]
            code_dt_grad = code_dt_grad + tn(w_m[h][:, 2 * width : 3 * width], in_grad)
        slope = sin_d[...] * code_dt_grad
        tgrad[1, :width] -= slope
        tgrad[0, :width] -= slope * delta[...]
        ones_f = jnp.ones((8, events), F32)
        for i in range(2):
            line = lax.dot_general(
                ones_f, tgrad[i, :width], (((1,), (1,)), ((), ())),
                precision=lax.Precision.HIGHEST, preferred_element_type=F32,
            )[0:1]
            for place in range(2):
                o_pack[place, row_b + 2 + i : row_b + 3 + i, 0:width] = line
        for place in range(2):
            o_pack[place, row_b + 4 : row_b + 5, 0:128] = jnp.broadcast_to(loss, (1, 128))
            o_pack[place, row_b + 5 : row_b + 6, 0:128] = stat[0:1, :]

    pl.run_scoped(
        rest,
        pltpu.VMEM((4 * PAD, nbrs * events), F32),
        pltpu.VMEM((4 * PAD, nbrs * events), BF),
    )


def pack_rows(units):
    step = -(-units // 8) * 8
    first = -(-3 * units // 8) * 8
    return first, first + step, first + 2 * step, first + 3 * step, first + 3 * step + -(-units // 16) * 8


def pack_height(units):
    return -(-(pack_rows(units)[-1] + 8) // 64) * 64


def memory_kernel(mem, fresh, src, wcount, out):
    units, rows = mem.shape
    pick = (lax.broadcasted_iota(jnp.int32, (rows, rows), 1) == src[...]).astype(BF)
    parts = split3(fresh[...])
    moved = nn(parts[0], pick) + nn(parts[1], pick) + nn(parts[2], pick)
    alive = (lax.broadcasted_iota(jnp.int32, (16, rows), 1) < wcount[0]).astype(BF)
    hit = nn(alive, pick)[0:1] > 0.5
    out[...] = jnp.where(hit, moved, mem[...])


def adam_step(master, moment, square, gradient):
    moment_new = BETA_ONE * moment + (1.0 - BETA_ONE) * gradient
    square_new = BETA_TWO * square + (1.0 - BETA_TWO) * gradient * gradient
    master_new = master - RATE * (moment_new / (1.0 - BETA_ONE**STEP)) / (
        jnp.sqrt(square_new / (1.0 - BETA_TWO**STEP)) + EPSILON
    )
    return (master_new, moment_new, square_new)


def flips(count, step):
    return [(i, i ^ step) for i in range(count)]


def per_device(
    n_row,
    memory, sources, dest_ids, neighbours, delta_t, nbr_delta, edge_feat, window_count,
    message_weight, message_weight_moment, message_weight_square,
    state_weight, state_weight_moment, state_weight_square,
    gate_bias, gate_bias_moment, gate_bias_square,
    time_param, time_param_moment, time_param_square,
    attend_weight, attend_weight_moment, attend_weight_square,
    dense_first, dense_first_moment, dense_first_square,
    dense_second, dense_second_moment, dense_second_square,
    target_weight, target_weight_moment, target_weight_square,
):
    rows, width = memory.shape
    units = width // 2
    events = rows // 2
    nbrs = neighbours.shape[1]
    planes = n_row // PLANE
    total_rows = n_row * rows
    head = lax.axis_index("head")
    row = lax.axis_index("row")
    meta = jnp.stack([row, head]).astype(jnp.int32)

    def own(x, axis):
        return lax.dynamic_slice_in_dim(x, head * events, events, axis)

    def swap(x):
        return lax.ppermute(x, "head", [(0, 1), (1, 0)])

    def hop(x, step):
        return lax.ppermute(x, "row", flips(n_row, step))

    mem_t = memory.T
    own_ids = own(dest_ids, 0)
    lines = jnp.stack(
        [
            own_ids // LO_BASE,
            own_ids % LO_BASE,
            jnp.broadcast_to(window_count[0] // LO_BASE, (events,)),
            jnp.broadcast_to(window_count[0] % LO_BASE, (events,)),
        ]
    )
    block = jnp.concatenate([own(mem_t, 1).astype(BF), lines.astype(BF)], 0)
    cut = 112
    part_a, part_b = block[:cut][None], block[cut:][None]
    line_a = jnp.concatenate([part_a] + [hop(part_a, d * PLANE) for d in range(1, planes)], 0)
    plane_b = jnp.concatenate([part_b] + [hop(part_b, d) for d in range(1, PLANE)], 0)
    all_a = jnp.stack([line_a] + [hop(line_a, d) for d in range(1, PLANE)])
    all_b = jnp.stack([plane_b] + [hop(plane_b, d * PLANE) for d in range(1, planes)])
    mem_a = jnp.stack([all_a, swap(all_a)])
    mem_b = jnp.stack([all_b, swap(all_b)])

    src = own(sources, 1)
    delta = own(delta_t[None], 1)
    ndelta = own(nbr_delta.T, 1)
    tcol = time_param.T
    code_shapes = (
        shape(width, events), shape(width, events, dtype=BF), shape(width, events),
        shape(width, nbrs * events, dtype=BF), shape(width, nbrs * events),
    )
    srct, code_d, sin_d, code_n, sin_n = vmem_call(codes_kernel, code_shapes, "vvvvv")(
        mem_t, src, delta, ndelta, tcol
    )
    mw, aw = message_weight.T, attend_weight.transpose(0, 2, 1)
    weights = (mw, state_weight, aw, dense_first, dense_second)
    pairs = []
    for w in weights:
        pairs += [w, swap(w)]
    gb = gate_bias.T
    gb_o = swap(gb)
    bias = jnp.where(head == 0, jnp.stack([gb, gb_o]), jnp.stack([gb_o, gb]))
    bf = functools.partial(shape, dtype=BF)
    w_shapes = (
        bf(2, 3 * units, 4 * width), bf(2, 3 * units, width), bf(2, units, 2 * width),
        bf(4 * PAD, 256), bf(4 * PAD, width), bf(2, width, 2 * PAD),
        bf(2, 2, units, width), bf(2, 2, width, units), bf(2, width, units), bf(2, units, width),
        bf(width, width),
    )
    prepared = vmem_call(weights_kernel, w_shapes, "s" + "v" * 11)(meta, *pairs, target_weight)

    index = jnp.concatenate([own(neighbours.T, 1).reshape(-1), own_ids])
    use_table = total_rows <= TABLE_ROWS_MAX
    lookups = (nbrs + 1) * events
    if use_table:
        gathered = jnp.zeros((16, 128), BF)
    else:
        order = jnp.arange(n_row, dtype=jnp.int32) ^ row
        full_a = mem_a.transpose(0, 2, 1, 4, 3).reshape(2, n_row, events, cut)
        full_b = mem_b.transpose(0, 1, 2, 4, 3).reshape(2, n_row, events, block.shape[0] - cut)
        full = jnp.concatenate([full_a, full_b], 3)
        at = index // rows
        half = (index % rows) // events
        gathered = full[half ^ head, at ^ row, index % events]
        gathered = jnp.pad(gathered, ((0, 0), (0, 256 - block.shape[0])))
        del order
    height = pack_height(units)
    hi_rows = total_rows // LO_BASE
    scratch = [
        pltpu.VMEM((lookups if use_table else 16, 256), BF),
        pltpu.VMEM((4 * width, events), F32),
        pltpu.VMEM((2 * width, events), F32),
        pltpu.VMEM((width, events), F32),
        pltpu.VMEM((2 * n_row if use_table else 1, width, events), BF),
        pltpu.VMEM((hi_rows, LO_BASE), F32),
        pltpu.VMEM((16, 128), F32),
        pltpu.VMEM((16, events), F32),
        pltpu.VMEM((3, 16, events), F32),
        pltpu.VMEM((2, PAD, events), F32),
        pltpu.VMEM((2, PAD, events), F32),
        pltpu.VMEM((2, 4, units, events), F32),
        pltpu.VMEM((block.shape[0], events), F32),
        pltpu.VMEM((2, PAD * 2, events), F32),
    ]
    fresh, pack = vmem_call(
        functools.partial(step_kernel, planes, use_table),
        (shape(2, units, events), shape(2, height, 4 * width)),
        "ss" + "v" * 24 + "s",
        scratch,
        VMEM_LIMIT if use_table else VMEM_WHOLE,
    )(
        meta, 2 * index, mem_a, mem_b, srct, code_d, sin_d, code_n, sin_n, own(edge_feat.T, 1),
        delta, ndelta, tcol, bias, *prepared, gathered, window_count,
    )

    fresh_own = lax.dynamic_index_in_dim(fresh, head, 0, False)
    fresh_sent = swap(lax.dynamic_index_in_dim(fresh, 1 - head, 0, False))
    both = jnp.where(
        head == 0,
        jnp.concatenate([fresh_own, fresh_sent], 1),
        jnp.concatenate([fresh_sent, fresh_own], 1),
    )
    base_cols = lax.dynamic_slice_in_dim(mem_t, head * units, units, 0)
    new_memory = vmem_call(memory_kernel, shape(units, rows), "vvvs")(
        base_cols, both, sources.reshape(rows, 1), window_count
    ).T

    buf = pack[0] + swap(pack[1])
    cut_steps = []
    step = 1
    while step < PLANE:
        bit = (row // step) % 2
        half = buf.shape[0] // 2
        keep = lax.dynamic_slice_in_dim(buf, bit * half, half, 0)
        send = lax.dynamic_slice_in_dim(buf, (1 - bit) * half, half, 0)
        buf = keep + hop(send, step)
        cut_steps.append((step, bit))
        step *= 2
    while step < n_row:
        buf = buf + hop(buf, step)
        step *= 2
    for step, bit in reversed(cut_steps):
        got = hop(buf, step)
        buf = jnp.where(bit == 0, jnp.concatenate([buf, got], 0), jnp.concatenate([got, buf], 0))

    row_qk, row_vf, row_sd, row_t, row_b = pack_rows(units)
    quarter = units // 2
    shared = buf[row_t : row_b + 8]
    shared_o = swap(shared)
    first = jnp.where(head == 0, shared, shared_o)
    second = jnp.where(head == 0, shared_o, shared)
    target_sum = jnp.concatenate(
        [p[:quarter, k * width : (k + 1) * width] for p in (first, second) for k in range(2)], 0
    )
    small = first[row_b - row_t :]
    time_sum = small[2:4, :width]
    loss_sum = small[4, 0]
    live_rows = small[5, 0] * (1.0 / (2 * n_row))
    bias_sum = buf[row_b : row_b + 2, : 3 * units]
    message_sum = buf[: 3 * units]
    query_sum = buf[row_qk : row_qk + units, : 2 * width]
    key_sum = buf[row_qk : row_qk + units, 2 * width :]
    value_sum = buf[row_vf : row_vf + units, : 2 * width]
    attend_sum = jnp.stack([query_sum, key_sum, value_sum])
    first_sum = jnp.stack(
        [buf[row_vf : row_vf + units, k * width : (k + 1) * width] for k in (2, 3)]
    )
    state_sum = jnp.concatenate(
        [buf[row_sd : row_sd + units, k : k + 3 * units] for k in (0, 4 * units)], 0
    )
    second_sum = jnp.concatenate(
        [buf[row_sd : row_sd + units, k : k + units] for k in (3 * units, 7 * units)], 0
    )

    def turned(x):
        return x.transpose(0, 2, 1)

    message_out = adam_step(mw, message_weight_moment.T, message_weight_square.T, message_sum)
    message_out = tuple(x.T for x in message_out)
    state_out = adam_step(state_weight, state_weight_moment, state_weight_square, state_sum)
    bias_out = adam_step(gate_bias, gate_bias_moment, gate_bias_square, bias_sum)
    time_out = adam_step(time_param, time_param_moment, time_param_square, time_sum)
    attend_out = adam_step(aw, turned(attend_weight_moment), turned(attend_weight_square), attend_sum)
    attend_out = tuple(turned(x) for x in attend_out)
    first_out = adam_step(dense_first, dense_first_moment, dense_first_square, first_sum)
    second_out = adam_step(dense_second, dense_second_moment, dense_second_square, second_sum)
    target_out = adam_step(target_weight, target_weight_moment, target_weight_square, target_sum)
    return (
        new_memory, loss_sum, live_rows,
        *message_out, *state_out, *bias_out, *time_out, *attend_out, *first_out, *second_out, *target_out,
    )


def solution(mesh):
    cols = P(None, "head")
    third = P(None, None, "head")
    middle = P(None, "head", None)
    by_row = P("row", None)
    in_specs = (
        (by_row, by_row, P("row"), by_row, P("row"), by_row, by_row, P("row"))
        + (cols,) * 9 + (P(),) * 3 + (third,) * 3 + (middle,) * 3 + (cols,) * 3 + (P(),) * 3
    )
    out_specs = (
        (P("row", "head"), P(), P())
        + (cols,) * 9 + (P(),) * 3 + (third,) * 3 + (middle,) * 3 + (cols,) * 3 + (P(),) * 3
    )
    return jax.shard_map(
        functools.partial(per_device, mesh.shape["row"]),
        mesh=mesh, in_specs=in_specs, out_specs=out_specs, check_vma=False,
    )
```

```python
import functools
import math

import jax
import jax.numpy as jnp
from jax import lax
from jax.experimental import pallas as pl
from jax.experimental.pallas import tpu as pltpu
from jax.sharding import PartitionSpec as P

STEP = 10
LOGIT_SCALE = 0.25
BETA_ONE = 0.9
BETA_TWO = 0.999
RATE = 0.05
EPSILON = 1e-08
BF = jnp.bfloat16
F32 = jnp.float32
PLANE = 4
PAD = 88
LO_BASE = 256
SAFE_LOGIT = 40.0
VMEM_LIMIT = 58 * 2**20
VMEM_WHOLE = 62 * 2**20
VMEM_SMALL = 12 * 2**20
VMEM_ADAM = 24 * 2**20
TABLE_ROWS_MAX = 16384


def nn(a, b):
    return jnp.dot(a, b, preferred_element_type=F32)


def nt(a, b):
    return lax.dot_general(a, b, (((1,), (1,)), ((), ())), preferred_element_type=F32)


def tn(a, b):
    return lax.dot_general(a, b, (((0,), (0,)), ((), ())), preferred_element_type=F32)


def split3(x):
    first = x.astype(BF)
    rest = x - first.astype(F32)
    second = rest.astype(BF)
    third = (rest - second.astype(F32)).astype(BF)
    return first, second, third


def sin_cos(x):
    turns = jnp.floor(x * (1.0 / math.pi) + 0.5)
    r = ((x - turns * 3.140625) - turns * 0.0009679794311523438) + turns * 3.2584135922775204e-07
    sign = 1.0 - 2.0 * (turns - 2.0 * jnp.floor(turns * 0.5))
    r2 = r * r
    s = SIN[4]
    for k in (3, 2, 1, 0):
        s = s * r2 + SIN[k]
    c = COS[5]
    for k in (4, 3, 2, 1, 0):
        c = c * r2 + COS[k]
    return sign * (r * s), sign * c


SIN = (
    0.9999999956301436,
    -0.16666657831257647,
    0.008333047252581481,
    -0.00019808792312667284,
    2.6045791061554316e-06,
)
COS = (
    0.9999999997746029,
    -0.49999999344091517,
    0.0416666357232742,
    -0.0013888354556677485,
    2.4759808628775167e-05,
    -2.604520000579671e-07,
)


def vmem_call(kernel, out_shape, in_spaces, scratch=(), limit=VMEM_LIMIT, micros=0, in_place=()):
    spaces = {"s": pltpu.SMEM, "v": pltpu.VMEM, "a": pl.ANY}

    def spec(item):
        if isinstance(item, list):
            return tuple(spec(i) for i in item)
        return pl.BlockSpec(memory_space=spaces[item])

    return pl.pallas_call(
        kernel,
        out_shape=out_shape,
        in_specs=[spec(item) for item in in_spaces],
        out_specs=jax.tree.map(
            lambda x: pl.BlockSpec(memory_space=pl.ANY if x in in_place else pltpu.VMEM), out_shape
        ),
        scratch_shapes=list(scratch),
        compiler_params=pltpu.CompilerParams(vmem_limit_bytes=limit),
        cost_estimate=pl.CostEstimate(
            flops=micros * 10**9, bytes_accessed=micros * 10**6, transcendentals=0
        ),
    )


def shape(*dims, dtype=F32):
    return jax.ShapeDtypeStruct(dims, dtype)


def block_kernel(meta, wcount, mem, ids, out):
    width = mem.shape[0]
    events = out.shape[1]
    cols = pl.ds(pl.multiple_of(meta[1] * events, events), events)
    own = ids[:, cols]
    line = lax.broadcasted_iota(jnp.int32, (8, events), 0)
    small = jnp.where(line == 4, own // LO_BASE, own % LO_BASE)
    small = jnp.where(line == 6, wcount[0] // LO_BASE, small)
    small = jnp.where(line == 7, wcount[0] % LO_BASE, small).astype(F32)
    value = mem[:, cols]
    last = jnp.concatenate([value[width - 4 :], small[4:]], 0)
    out[...] = jnp.concatenate([value[: width - 4], last], 0).astype(BF)


def codes_kernel(meta, mem, src, delta, ndelta, tcol, edge, srct, msg, sin_d, code_n, sin_n):
    rows = mem.shape[1]
    events = srct.shape[1]
    nbrs = ndelta.shape[0]
    own = pl.ds(pl.multiple_of(meta[1] * events, events), events)
    pick = (lax.broadcasted_iota(jnp.int32, (rows, events), 0) == src[:, own]).astype(BF)
    parts = split3(mem[...])
    source = nn(parts[0], pick) + nn(parts[1], pick) + nn(parts[2], pick)
    srct[...] = source
    freq, phase = tcol[:, 0:1], tcol[:, 1:2]
    sin_v, cos_v = sin_cos(delta[:, own] * freq + phase)
    sin_d[...] = sin_v
    msg[...] = jnp.concatenate([source, cos_v, edge[:, own].astype(F32)], 0).astype(BF)

    def body(j, carry):
        cols = pl.ds(pl.multiple_of(j * events, events), events)
        s, c = sin_cos(ndelta[pl.ds(j, 1), own] * freq + phase)
        code_n[:, cols] = c.astype(BF)
        sin_n[:, cols] = s.astype(BF)
        return carry

    lax.fori_loop(0, nbrs, body, 0)


WP_QK, WP_VF, WP_SD, WP_B = 272, 368, 464, 736
WP_ROWS, WP_LANES = 752, 768


def pack_weights_kernel(mw, sw, aw, df, ds, gb, out):
    width, units = ds.shape
    out[0 : 3 * units, 0 : 4 * width] = mw[...].astype(BF)
    out[WP_QK : WP_QK + units, 0 : 4 * width] = jnp.concatenate([aw[0], aw[1]], 1).astype(BF)
    out[WP_VF : WP_VF + units, 0 : 4 * width] = jnp.concatenate([aw[2], df[0], df[1]], 1).astype(BF)
    out[WP_SD : WP_SD + 3 * units, 0:width] = sw[...].T.astype(BF)
    out[WP_SD : WP_SD + width, 256 : 256 + units] = ds[...].astype(BF)
    out[WP_SD : WP_SD + units, 384 : 384 + width] = ds[...].T.astype(BF)
    parts = split3(gb[...])
    small = jnp.concatenate([p.astype(F32) for p in parts] + [jnp.zeros((10, gb.shape[1]), F32)], 0)
    out[WP_B : WP_B + 16, 0 : 3 * units] = small.astype(BF)


def weights_kernel(
    meta, own, other, tw, msg,
    o_md, o_mc, o_q, o_kvm, o_kvc, o_kvct, o_f, o_ft, o_d, o_dt, o_tt, o_gin, o_gst,
):
    width = tw.shape[0]
    units = width // 2
    gates = 3 * units

    def put(h, w):
        mw = w[0:gates, 0 : 4 * width].astype(F32)
        o_md[h] = jnp.concatenate(
            [mw[:, width : 2 * width], jnp.zeros((gates, 256 - width), F32)], 1
        ).astype(BF)
        o_mc[h] = mw[:, 2 * width : 3 * width].astype(BF)
        rest = jnp.concatenate([mw[:, :width], mw[:, 2 * width :]], 1).astype(BF)
        small = w[WP_B : WP_B + 16, 0:gates].astype(F32)
        bias = (small[0:2] + small[2:4]) + small[4:6]
        bias = jnp.concatenate([bias, jnp.zeros((6, gates), F32)], 0).T
        o_gin[h] = nn(rest, msg[...]) + bias[:, 0:1]
        o_gst[h] = nn(w[WP_SD : WP_SD + gates, 0:width], msg[0:width]) + bias[:, 1:2]
        o_q[h] = w[WP_QK : WP_QK + units, 0 : 2 * width]
        zero = jnp.zeros((PAD - units, 2 * width), F32)
        key = w[WP_QK : WP_QK + units, 2 * width : 4 * width].astype(F32)
        value = w[WP_VF : WP_VF + units, 0 : 2 * width].astype(F32)
        pair = jnp.concatenate([key, zero, value, zero], 0)
        wide = jnp.concatenate([pair[:, :width], jnp.zeros((2 * PAD, 256 - width), F32)], 1)
        rows = pl.ds(pl.multiple_of(h * 2 * PAD, 2 * PAD), 2 * PAD)
        o_kvm[rows] = wide.astype(BF)
        code = pair[:, width:]
        o_kvc[rows] = code.astype(BF)
        o_kvct[h] = code.T.astype(BF)
        for i in range(2):
            dense = w[WP_VF : WP_VF + units, (2 + i) * width : (3 + i) * width]
            o_f[i, h] = dense
            o_ft[i, h] = dense.astype(F32).T.astype(BF)
        o_d[h] = w[WP_SD : WP_SD + width, 256 : 256 + units]
        o_dt[h] = w[WP_SD : WP_SD + units, 384 : 384 + width]

    put(meta[1], own)
    put(1 - meta[1], other)
    o_tt[...] = tw[...].T.astype(BF)


def step_kernel(
    planes, use_table,
    meta, idx, wcount, own_piece, z_pieces, xy_pieces, far_a, far_b, code_any, sin_any, kvc_any,
    srct, msg, sin_d, delta_all, ndelta_all, tcol,
    w_md, w_mc, w_q, w_kvm, w_kvct, w_f, w_ft, w_d, w_dt, w_tt, gin0, gst, gathered_in,
    o_fresh, o_own, o_other, o_live,
    sems, mem_all, code_n, sin_n, w_kvc, coarse, fine, near, qin, emb, keyt, count, stat, norm,
    scores, probs, fresh_s, att_s, gates, acc_m, tgrad,
):
    width, events = srct.shape
    units = width // 2
    nbrs = ndelta_all.shape[0]
    groups, full, wide_cols = mem_all.shape
    per_group = wide_cols // events
    lookups = (nbrs + 1) * events
    scale = 1.0 / math.sqrt(units)
    row_pos, head = meta[0], meta[1]
    hi_rows = count.shape[0]
    own_cols = pl.ds(pl.multiple_of(head * events, events), events)

    copies = []

    def start(src, dst):
        copy = pltpu.make_async_copy(src, dst, sems.at[len(copies)])
        copy.start()
        copies.append(copy)

    def bring(src, row, half, first, last):
        lanes = pl.ds(pl.multiple_of((lax.rem(row, 2) * 2 + half) * events, events), events)
        start(src, mem_all.at[lax.div(row, 2), pl.ds(first, last - first), lanes])

    cut = z_pieces[0].shape[1]
    for k in range(2):
        half = head ^ k
        bring(own_piece[k], row_pos, half, 0, full)
        for d in range(1, planes):
            bring(z_pieces[k].at[d - 1], row_pos ^ (d * PLANE), half, 0, cut)
        for d in range(1, PLANE):
            bring(xy_pieces[0][d - 1] if k == 0 else xy_pieces[1].at[d - 1], row_pos ^ d, half, 0, full)
            for e in range(1, planes):
                bring(far_a[k][d - 1].at[e - 1], row_pos ^ (e * PLANE + d), half, 0, cut)
        for e in range(1, planes):
            for d in range(PLANE):
                bring(far_b[k][e - 1].at[d], row_pos ^ (e * PLANE + d), half, cut, full)
    n_memory = len(copies)
    start(code_any, code_n)
    start(kvc_any, w_kvc)
    start(sin_any, sin_n)
    for copy in copies[:n_memory]:
        copy.wait()

    count[...] = jnp.zeros_like(count)
    norm[...] = jnp.zeros_like(norm)
    stat[...] = jnp.zeros_like(stat)
    target_t = w_tt[...]

    def keys_of(g):
        return nn(target_t, mem_all[g, 0:width]).astype(BF)

    def per_group_rows(g, table):
        x = mem_all[g]
        wide = x.astype(F32)
        keys = keys_of(g)
        if use_table:
            keyt[g, 0:width] = keys
        keys = keys.astype(F32)
        norm[0:1] = jnp.maximum(norm[0:1], jnp.sum(keys * keys, 0, keepdims=True))
        id_hi = wide[width : width + 1].astype(jnp.int32)
        id_lo = wide[width + 1 : width + 2].astype(jnp.int32)
        hot_hi = (lax.broadcasted_iota(jnp.int32, (hi_rows, wide_cols), 0) == id_hi).astype(BF)
        hot_lo = (lax.broadcasted_iota(jnp.int32, (LO_BASE, wide_cols), 0) == id_lo).astype(BF)
        count[...] += nt(hot_hi, hot_lo)
        here = wide[width + 2 : width + 3] * LO_BASE + wide[width + 3 : width + 4]
        for k in range(0, per_group, 2):
            stat[0:1, :] += here[:, k * events : k * events + 128]
        if table is not None:
            turned = wide.T
            base = pl.multiple_of(g * 2 * wide_cols, 2 * wide_cols)
            table[pl.ds(base, wide_cols, stride=2), :] = turned[:, :128]
            table[pl.ds(base + 1, wide_cols, stride=2), :] = jnp.concatenate(
                [turned[:, 128:], jnp.zeros((wide_cols, 256 - full), F32)], 1
            )

    def gather_rows(table, gathered):
        lax.fori_loop(0, groups, lambda g, s: (per_group_rows(g, table), s)[1], 0)
        unroll = 32

        def body(i, carry):
            for u in range(unroll):
                k = i * unroll + u
                gathered[pl.ds(pl.multiple_of(2 * k, 2), 2), :] = table[
                    pl.ds(pl.multiple_of(idx[k], 2), 2), :
                ]
            return carry

        lax.fori_loop(0, lookups // unroll, body, 0)
        for j in range(nbrs + 1):
            low = gathered[pl.ds(2 * j * events, events, stride=2), :]
            high = gathered[pl.ds(2 * j * events + 1, events, stride=2), :]
            near[pl.ds(j * events, events), :] = jnp.concatenate([low, high], 1).astype(BF)

    if use_table:
        pl.run_scoped(
            gather_rows,
            pltpu.VMEM((2 * groups * wide_cols, 128), F32),
            pltpu.VMEM((2 * lookups, 128), F32),
        )
    else:
        lax.fori_loop(0, groups, lambda g, s: (per_group_rows(g, None), s)[1], 0)
        near = gathered_in

    def count_lines(g, keys):
        at = g * (wide_cols // LO_BASE)
        line = jnp.concatenate(
            [count[pl.ds(at + k, 1), :] for k in range(wide_cols // LO_BASE)], 1
        )
        line = jnp.where(line > 0.5, jnp.log(jnp.maximum(line, 1.0)), -1e30)
        parts = split3(line)
        place = lax.broadcasted_iota(jnp.int32, (16, wide_cols), 0)
        first = full - 16
        tail = jnp.where(place >= width - first, 0.0, keys.astype(F32))
        for k in range(3):
            tail = jnp.where(place == width - first + k, parts[k].astype(F32), tail)
        return tail.astype(BF)

    if use_table:

        def add_lines(g, carry):
            keyt[g, full - 16 : full] = count_lines(g, keyt[g, full - 16 : full])
            return carry

        lax.fori_loop(0, groups, add_lines, 0)

    def keys_with_lines(g):
        if use_table:
            return keyt[g]
        keys = jnp.concatenate([keys_of(g).astype(F32), jnp.zeros((full - width, wide_cols), F32)], 0)
        keys = keys.astype(BF)
        return jnp.concatenate([keys[: full - 16], count_lines(g, keys[full - 16 :])], 0)

    live_rows = stat[0:1, 0:1]

    def rest(kvt, pair):
        dest = near[pl.ds(nbrs * events, events), :]
        dest_t = dest.astype(F32).T[:width]
        dest_key = nn(target_t, dest_t.astype(BF)).astype(BF)
        for h in range(2):
            gate_in = gin0[h] + nt(w_md[h], dest)
            gate_state = gst[h]
            reset = jax.nn.sigmoid(gate_in[:units] + gate_state[:units])
            update = jax.nn.sigmoid(
                gate_in[units : 2 * units] + gate_state[units : 2 * units]
            )
            state_c = gate_state[2 * units :]
            candidate = jnp.tanh(gate_in[2 * units :] + reset * state_c)
            for k, v in enumerate((reset, update, candidate, state_c)):
                gates[h, k] = v
            fresh = (1.0 - update) * candidate + update * srct[h * units : (h + 1) * units]
            o_fresh[h] = fresh
            qin[h * units : (h + 1) * units] = fresh
        zero_sin, zero_cos = sin_cos(tcol[...])
        qin[width : 2 * width] = jnp.broadcast_to(zero_cos[:, 1:2], (width, events))
        query_in = qin[...].astype(BF)
        copies[n_memory].wait()
        copies[n_memory + 1].wait()

        def project(j, carry):
            cols = pl.ds(pl.multiple_of(j * events, events), events)
            kvt[:, cols] = nt(w_kvm[...], near[cols, :]) + nn(w_kvc[...], code_n[:, cols])
            return carry

        lax.fori_loop(0, nbrs, project, 0)
        attended_low = []
        for h in range(2):
            key_at, value_at = h * 2 * PAD, h * 2 * PAD + PAD
            queries = nn(w_q[h], query_in)
            fresh_s[h, :units] = queries
            for j in range(nbrs):
                cols = pl.ds(j * events, events)
                scores[j : j + 1] = (
                    jnp.sum(queries * kvt[key_at : key_at + units, cols], 0, keepdims=True) * scale
                )
            score = scores[0:nbrs]
            grown = jnp.exp(score - jnp.max(score, 0, keepdims=True))
            prob = grown / jnp.sum(grown, 0, keepdims=True)
            probs[h, 0:nbrs] = prob
            total = jnp.zeros((units, events), F32)
            for j in range(nbrs):
                cols = pl.ds(j * events, events)
                total = total + prob[j : j + 1] * kvt[value_at : value_at + units, cols]
            att_s[h, :units] = total
            attended_low.append(total.astype(BF))
        fresh_lows = [qin[h * units : (h + 1) * units].astype(BF) for h in range(2)]
        hidden = (nn(w_ft[0, 0], attended_low[0]) + nn(w_ft[0, 1], attended_low[1])) + (
            nn(w_ft[1, 0], fresh_lows[0]) + nn(w_ft[1, 1], fresh_lows[1])
        )
        sigmoid_h = jax.nn.sigmoid(hidden)
        mixed_low = (hidden * sigmoid_h).astype(BF)
        emb_halves = [nn(w_dt[h], mixed_low) for h in range(2)]
        emb[0:units] = emb_halves[0]
        emb[units:width] = emb_halves[1]
        emb_low = emb[...].astype(BF)
        ones_line = (lax.broadcasted_iota(jnp.int32, (full - width, events), 0) < 3).astype(F32)
        emb_aug = jnp.concatenate([LOGIT_SCALE * emb_low.astype(F32), ones_line], 0)
        emb_rows = emb_aug.T.astype(BF)
        emb_norm = jnp.max(jnp.sum(emb[...] * emb[...], 0, keepdims=True))
        bound = LOGIT_SCALE * LOGIT_SCALE * emb_norm * jnp.max(norm[0:1])
        own_logit = LOGIT_SCALE * jnp.sum(
            emb_low.astype(F32) * dest_key.astype(F32), 0, keepdims=True
        )

        def soft_section(acc, top, total):
            total[...] = jnp.zeros_like(total)
            acc[...] = jnp.zeros_like(acc)
            small = bound < SAFE_LOGIT * SAFE_LOGIT

            @pl.when(small)
            def _():
                top[...] = jnp.zeros_like(top)

                def body(g, carry):
                    grown = jnp.exp(nn(emb_rows, keys_with_lines(g)))
                    lanes = grown[:, 0:128]
                    for k in range(1, wide_cols // 128):
                        lanes = lanes + grown[:, k * 128 : (k + 1) * 128]
                    total[...] += lanes
                    acc[...] += nt(grown.astype(BF), mem_all[g])
                    return carry

                lax.fori_loop(0, groups, body, 0)
                total[...] = jnp.broadcast_to(jnp.sum(total[...], 1, keepdims=True), total.shape)

            @pl.when(jnp.logical_not(small))
            def _():
                top[...] = jnp.full_like(top, -1e30)

                def body(g, carry):
                    logits = nn(emb_rows, keys_with_lines(g))
                    old = top[:, 0:1]
                    new = jnp.maximum(old, jnp.max(logits, 1, keepdims=True))
                    grown = jnp.exp(logits - new)
                    fade = jnp.exp(old - new)
                    total[...] = total[...] * fade + jnp.sum(grown, 1, keepdims=True)
                    top[...] = jnp.broadcast_to(new, top.shape)
                    acc[...] = acc[...] * fade + nt(grown.astype(BF), mem_all[g])
                    return carry

                lax.fori_loop(0, groups, body, 0)

            acc_m[...] = (acc[...] / total[:, 0:1]).T
            probs[2] = jnp.broadcast_to(top[:, 0:1] + jnp.log(total[:, 0:1]), (events, 128)).T[:16]

        pl.run_scoped(
            soft_section,
            pltpu.VMEM((events, full), F32),
            pltpu.VMEM((events, 128), F32),
            pltpu.VMEM((events, 128), F32),
        )
        log_total = probs[2, 0:1]
        position = lax.broadcasted_iota(jnp.int32, (1, events), 1) + head * events
        live = (position < wcount[0]).astype(F32)
        loss = jnp.sum((log_total - own_logit) * live, 1, keepdims=True)
        weight = live / live_rows
        own_prob = jnp.exp(own_logit - log_total)
        own_grad = ((own_prob - 1.0) * weight).astype(BF).astype(F32) - own_prob * weight
        mean_mem = acc_m[:width]
        spread = weight * mean_mem + own_grad * dest_t
        parts = split3(spread)
        target_grad = LOGIT_SCALE * (nt(parts[0], emb_low) + nt(parts[1], emb_low) + nt(parts[2], emb_low))
        parts = split3(mean_mem)
        mean_key = nn(target_t, parts[0]) + nn(target_t, parts[1]) + nn(target_t, parts[2])
        emb_grad = LOGIT_SCALE * (weight * mean_key + own_grad * dest_key.astype(F32))

        coarse[...] = jnp.zeros_like(coarse)
        fine[...] = jnp.zeros_like(fine)
        blocks = state_blocks(units)
        quarter = units // 2

        def slot(h):
            return h ^ head

        emb_grad_low = [emb_grad[h * units : (h + 1) * units].astype(BF) for h in range(2)]
        mixed_grad = nn(w_d[0], emb_grad_low[0]) + nn(w_d[1], emb_grad_low[1])
        hidden_grad = (mixed_grad * sigmoid_h * (1.0 + hidden * (1.0 - sigmoid_h))).astype(BF)
        for h in range(2):
            second = nt(mixed_low, emb_grad_low[h])
            place = slot(h)
            for i, v in enumerate((attended_low[h], fresh_lows[h])):
                fine[place, units:width, (2 + i) * width : (3 + i) * width] = nt(v, hidden_grad)
            for k in range(2):
                fine[place, ROW_T : ROW_T + quarter, k * width : (k + 1) * width] = target_grad[
                    h * units + k * quarter : h * units + (k + 1) * quarter
                ]
            for k in range(4):
                at = 2 * width + k * units
                fine[place, ROW_T : ROW_T + quarter, at : at + units] = second[
                    k * quarter : (k + 1) * quarter
                ]

        copies[n_memory + 2].wait()
        tgrad[...] = jnp.zeros_like(tgrad)
        query_lows = []
        prob_terms = []
        att_grads = []
        for h in range(2):
            value_at = h * 2 * PAD + PAD
            att_grad = nn(w_f[0, h], hidden_grad)
            prob = probs[h, 0:nbrs]
            for j in range(nbrs):
                cols = pl.ds(j * events, events)
                scores[j : j + 1] = jnp.sum(
                    att_grad * kvt[value_at : value_at + units, cols], 0, keepdims=True
                )
            prob_grad = scores[0:nbrs]
            prob_terms.append(prob * (prob_grad - jnp.sum(prob * prob_grad, 0, keepdims=True)))
            att_grads.append(att_grad)
            total = jnp.zeros((units, events), F32)
            key_at = h * 2 * PAD
            for j in range(nbrs):
                cols = pl.ds(j * events, events)
                total = total + prob_terms[h][j : j + 1] * kvt[key_at : key_at + units, cols]
            query_lows.append((total * scale).astype(BF))
        fill = jnp.zeros((PAD - units, events), F32)
        for j in range(nbrs):
            cols = pl.ds(j * events, events)
            pieces = []
            for h in range(2):
                pieces += [
                    (prob_terms[h][j : j + 1] * scale) * fresh_s[h, :units], fill,
                    probs[h, j : j + 1] * att_grads[h], fill,
                ]
            pair_j = jnp.concatenate(pieces, 0).astype(BF)
            pair[:, cols] = pair_j
            code_grad = nn(w_kvct[0], pair_j[: 2 * PAD]) + nn(w_kvct[1], pair_j[2 * PAD :])
            slope = sin_n[:, cols].astype(F32) * code_grad
            tgrad[1, :width] -= slope
            tgrad[0, :width] -= slope * ndelta_all[j : j + 1, own_cols]
        near_grad = nn(pair[...], near[pl.ds(0, nbrs * events), :])
        code_wgrad = nt(pair[...], code_n[...])
        for h in range(2):
            place = slot(h)
            base = h * 2 * PAD
            query_grad = nt(query_lows[h], query_in)
            fine[place, 0:units, 0 : 2 * width] = query_grad
            for k, (row, lane) in enumerate(((0, 2 * width), (units, 0))):
                at = base + k * PAD
                fine[place, row : row + units, lane : lane + width] = near_grad[
                    at : at + units, :width
                ]
                fine[place, row : row + units, lane + width : lane + 2 * width] = code_wgrad[
                    at : at + units
                ]
        query_in_grad = tn(w_q[0], query_lows[0]) + tn(w_q[1], query_lows[1])
        zero_term = zero_sin[:, 1:2] * query_in_grad[width:]
        tgrad[1, :width] -= zero_term

        def send_fine(k):
            for place, out in ((1, o_other), (0, o_own)):
                start(fine.at[place, pl.ds(k * FINE, FINE)], out.at[k, pl.ds(COARSE, FINE)])

        for k in range(3):
            send_fine(k)

        code_dt_grad = jnp.zeros((width, events), F32)
        ones = jnp.ones((8, events), BF)
        for h in range(2):
            place = slot(h)
            reset, update, candidate, state_c = (gates[h, k] for k in range(4))
            fresh_grad = nn(w_f[1, h], hidden_grad) + query_in_grad[h * units : (h + 1) * units]
            own_state = srct[h * units : (h + 1) * units]
            candidate_pre = fresh_grad * (1.0 - update) * (1.0 - candidate * candidate)
            update_pre = fresh_grad * (own_state - candidate) * update * (1.0 - update)
            reset_pre = candidate_pre * state_c * reset * (1.0 - reset)
            in_grad = jnp.concatenate([reset_pre, update_pre, candidate_pre], 0).astype(BF)
            state_grad = jnp.concatenate([reset_pre, update_pre, candidate_pre * reset], 0).astype(BF)
            gate_rows = 3 * units
            coarse[place, 0:gate_rows, width : 2 * width] = nn(in_grad, dest)[:, :width]
            rest_grad = nt(in_grad, msg[...])
            coarse[place, 0:gate_rows, 0:width] = rest_grad[:, :width]
            coarse[place, 0:gate_rows, 2 * width : 4 * width] = rest_grad[:, width:]
            state_w = nt(msg[0:width], state_grad)
            coarse[place, 0:width, 4 * width : 4 * width + gate_rows - 256] = state_w[:, 256:]
            for k, (first, last) in enumerate(blocks):
                coarse[place, gate_rows : gate_rows + last - first, k * 256 : (k + 1) * 256] = state_w[
                    first:last, 0:256
                ]
            fine[place, ROW_B : ROW_B + 1, 0:gate_rows] = nt(ones, in_grad)[0:1]
            fine[place, ROW_B + 1 : ROW_B + 2, 0:gate_rows] = nt(ones, state_grad)[0:1]
            code_dt_grad = code_dt_grad + tn(w_mc[h], in_grad)
        slope = sin_d[...] * code_dt_grad
        tgrad[1, :width] -= slope
        tgrad[0, :width] -= slope * delta_all[:, own_cols]
        ones_f = jnp.ones((8, events), F32)
        for i in range(2):
            line = lax.dot_general(
                ones_f, tgrad[i, :width], (((1,), (1,)), ((), ())),
                precision=lax.Precision.HIGHEST, preferred_element_type=F32,
            )[0:1]
            for place in range(2):
                fine[place, ROW_B + 2 + i : ROW_B + 3 + i, 0:width] = line
        for place in range(2):
            fine[place, ROW_B + 4 : ROW_B + 5, 0:128] = jnp.broadcast_to(loss, (1, 128))
        o_live[...] = jnp.broadcast_to(stat[0:1, :], o_live.shape)
        send_fine(3)
        for k in range(4):
            for place, out in ((1, o_other), (0, o_own)):
                start(coarse.at[place, pl.ds(k * COARSE, COARSE)], out.at[k, pl.ds(0, COARSE)])
        for copy in copies[n_memory + 3 :]:
            copy.wait()

    pl.run_scoped(
        rest,
        pltpu.VMEM((4 * PAD, nbrs * events), F32),
        pltpu.VMEM((4 * PAD, nbrs * events), BF),
    )


COARSE, FINE, LANES = 80, 64, 768
ROWS = COARSE + FINE
EXTRA = 16
ROW_T, ROW_B = 192, 240


def state_blocks(units):
    room = 4 * COARSE - 3 * units
    return [(k * room, min((k + 1) * room, 2 * units)) for k in range(3)]


def to_half_wire(out, value):
    high = value.astype(BF)
    out[0:ROWS] = high
    out[ROWS:] = (value - high.astype(F32))[ROWS - EXTRA :].astype(BF)


def from_half_wire(w):
    high = w[0:ROWS].astype(F32)
    last = high[ROWS - EXTRA :] + w[ROWS:].astype(F32)
    return jnp.concatenate([high[: ROWS - EXTRA], last], 0)


def to_wire(out, value):
    high = value.astype(BF)
    out[0:ROWS] = high
    out[ROWS:] = (value - high.astype(F32)).astype(BF)


def from_wire(w):
    return w[0:ROWS].astype(F32) + w[ROWS:].astype(F32)


def first_sum_kernel(bits, own, got, o_keep, o_send):
    for k in range(2):
        q = bits[0] * 2 + k
        o_keep[k] = own[q] + got[q]
        q = (1 - bits[0]) * 2 + k
        to_half_wire(o_send.at[k], own[q] + got[q])


def second_sum_kernel(bits, keep, got, o_keep, o_send):
    q = bits[1]
    o_keep[...] = keep[q] + from_half_wire(got[q])
    q = 1 - bits[1]
    to_half_wire(o_send, keep[q] + from_half_wire(got[q]))


def third_sum_kernel(keep, got, o_send):
    to_wire(o_send, keep[...] + from_half_wire(got[...]))


def wire_sum_kernel(one, two, o_send):
    to_wire(o_send, from_wire(one[...]) + from_wire(two[...]))


def quarter_of(bits, k):
    one = bits[0] if k < 2 else 1 - bits[0]
    two = bits[1] if k % 2 == 0 else 1 - bits[1]
    return one * 2 + two


def shared_kernel(bits, w0, w1, w2, w3, out):
    for k, w in enumerate((w0, w1, w2, w3)):

        @pl.when(quarter_of(bits, k) == 3)
        def _(w=w):
            out[0:FINE] = w[COARSE:ROWS]
            out[FINE:] = w[ROWS + COARSE :]


def adam_kernel(bits, w0, w1, w2, w3, *refs):
    params, outs = refs[:18], refs[18:36]
    coarse, fine = refs[36:]
    for k, w in enumerate((w0, w1, w2, w3)):
        q = quarter_of(bits, k)
        value = from_wire(w[...])
        coarse[pl.ds(pl.multiple_of(q * COARSE, COARSE), COARSE)] = value[0:COARSE]
        fine[pl.ds(pl.multiple_of(q * FINE, FINE), FINE)] = value[COARSE:]
    units, gates = params[15].shape[1], params[3].shape[1]
    width = 2 * units

    def step(which, at, gradient):
        values = [params[3 * which + i][at] for i in range(3)]
        for i, v in enumerate(adam_step(*values, gradient)):
            outs[3 * which + i][at] = v

    every = (slice(None), slice(None))
    step(0, every, coarse[0:gates, 0 : 4 * width])
    for k, (first, last) in enumerate(state_blocks(units)):
        step(
            1, (slice(first, last), slice(0, 256)),
            coarse[gates : gates + last - first, k * 256 : (k + 1) * 256],
        )
    step(1, (slice(None), slice(256, gates)), coarse[0:width, 4 * width : 4 * width + gates - 256])
    step(2, every, fine[ROW_B : ROW_B + 2, 0:gates])
    step(3, 0, fine[0:units, 0 : 2 * width])
    step(3, 1, fine[0:units, 2 * width : 4 * width])
    step(3, 2, fine[units:width, 0 : 2 * width])
    for i in range(2):
        step(4, (slice(None), i), fine[units:width, (2 + i) * width : (3 + i) * width])
    quarter = units // 2
    for k in range(4):
        at = 2 * width + k * units
        step(5, (slice(k * quarter, (k + 1) * quarter), slice(None)), fine[ROW_T : ROW_T + quarter, at : at + units])


def shared_adam_kernel(meta, own, other, *refs):
    params, outs, o_loss = refs[:6], refs[6:12], refs[12]
    width = params[0].shape[0]
    quarter = width // 4

    def step(which, at, gradient):
        values = [params[3 * which + i][at] for i in range(3)]
        for i, v in enumerate(adam_step(*values, gradient)):
            outs[3 * which + i][at] = v

    def run(first, second):
        parts = [w[0:FINE].astype(F32) + w[FINE:].astype(F32) for w in (first, second)]
        for h in range(2):
            for k in range(2):
                at = (h * 2 + k) * quarter
                step(
                    0, (slice(at, at + quarter), slice(None)),
                    parts[h][0:quarter, k * width : (k + 1) * width],
                )
        row = ROW_B - 3 * FINE
        step(1, (slice(None), slice(None)), parts[0][row + 2 : row + 4, 0:width])
        o_loss[...] = jnp.broadcast_to(parts[0][row + 4 : row + 5, 0:128], o_loss.shape)

    @pl.when(meta[1] == 0)
    def _():
        run(own, other)

    @pl.when(meta[1] == 1)
    def _():
        run(other, own)


def memory_kernel(mem, fresh, src, wcount, out):
    units, rows = mem.shape
    pick = (lax.broadcasted_iota(jnp.int32, (rows, rows), 1) == src[...]).astype(BF)
    parts = split3(fresh[...])
    moved = nn(parts[0], pick) + nn(parts[1], pick) + nn(parts[2], pick)
    alive = (lax.broadcasted_iota(jnp.int32, (16, rows), 1) < wcount[0]).astype(BF)
    hit = nn(alive, pick)[0:1] > 0.5
    out[...] = jnp.where(hit, moved, mem[...])


def adam_step(master, moment, square, gradient):
    moment_new = BETA_ONE * moment + (1.0 - BETA_ONE) * gradient
    square_new = BETA_TWO * square + (1.0 - BETA_TWO) * gradient * gradient
    master_new = master - RATE * (moment_new / (1.0 - BETA_ONE**STEP)) / (
        jnp.sqrt(square_new / (1.0 - BETA_TWO**STEP)) + EPSILON
    )
    return (master_new, moment_new, square_new)


def axis_orders(n_row):
    bits = []
    step = PLANE
    while step < n_row:
        bits.append(step)
        step *= 2
    first = [1, 2] + bits
    second = bits[:2] + [1, 2] + bits[2:]
    return list(zip(first, second))


def flips(count, step):
    return [(i, i ^ step) for i in range(count)]


def per_device(
    n_row,
    memory, sources, dest_ids, neighbours, delta_t, nbr_delta, edge_feat, window_count,
    message_weight, message_weight_moment, message_weight_square,
    state_weight, state_weight_moment, state_weight_square,
    gate_bias, gate_bias_moment, gate_bias_square,
    time_param, time_param_moment, time_param_square,
    attend_weight, attend_weight_moment, attend_weight_square,
    dense_first, dense_first_moment, dense_first_square,
    dense_second, dense_second_moment, dense_second_square,
    target_weight, target_weight_moment, target_weight_square,
):
    rows, width = memory.shape
    units = width // 2
    events = rows // 2
    nbrs = neighbours.shape[1]
    planes = n_row // PLANE
    total_rows = n_row * rows
    head = lax.axis_index("head")
    row = lax.axis_index("row")
    meta = jnp.stack([row, head]).astype(jnp.int32)

    def own(x, axis):
        return lax.dynamic_slice_in_dim(x, head * events, events, axis)

    def swap(x):
        return lax.ppermute(x, "head", [(0, 1), (1, 0)])

    def hop(x, step):
        return lax.ppermute(x, "row", flips(n_row, step))

    bf = functools.partial(shape, dtype=BF)
    full = -(-(width + 4) // 16) * 16

    mem_t = memory.T
    block = vmem_call(block_kernel, bf(full, events), "ssvv", micros=1)(
        meta, window_count, mem_t, dest_ids[None]
    )
    cut = 128
    near_z = [hop(block[:cut], e * PLANE) for e in range(1, planes)]
    near_xy = [hop(block, d) for d in range(1, PLANE)]
    mw, aw, gb = message_weight.T, attend_weight.transpose(0, 2, 1), gate_bias
    packed = vmem_call(pack_weights_kernel, bf(WP_ROWS, WP_LANES), "vvvvvv", limit=VMEM_SMALL, micros=2)(
        mw, state_weight, aw, dense_first, dense_second, gb
    )
    line_a = jnp.stack(near_z)
    plane_b = jnp.stack([block[cut:]] + [p[cut:] for p in near_xy])
    line_a, plane_b = lax.optimization_barrier((line_a, plane_b))
    packed, _ = lax.optimization_barrier((packed, line_a))
    packed_o = swap(packed)
    far_a = tuple(hop(line_a, d) for d in range(1, PLANE))
    far_b = tuple(hop(plane_b, e * PLANE) for e in range(1, planes))
    delta, ndelta, edge, tcol, packed_o, _ = lax.optimization_barrier(
        (delta_t[None], nbr_delta.T, edge_feat.T, time_param.T, packed_o, plane_b)
    )
    code_shapes = (
        shape(width, events), bf(3 * width, events), shape(width, events),
        bf(width, nbrs * events), bf(width, nbrs * events),
    )
    srct, msg, sin_d, code_n, sin_n = vmem_call(codes_kernel, code_shapes, "svvvvvv", micros=9)(
        meta, mem_t, sources, delta, ndelta, tcol, edge
    )
    w_shapes = (
        bf(2, 3 * units, 256), bf(2, 3 * units, width), bf(2, units, 2 * width),
        bf(4 * PAD, 256), bf(4 * PAD, width), bf(2, width, 2 * PAD),
        bf(2, 2, units, width), bf(2, 2, width, units), bf(2, width, units), bf(2, units, width),
        bf(width, width), shape(2, 3 * units, events), shape(2, 3 * units, events),
    )
    w_md, w_mc, w_q, w_kvm, w_kvc, *w_more = vmem_call(weights_kernel, w_shapes, "svvvv", micros=6)(
        meta, packed, packed_o, target_weight, msg
    )

    far_a, far_b, _ = lax.optimization_barrier((far_a, far_b, w_md))
    block, line_a, near_xy, _ = lax.optimization_barrier((block, line_a, near_xy, srct))
    own_piece = (block, swap(block))
    z_pieces = (line_a, swap(line_a))
    xy_pieces = (tuple(near_xy), swap(jnp.stack(near_xy)))
    far_a = (far_a, tuple(swap(p) for p in far_a))
    far_b = (far_b, tuple(swap(p) for p in far_b))

    index = jnp.concatenate([own(neighbours.T, 1).reshape(-1), own(dest_ids, 0)])
    use_table = total_rows <= TABLE_ROWS_MAX
    lookups = (nbrs + 1) * events
    if use_table:
        gathered = tcol
    else:
        parts = {}
        for k in range(2):
            parts[0, 0, k] = own_piece[k]
            for e in range(1, planes):
                parts[e, 0, k] = jnp.concatenate([z_pieces[k][e - 1], far_b[k][e - 1][0]], 0)
            for d in range(1, PLANE):
                parts[0, d, k] = xy_pieces[k][d - 1]
                for e in range(1, planes):
                    parts[e, d, k] = jnp.concatenate([far_a[k][d - 1][e - 1], far_b[k][e - 1][d]], 0)
        table = jnp.stack([parts[e, d, k].T for e in range(planes) for d in range(PLANE) for k in range(2)])
        half = (index % rows) // events
        gathered = table[((index // rows) ^ row) * 2 + (half ^ head), index % events]
        gathered = jnp.pad(gathered, ((0, 0), (0, 256 - full)))
    hi_rows = total_rows // LO_BASE
    wide_cols = 4 * events
    groups = total_rows // wide_cols
    n_copies = 2 * (1 + (planes - 1) + (PLANE - 1) * planes + (planes - 1) * PLANE) + 3 + 16
    scratch = [
        pltpu.SemaphoreType.DMA((n_copies,)),
        pltpu.VMEM((groups, full, wide_cols), BF),
        pltpu.VMEM((width, nbrs * events), BF),
        pltpu.VMEM((width, nbrs * events), BF),
        pltpu.VMEM((4 * PAD, width), BF),
        pltpu.VMEM((2, 4 * COARSE, LANES), F32),
        pltpu.VMEM((2, 4 * FINE, LANES), F32),
        pltpu.VMEM((lookups if use_table else 16, 256), BF),
        pltpu.VMEM((2 * width, events), F32),
        pltpu.VMEM((width, events), F32),
        pltpu.VMEM((groups if use_table else 1, full, wide_cols), BF),
        pltpu.VMEM((hi_rows, LO_BASE), F32),
        pltpu.VMEM((8, 128), F32),
        pltpu.VMEM((8, wide_cols), F32),
        pltpu.VMEM((16, events), F32),
        pltpu.VMEM((3, 16, events), F32),
        pltpu.VMEM((2, PAD, events), F32),
        pltpu.VMEM((2, PAD, events), F32),
        pltpu.VMEM((2, 4, units, events), F32),
        pltpu.VMEM((full, events), F32),
        pltpu.VMEM((2, PAD * 2, events), F32),
    ]
    spaces = [
        "s", "s", "s", ["a", "a"], ["a", "a"], [["a"] * (PLANE - 1), "a"],
        [["a"] * (PLANE - 1)] * 2, [["a"] * (planes - 1)] * 2, "a", "a", "a",
    ] + ["v"] * 19
    fresh, pack_own, pack_other, live = vmem_call(
        functools.partial(step_kernel, planes, use_table),
        (
            shape(2, units, events), shape(4, ROWS, LANES), shape(4, ROWS, LANES), shape(8, 128),
        ),
        spaces,
        scratch,
        VMEM_LIMIT if use_table else VMEM_WHOLE,
        micros=40,
        in_place=(shape(4, ROWS, LANES),),
    )(
        meta, 2 * index, window_count, own_piece, z_pieces, xy_pieces, far_a, far_b, code_n, sin_n, w_kvc,
        srct, msg, sin_d, delta, ndelta, tcol, w_md, w_mc, w_q, w_kvm, *w_more, gathered,
    )

    fresh_own = lax.dynamic_index_in_dim(fresh, head, 0, False)
    fresh_sent = swap(lax.dynamic_index_in_dim(fresh, 1 - head, 0, False))
    both = jnp.where(
        head == 0,
        jnp.concatenate([fresh_own, fresh_sent], 1),
        jnp.concatenate([fresh_sent, fresh_own], 1),
    )
    base_cols = lax.dynamic_slice_in_dim(mem_t, head * units, units, 0)
    new_memory = vmem_call(memory_kernel, shape(units, rows), "vvvs", limit=VMEM_SMALL, micros=3)(
        base_cols, both, sources.reshape(rows, 1), window_count
    ).T

    orders = axis_orders(n_row)

    def joint_hop(x, steps):
        pairs = [(2 * i + c, 2 * (i ^ steps[c]) + c) for i in range(n_row) for c in range(2)]
        return lax.ppermute(x, ("row", "head"), pairs)

    bits = jnp.stack(
        [jnp.where(head == 0, (row // steps[0]) % 2, (row // steps[1]) % 2) for steps in orders[:2]]
    ).astype(jnp.int32)
    wire = bf(2 * ROWS, LANES)
    keep, send = vmem_call(
        first_sum_kernel, (shape(2, ROWS, LANES), bf(2, ROWS + EXTRA, LANES)), "svv", limit=VMEM_SMALL, micros=1
    )(bits, pack_own, swap(pack_other))
    keep, send = vmem_call(
        second_sum_kernel, (shape(ROWS, LANES), bf(ROWS + EXTRA, LANES)), "svv", limit=VMEM_SMALL, micros=1
    )(bits, keep, joint_hop(send, orders[0]))
    total = vmem_call(third_sum_kernel, wire, "vv", limit=VMEM_SMALL, micros=1)(keep, joint_hop(send, orders[1]))
    for steps in orders[2:]:
        total = vmem_call(wire_sum_kernel, wire, "vv", limit=VMEM_SMALL, micros=1)(total, joint_hop(total, steps))
    second_q = joint_hop(total, orders[1])
    first_q = joint_hop(total, orders[0])
    last_q = joint_hop(second_q, orders[0])
    quarters = (total, second_q, first_q, last_q)
    shared = vmem_call(shared_kernel, bf(2 * FINE, LANES), "svvvv", limit=VMEM_SMALL, micros=1)(bits, *quarters)
    shared_o = swap(shared)

    def turned(x):
        return x.transpose(0, 2, 1)

    def middle(x):
        return x.transpose(1, 0, 2)

    views = (lambda x: x.T, lambda x: x, lambda x: x, turned, middle, lambda x: x)
    params = (
        message_weight, message_weight_moment, message_weight_square,
        state_weight, state_weight_moment, state_weight_square,
        gate_bias, gate_bias_moment, gate_bias_square,
        attend_weight, attend_weight_moment, attend_weight_square,
        dense_first, dense_first_moment, dense_first_square,
        dense_second, dense_second_moment, dense_second_square,
    )
    params = [views[i // 3](p) for i, p in enumerate(params)]
    stepped = vmem_call(
        adam_kernel, tuple(shape(*p.shape) for p in params), "svvvv" + "v" * 18,
        [pltpu.VMEM((4 * COARSE, LANES), F32), pltpu.VMEM((4 * FINE, LANES), F32)], limit=VMEM_ADAM, micros=4,
    )(bits, *quarters, *params)
    back = (lambda x: x.T, lambda x: x, lambda x: x, turned, middle, lambda x: x)
    stepped = [back[i // 3](p) for i, p in enumerate(stepped)]
    rest = (
        target_weight, target_weight_moment, target_weight_square,
        time_param, time_param_moment, time_param_square,
    )
    *others, loss = vmem_call(
        shared_adam_kernel, tuple(shape(*p.shape) for p in rest) + (shape(8, 128),), "svv" + "v" * 6, limit=VMEM_SMALL, micros=2
    )(meta, shared, shared_o, *rest)
    return (
        new_memory, loss[0, 0], live[0, 0], *stepped[:9], *others[3:], *stepped[9:], *others[:3],
    )


def solution(mesh):
    cols = P(None, "head")
    third = P(None, None, "head")
    middle = P(None, "head", None)
    by_row = P("row", None)
    in_specs = (
        (by_row, by_row, P("row"), by_row, P("row"), by_row, by_row, P("row"))
        + (cols,) * 9 + (P(),) * 3 + (third,) * 3 + (middle,) * 3 + (cols,) * 3 + (P(),) * 3
    )
    out_specs = (
        (P("row", "head"), P(), P())
        + (cols,) * 9 + (P(),) * 3 + (third,) * 3 + (middle,) * 3 + (cols,) * 3 + (P(),) * 3
    )
    return jax.shard_map(
        functools.partial(per_device, mesh.shape["row"]),
        mesh=mesh, in_specs=in_specs, out_specs=out_specs, check_vma=False,
    )
```

```python
import functools
import math

import jax
import jax.numpy as jnp
from jax import lax
from jax.experimental import pallas as pl
from jax.experimental.pallas import tpu as pltpu
from jax.sharding import PartitionSpec as P

STEP = 10
LOGIT_SCALE = 0.25
BETA_ONE = 0.9
BETA_TWO = 0.999
RATE = 0.05
EPSILON = 1e-08
BF = jnp.bfloat16
F32 = jnp.float32
PLANE = 4
PAD = 88
LO_BASE = 256
COLS = 128
SAFE_LOGIT = 40.0
VMEM_LIMIT = 58 * 2**20
VMEM_WHOLE = 62 * 2**20
VMEM_SMALL = 12 * 2**20
VMEM_ADAM = 24 * 2**20
TABLE_ROWS_MAX = 16384


def nn(a, b):
    return jnp.dot(a, b, preferred_element_type=F32)


def nt(a, b):
    return lax.dot_general(a, b, (((1,), (1,)), ((), ())), preferred_element_type=F32)


def tn(a, b):
    return lax.dot_general(a, b, (((0,), (0,)), ((), ())), preferred_element_type=F32)


def sigmoid(x):
    return 0.5 * jnp.tanh(0.5 * x) + 0.5


def split3(x):
    first = x.astype(BF)
    rest = x - first.astype(F32)
    second = rest.astype(BF)
    third = (rest - second.astype(F32)).astype(BF)
    return first, second, third


def sin_cos(x):
    turns = jnp.floor(x * (1.0 / math.pi) + 0.5)
    r = ((x - turns * 3.140625) - turns * 0.0009679794311523438) + turns * 3.2584135922775204e-07
    sign = 1.0 - 2.0 * (turns - 2.0 * jnp.floor(turns * 0.5))
    r2 = r * r
    s = SIN[4]
    for k in (3, 2, 1, 0):
        s = s * r2 + SIN[k]
    c = COS[5]
    for k in (4, 3, 2, 1, 0):
        c = c * r2 + COS[k]
    return sign * (r * s), sign * c


SIN = (
    0.9999999956301436,
    -0.16666657831257647,
    0.008333047252581481,
    -0.00019808792312667284,
    2.6045791061554316e-06,
)
COS = (
    0.9999999997746029,
    -0.49999999344091517,
    0.0416666357232742,
    -0.0013888354556677485,
    2.4759808628775167e-05,
    -2.604520000579671e-07,
)


def vmem_call(kernel, out_shape, in_spaces, scratch=(), limit=VMEM_LIMIT, micros=0, in_place=()):
    spaces = {"s": pltpu.SMEM, "v": pltpu.VMEM, "a": pl.ANY}

    def spec(item):
        if isinstance(item, list):
            return tuple(spec(i) for i in item)
        return pl.BlockSpec(memory_space=spaces[item])

    return pl.pallas_call(
        kernel,
        out_shape=out_shape,
        in_specs=[spec(item) for item in in_spaces],
        out_specs=jax.tree.map(
            lambda x: pl.BlockSpec(memory_space=pl.ANY if x in in_place else pltpu.VMEM), out_shape
        ),
        scratch_shapes=list(scratch),
        compiler_params=pltpu.CompilerParams(vmem_limit_bytes=limit),
        cost_estimate=pl.CostEstimate(
            flops=micros * 10**9, bytes_accessed=micros * 10**6, transcendentals=0
        ),
    )


def shape(*dims, dtype=F32):
    return jax.ShapeDtypeStruct(dims, dtype)


def block_kernel(meta, wcount, mem, ids, out):
    width = mem.shape[0]
    events = out.shape[1]
    cols = pl.ds(pl.multiple_of(meta[1] * events, events), events)
    own = ids[:, cols]
    line = lax.broadcasted_iota(jnp.int32, (8, events), 0)
    small = jnp.where(line == 4, own // LO_BASE, own % LO_BASE)
    small = jnp.where(line == 6, wcount[0] // LO_BASE, small)
    small = jnp.where(line == 7, wcount[0] % LO_BASE, small).astype(F32)
    value = mem[:, cols]
    last = jnp.concatenate([value[width - 4 :], small[4:]], 0)
    out[...] = jnp.concatenate([value[: width - 4], last], 0).astype(BF)


def codes_kernel(meta, mem, src, delta, ndelta, tcol, edge, srct, msg, sin_d, code_n, sin_n):
    rows = mem.shape[1]
    events = srct.shape[2]
    nbrs = ndelta.shape[0]
    own = pl.ds(pl.multiple_of(meta[1] * events, events), events)
    pick = (lax.broadcasted_iota(jnp.int32, (rows, events), 0) == src[:, own]).astype(BF)
    parts = split3(mem[...])
    source = nn(parts[0], pick) + nn(parts[1], pick) + nn(parts[2], pick)
    units = source.shape[0] // 2
    fill = jnp.zeros((PAD - units, events), F32)
    for h in range(2):
        srct[h] = jnp.concatenate([source[h * units : (h + 1) * units], fill], 0)
    freq, phase = tcol[:, 0:1], tcol[:, 1:2]
    sin_v, cos_v = sin_cos(delta[:, own] * freq + phase)
    sin_d[...] = sin_v
    msg[...] = jnp.concatenate([source, cos_v, edge[:, own].astype(F32)], 0).astype(BF)

    def body(j, carry):
        cols = pl.ds(pl.multiple_of(j * events, events), events)
        s, c = sin_cos(ndelta[pl.ds(j, 1), own] * freq + phase)
        code_n[:, cols] = c.astype(BF)
        sin_n[:, cols] = s.astype(BF)
        return carry

    lax.fori_loop(0, nbrs, body, 0)


WP_QK, WP_VF, WP_SD, WP_B = 272, 368, 464, 736
WP_ROWS, WP_LANES = 752, 768


def pack_weights_kernel(mw, sw, aw, df, ds, gb, out):
    width, units = ds.shape
    out[0 : 3 * units, 0 : 4 * width] = mw[...].astype(BF)
    out[WP_QK : WP_QK + units, 0 : 4 * width] = jnp.concatenate([aw[0], aw[1]], 1).astype(BF)
    out[WP_VF : WP_VF + units, 0 : 4 * width] = jnp.concatenate([aw[2], df[0], df[1]], 1).astype(BF)
    out[WP_SD : WP_SD + 3 * units, 0:width] = sw[...].T.astype(BF)
    out[WP_SD : WP_SD + width, 256 : 256 + units] = ds[...].astype(BF)
    out[WP_SD : WP_SD + units, 384 : 384 + width] = ds[...].T.astype(BF)
    parts = split3(gb[...])
    small = jnp.concatenate([p.astype(F32) for p in parts] + [jnp.zeros((10, gb.shape[1]), F32)], 0)
    out[WP_B : WP_B + 16, 0 : 3 * units] = small.astype(BF)


def weights_kernel(
    meta, own, other, tw, msg,
    o_md, o_mc, o_q, o_kvm, o_kvc, o_kvct, o_f, o_ft, o_d, o_dt, o_tt, o_gin, o_gst,
):
    width = tw.shape[0]
    units = width // 2
    gates = 3 * units

    def rows_padded(x):
        zero = jnp.zeros((PAD - units, x.shape[1]), F32)
        parts = []
        for k in range(x.shape[0] // units):
            parts += [x[k * units : (k + 1) * units], zero]
        return jnp.concatenate(parts, 0)

    def put(h, w):
        mw = w[0:gates, 0 : 4 * width].astype(F32)
        o_mc[h] = mw[:, 2 * width : 3 * width].astype(BF)
        mw = rows_padded(mw)
        o_md[h] = jnp.concatenate(
            [mw[:, width : 2 * width], jnp.zeros((3 * PAD, 256 - width), F32)], 1
        ).astype(BF)
        rest = jnp.concatenate([mw[:, :width], mw[:, 2 * width :]], 1).astype(BF)
        small = w[WP_B : WP_B + 16, 0:gates].astype(F32)
        bias = (small[0:2] + small[2:4]) + small[4:6]
        bias = jnp.concatenate([bias, jnp.zeros((6, gates), F32)], 0).T
        bias = rows_padded(bias)
        state = rows_padded(w[WP_SD : WP_SD + gates, 0:width].astype(F32)).astype(BF)
        o_gin[h] = nn(rest, msg[...]) + bias[:, 0:1]
        o_gst[h] = nn(state, msg[0:width]) + bias[:, 1:2]
        query = rows_padded(w[WP_QK : WP_QK + units, 0 : 2 * width].astype(F32))
        zero = jnp.zeros((PAD, PAD - units), F32)
        o_q[h] = jnp.concatenate(
            [query[:, :units], zero, query[:, units:width], zero, query[:, width:]], 1
        ).astype(BF)
        key = w[WP_QK : WP_QK + units, 2 * width : 4 * width].astype(F32)
        value = w[WP_VF : WP_VF + units, 0 : 2 * width].astype(F32)
        pair = rows_padded(jnp.concatenate([key, value], 0))
        wide = jnp.concatenate([pair[:, :width], jnp.zeros((2 * PAD, 256 - width), F32)], 1)
        rows = pl.ds(pl.multiple_of(h * 2 * PAD, 2 * PAD), 2 * PAD)
        o_kvm[rows] = wide.astype(BF)
        code = pair[:, width:]
        o_kvc[rows] = code.astype(BF)
        o_kvct[h] = code.T.astype(BF)
        for i in range(2):
            dense = w[WP_VF : WP_VF + units, (2 + i) * width : (3 + i) * width].astype(F32)
            dense = rows_padded(dense)
            o_f[i, h] = dense.astype(BF)
            o_ft[i, h] = dense.T.astype(BF)

    def second(one, two):
        o_d[...] = jnp.concatenate(
            [w[WP_SD : WP_SD + width, 256 : 256 + units].astype(F32) for w in (one, two)], 1
        ).astype(BF)
        o_dt[...] = jnp.concatenate(
            [w[WP_SD : WP_SD + units, 384 : 384 + width].astype(F32) for w in (one, two)], 0
        ).astype(BF)

    @pl.when(meta[1] == 0)
    def _():
        second(own, other)

    @pl.when(meta[1] == 1)
    def _():
        second(other, own)

    put(meta[1], own)
    put(1 - meta[1], other)
    o_tt[...] = tw[...].T.astype(BF)


def step_kernel(
    planes, use_table,
    meta, idx, wcount, own_piece, z_pieces, xy_pieces, far_a, far_b, late_in,
    delta_all, ndelta_all, tcol, w_tt, gathered_in,
    o_fresh, o_own, o_other, o_live,
    sems, mem_all, late, coarse, fine, near, qin, emb, keyt, count, stat, norm,
    scores, probs, fresh_s, gates, acc_m, tgrad,
):
    (
        srct, msg, sin_d, w_md, w_mc, w_q, w_kvm, w_kvct, w_f, w_ft, w_d, w_dt, gin0, gst,
        code_n, w_kvc, sin_n,
    ) = late
    width, events = sin_d.shape
    units = width // 2
    nbrs = ndelta_all.shape[0]
    groups, full, wide_cols = mem_all.shape
    per_group = wide_cols // events
    lookups = (nbrs + 1) * events
    scale = 1.0 / math.sqrt(units)
    row_pos, head = meta[0], meta[1]
    hi_rows = count.shape[0]
    own_cols = pl.ds(pl.multiple_of(head * events, events), events)

    copies = []

    def start(src, dst):
        copy = pltpu.make_async_copy(src, dst, sems.at[len(copies)])
        copy.start()
        copies.append(copy)

    def bring(src, row, half, first, last):
        lanes = pl.ds(pl.multiple_of((lax.rem(row, 2) * 2 + half) * events, events), events)
        start(src, mem_all.at[lax.div(row, 2), pl.ds(first, last - first), lanes])

    cut = z_pieces[0].shape[1]
    first_copy = []
    for r in range(groups):
        first_copy.append(len(copies))
        for e, d in (divmod(2 * r, PLANE), divmod(2 * r + 1, PLANE)):
            row = row_pos ^ (e * PLANE + d)
            for k in range(2):
                half = head ^ k
                if e == 0 and d == 0:
                    bring(own_piece[k], row, half, 0, full)
                elif e == 0:
                    bring(xy_pieces[0][d - 1] if k == 0 else xy_pieces[1].at[d - 1], row, half, 0, full)
                else:
                    bring(z_pieces[k].at[e - 1] if d == 0 else far_a[k][d - 1].at[e - 1], row, half, 0, cut)
                    bring(far_b[k][e - 1].at[d], row, half, cut, full)
    n_memory = len(copies)
    first_copy.append(n_memory)
    for src, dst in zip(late_in, late):
        start(src, dst)
    n_late = len(copies)

    def group_here(r):
        for copy in copies[first_copy[r] : first_copy[r + 1]]:
            copy.wait()
        return lax.div(row_pos, 2) ^ r

    def each_group(work):
        if groups <= 8:
            for r in range(groups):
                work(group_here(r))
        else:
            for r in range(groups):
                group_here(r)
            lax.fori_loop(0, groups, lambda g, s: (work(g), s)[1], 0)

    count[...] = jnp.zeros_like(count)
    norm[...] = jnp.zeros_like(norm)
    stat[...] = jnp.zeros_like(stat)
    target_t = w_tt[...]

    def keys_of(g):
        return nn(target_t, mem_all[g, 0:width]).astype(BF)

    def per_group_rows(g, table):
        x = mem_all[g]
        wide = x.astype(F32)
        keys = keys_of(g)
        if use_table:
            keyt[g, 0:width] = keys
        keys = keys.astype(F32)
        norm[0:1] = jnp.maximum(norm[0:1], jnp.sum(keys * keys, 0, keepdims=True))
        ids = (wide[width : width + 1] * LO_BASE + wide[width + 1 : width + 2]).astype(jnp.int32)
        hot = []
        for size, part in ((hi_rows, ids // COLS), (COLS, ids % COLS)):
            place = lax.broadcasted_iota(jnp.int32, (size, wide_cols), 0).astype(F32)
            hot.append(jnp.where(place == part.astype(F32), 1.0, 0.0).astype(BF))
        count[...] += nt(hot[0], hot[1])
        here = wide[width + 2 : width + 3] * LO_BASE + wide[width + 3 : width + 4]
        for k in range(0, per_group, 2):
            stat[0:1, :] += here[:, k * events : k * events + 128]
        if table is not None:
            turned = wide.T
            base = pl.multiple_of(g * 2 * wide_cols, 2 * wide_cols)
            table[pl.ds(base, wide_cols, stride=2), :] = turned[:, :128]
            table[pl.ds(base + 1, wide_cols, stride=2), :] = jnp.concatenate(
                [turned[:, 128:], jnp.zeros((wide_cols, 256 - full), F32)], 1
            )

    def gather_rows(table, gathered):
        each_group(lambda g: per_group_rows(g, table))
        unroll = 32

        def body(i, carry):
            for u in range(unroll):
                k = i * unroll + u
                gathered[pl.ds(pl.multiple_of(2 * k, 2), 2), :] = table[
                    pl.ds(pl.multiple_of(idx[k], 2), 2), :
                ]
            return carry

        lax.fori_loop(0, lookups // unroll, body, 0)
        for j in range(nbrs + 1):
            low = gathered[pl.ds(2 * j * events, events, stride=2), :]
            high = gathered[pl.ds(2 * j * events + 1, events, stride=2), :]
            near[pl.ds(j * events, events), :] = jnp.concatenate([low, high], 1).astype(BF)

    if use_table:
        pl.run_scoped(
            gather_rows,
            pltpu.VMEM((2 * groups * wide_cols, 128), F32),
            pltpu.VMEM((2 * lookups, 128), F32),
        )
    else:
        each_group(lambda g: per_group_rows(g, None))
        near = gathered_in

    def count_lines(g, keys):
        at = g * (wide_cols // COLS)
        line = jnp.concatenate([count[pl.ds(at + k, 1), :] for k in range(wide_cols // COLS)], 1)
        line = jnp.where(line > 0.5, jnp.log(jnp.maximum(line, 1.0)), -1e30)
        parts = split3(line)
        place = lax.broadcasted_iota(jnp.int32, (16, wide_cols), 0)
        first = full - 16
        tail = jnp.where(place >= width - first, 0.0, keys.astype(F32))
        for k in range(3):
            tail = jnp.where(place == width - first + k, parts[k].astype(F32), tail)
        return tail.astype(BF)

    if use_table:

        def add_lines(g, carry):
            keyt[g, full - 16 : full] = count_lines(g, keyt[g, full - 16 : full])
            return carry

        lax.fori_loop(0, groups, add_lines, 0)

    def keys_with_lines(g):
        if use_table:
            return keyt[g]
        keys = jnp.concatenate([keys_of(g).astype(F32), jnp.zeros((full - width, wide_cols), F32)], 0)
        keys = keys.astype(BF)
        return jnp.concatenate([keys[: full - 16], count_lines(g, keys[full - 16 :])], 0)

    live_rows = stat[0:1, 0:1]

    def rest(kvt, pair):
        for copy in copies[n_memory : n_late - 3]:
            copy.wait()
        dest = near[pl.ds(nbrs * events, events), :]
        dest_t = dest.astype(F32).T[:width]
        dest_key = nn(target_t, dest_t.astype(BF)).astype(BF)
        for h in range(2):
            gate_in = gin0[h] + nt(w_md[h], dest)
            gate_state = gst[h]
            reset = sigmoid(gate_in[:PAD] + gate_state[:PAD])
            update = sigmoid(gate_in[PAD : 2 * PAD] + gate_state[PAD : 2 * PAD])
            state_c = gate_state[2 * PAD :]
            candidate = jnp.tanh(gate_in[2 * PAD :] + reset * state_c)
            for k, v in enumerate((reset, update, candidate, state_c)):
                gates[h, k] = v
            fresh = (1.0 - update) * candidate + update * srct[h]
            o_fresh[h] = fresh
            qin[h * PAD : (h + 1) * PAD] = fresh
        zero_sin, zero_cos = sin_cos(tcol[...])
        qin[2 * PAD :] = jnp.broadcast_to(zero_cos[:, 1:2], (width, events))
        query_in = qin[...].astype(BF)
        copies[n_late - 3].wait()
        copies[n_late - 2].wait()

        def project(j, carry):
            cols = pl.ds(pl.multiple_of(j * events, events), events)
            kvt[:, cols] = nt(w_kvm[...], near[cols, :]) + nn(w_kvc[...], code_n[:, cols])
            return carry

        lax.fori_loop(0, nbrs, project, 0)
        attended_low = []
        for h in range(2):
            key_at, value_at = h * 2 * PAD, h * 2 * PAD + PAD
            queries = nn(w_q[h], query_in)
            fresh_s[h] = queries
            for j in range(nbrs):
                cols = pl.ds(j * events, events)
                scores[j : j + 1] = (
                    jnp.sum(queries * kvt[key_at : key_at + PAD, cols], 0, keepdims=True) * scale
                )
            score = scores[0:nbrs]
            grown = jnp.exp(score - jnp.max(score, 0, keepdims=True))
            prob = grown / jnp.sum(grown, 0, keepdims=True)
            probs[h, 0:nbrs] = prob
            total = jnp.zeros((PAD, events), F32)
            for j in range(nbrs):
                cols = pl.ds(j * events, events)
                total = total + prob[j : j + 1] * kvt[value_at : value_at + PAD, cols]
            attended_low.append(total.astype(BF))
        fresh_lows = [qin[h * PAD : (h + 1) * PAD].astype(BF) for h in range(2)]
        hidden = (nn(w_ft[0, 0], attended_low[0]) + nn(w_ft[0, 1], attended_low[1])) + (
            nn(w_ft[1, 0], fresh_lows[0]) + nn(w_ft[1, 1], fresh_lows[1])
        )
        sigmoid_h = sigmoid(hidden)
        mixed_low = (hidden * sigmoid_h).astype(BF)
        emb[...] = nn(w_dt[...], mixed_low)
        emb_low = emb[...].astype(BF)
        ones_line = (lax.broadcasted_iota(jnp.int32, (full - width, events), 0) < 3).astype(F32)
        emb_aug = jnp.concatenate([LOGIT_SCALE * emb_low.astype(F32), ones_line], 0)
        emb_rows = emb_aug.T.astype(BF)
        emb_norm = jnp.max(jnp.sum(emb[...] * emb[...], 0, keepdims=True))
        bound = LOGIT_SCALE * LOGIT_SCALE * emb_norm * jnp.max(norm[0:1])
        own_logit = LOGIT_SCALE * jnp.sum(
            emb_low.astype(F32) * dest_key.astype(F32), 0, keepdims=True
        )

        def soft_section(acc, top, total):
            total[...] = jnp.zeros_like(total)
            acc[...] = jnp.zeros_like(acc)
            small = bound < SAFE_LOGIT * SAFE_LOGIT

            @pl.when(small)
            def _():
                top[...] = jnp.zeros_like(top)

                def body(g, carry):
                    grown = jnp.exp(nn(emb_rows, keys_with_lines(g)))
                    lanes = grown[:, 0:128]
                    for k in range(1, wide_cols // 128):
                        lanes = lanes + grown[:, k * 128 : (k + 1) * 128]
                    total[...] += lanes
                    acc[...] += nt(grown.astype(BF), mem_all[g])
                    return carry

                lax.fori_loop(0, groups, body, 0)
                total[...] = jnp.broadcast_to(jnp.sum(total[...], 1, keepdims=True), total.shape)

            @pl.when(jnp.logical_not(small))
            def _():
                top[...] = jnp.full_like(top, -1e30)

                def body(g, carry):
                    logits = nn(emb_rows, keys_with_lines(g))
                    old = top[:, 0:1]
                    new = jnp.maximum(old, jnp.max(logits, 1, keepdims=True))
                    grown = jnp.exp(logits - new)
                    fade = jnp.exp(old - new)
                    total[...] = total[...] * fade + jnp.sum(grown, 1, keepdims=True)
                    top[...] = jnp.broadcast_to(new, top.shape)
                    acc[...] = acc[...] * fade + nt(grown.astype(BF), mem_all[g])
                    return carry

                lax.fori_loop(0, groups, body, 0)

            acc_m[...] = (acc[...] / total[:, 0:1]).T
            probs[2] = jnp.broadcast_to(top[:, 0:1] + jnp.log(total[:, 0:1]), (events, 128)).T[:16]

        pl.run_scoped(
            soft_section,
            pltpu.VMEM((events, full), F32),
            pltpu.VMEM((events, 128), F32),
            pltpu.VMEM((events, 128), F32),
        )
        log_total = probs[2, 0:1]
        position = lax.broadcasted_iota(jnp.int32, (1, events), 1) + head * events
        live = (position < wcount[0]).astype(F32)
        loss = jnp.sum((log_total - own_logit) * live, 1, keepdims=True)
        weight = live / live_rows
        own_prob = jnp.exp(own_logit - log_total)
        own_grad = ((own_prob - 1.0) * weight).astype(BF).astype(F32) - own_prob * weight
        mean_mem = acc_m[:width]
        spread = weight * mean_mem + own_grad * dest_t
        parts = split3(spread)
        target_grad = LOGIT_SCALE * (nt(parts[0], emb_low) + nt(parts[1], emb_low) + nt(parts[2], emb_low))
        parts = split3(mean_mem)
        mean_key = nn(target_t, parts[0]) + nn(target_t, parts[1]) + nn(target_t, parts[2])
        emb_grad = LOGIT_SCALE * (weight * mean_key + own_grad * dest_key.astype(F32))

        coarse[...] = jnp.zeros_like(coarse)
        fine[...] = jnp.zeros_like(fine)
        blocks = state_blocks(units)
        quarter = units // 2

        def slot(h):
            return h ^ head

        emb_grad_low = emb_grad.astype(BF)
        mixed_grad = nn(w_d[...], emb_grad_low)
        second = nt(mixed_low, emb_grad_low)
        hidden_grad = (mixed_grad * sigmoid_h * (1.0 + hidden * (1.0 - sigmoid_h))).astype(BF)
        for h in range(2):
            place = slot(h)
            for i, v in enumerate((attended_low[h], fresh_lows[h])):
                fine[place, units:width, (2 + i) * width : (3 + i) * width] = nt(v, hidden_grad)[:units]
            for k in range(2):
                fine[place, ROW_T : ROW_T + quarter, k * width : (k + 1) * width] = target_grad[
                    h * units + k * quarter : h * units + (k + 1) * quarter
                ]
            for k in range(4):
                at = 2 * width + k * units
                fine[place, ROW_T : ROW_T + quarter, at : at + units] = second[
                    k * quarter : (k + 1) * quarter, h * units : (h + 1) * units
                ]

        copies[n_late - 1].wait()
        tgrad[...] = jnp.zeros_like(tgrad)
        query_lows = []
        prob_terms = []
        att_grads = []
        for h in range(2):
            value_at = h * 2 * PAD + PAD
            att_grad = nn(w_f[0, h], hidden_grad)
            prob = probs[h, 0:nbrs]
            for j in range(nbrs):
                cols = pl.ds(j * events, events)
                scores[j : j + 1] = jnp.sum(
                    att_grad * kvt[value_at : value_at + PAD, cols], 0, keepdims=True
                )
            prob_grad = scores[0:nbrs]
            prob_terms.append(prob * (prob_grad - jnp.sum(prob * prob_grad, 0, keepdims=True)))
            att_grads.append(att_grad)
            total = jnp.zeros((PAD, events), F32)
            key_at = h * 2 * PAD
            for j in range(nbrs):
                cols = pl.ds(j * events, events)
                total = total + prob_terms[h][j : j + 1] * kvt[key_at : key_at + PAD, cols]
            query_lows.append((total * scale).astype(BF))
        for j in range(nbrs):
            cols = pl.ds(j * events, events)
            pieces = []
            for h in range(2):
                pieces += [
                    (prob_terms[h][j : j + 1] * scale) * fresh_s[h], probs[h, j : j + 1] * att_grads[h],
                ]
            pair_j = jnp.concatenate(pieces, 0).astype(BF)
            pair[:, cols] = pair_j
            code_grad = nn(w_kvct[0], pair_j[: 2 * PAD]) + nn(w_kvct[1], pair_j[2 * PAD :])
            slope = sin_n[:, cols].astype(F32) * code_grad
            tgrad[1, :width] -= slope
            tgrad[0, :width] -= slope * ndelta_all[j : j + 1, own_cols]
        near_grad = nn(pair[...], near[pl.ds(0, nbrs * events), :])
        code_wgrad = nt(pair[...], code_n[...])
        for h in range(2):
            place = slot(h)
            base = h * 2 * PAD
            query_grad = nt(query_lows[h], query_in)
            fine[place, 0:units, 0:units] = query_grad[:units, 0:units]
            fine[place, 0:units, units:width] = query_grad[:units, PAD : PAD + units]
            fine[place, 0:units, width : 2 * width] = query_grad[:units, 2 * PAD :]
            for k, (row, lane) in enumerate(((0, 2 * width), (units, 0))):
                at = base + k * PAD
                fine[place, row : row + units, lane : lane + width] = near_grad[
                    at : at + units, :width
                ]
                fine[place, row : row + units, lane + width : lane + 2 * width] = code_wgrad[
                    at : at + units
                ]
        query_in_grad = tn(w_q[0], query_lows[0]) + tn(w_q[1], query_lows[1])
        zero_term = zero_sin[:, 1:2] * query_in_grad[2 * PAD :]
        tgrad[1, :width] -= zero_term

        def send_fine(k):
            for place, out in ((1, o_other), (0, o_own)):
                start(fine.at[place, pl.ds(k * FINE, FINE)], out.at[k, pl.ds(COARSE, FINE)])

        for k in range(3):
            send_fine(k)

        code_dt_grad = jnp.zeros((width, events), F32)
        ones = jnp.ones((8, events), BF)
        for h in range(2):
            place = slot(h)
            reset, update, candidate, state_c = (gates[h, k] for k in range(4))
            fresh_grad = nn(w_f[1, h], hidden_grad) + query_in_grad[h * PAD : (h + 1) * PAD]
            own_state = srct[h]
            candidate_pre = fresh_grad * (1.0 - update) * (1.0 - candidate * candidate)
            update_pre = fresh_grad * (own_state - candidate) * update * (1.0 - update)
            reset_pre = candidate_pre * state_c * reset * (1.0 - reset)
            last_pre = candidate_pre * reset
            shared = [reset_pre[:units], update_pre[:units]]
            in_grad = jnp.concatenate(shared + [candidate_pre[:units]], 0).astype(BF)
            state_grad = jnp.concatenate(shared + [last_pre[:units]], 0).astype(BF)
            gate_rows = 3 * units
            coarse[place, 0:gate_rows, width : 2 * width] = nn(in_grad, dest)[:, :width]
            rest_grad = nt(in_grad, msg[...])
            coarse[place, 0:gate_rows, 0:width] = rest_grad[:, :width]
            coarse[place, 0:gate_rows, 2 * width : 4 * width] = rest_grad[:, width:]
            state_w = nt(msg[0:width], state_grad)
            coarse[place, 0:width, 4 * width : 4 * width + gate_rows - 256] = state_w[:, 256:]
            for k, (first, last) in enumerate(blocks):
                coarse[place, gate_rows : gate_rows + last - first, k * 256 : (k + 1) * 256] = state_w[
                    first:last, 0:256
                ]
            fine[place, ROW_B : ROW_B + 1, 0:gate_rows] = nt(ones, in_grad)[0:1]
            fine[place, ROW_B + 1 : ROW_B + 2, 0:gate_rows] = nt(ones, state_grad)[0:1]
            code_dt_grad = code_dt_grad + tn(w_mc[h], in_grad)
        slope = sin_d[...] * code_dt_grad
        tgrad[1, :width] -= slope
        tgrad[0, :width] -= slope * delta_all[:, own_cols]
        ones_f = jnp.ones((8, events), F32)
        for i in range(2):
            line = lax.dot_general(
                ones_f, tgrad[i, :width], (((1,), (1,)), ((), ())),
                precision=lax.Precision.HIGHEST, preferred_element_type=F32,
            )[0:1]
            for place in range(2):
                fine[place, ROW_B + 2 + i : ROW_B + 3 + i, 0:width] = line
        for place in range(2):
            fine[place, ROW_B + 4 : ROW_B + 5, 0:128] = jnp.broadcast_to(loss, (1, 128))
        o_live[...] = jnp.broadcast_to(stat[0:1, :], o_live.shape)
        send_fine(3)
        for k in range(4):
            for place, out in ((1, o_other), (0, o_own)):
                start(coarse.at[place, pl.ds(k * COARSE, COARSE)], out.at[k, pl.ds(0, COARSE)])
        for copy in copies[n_late:]:
            copy.wait()

    pl.run_scoped(
        rest,
        pltpu.VMEM((4 * PAD, nbrs * events), F32),
        pltpu.VMEM((4 * PAD, nbrs * events), BF),
    )


COARSE, FINE, LANES = 80, 64, 768
ROWS = COARSE + FINE
EXTRA = 16
ROW_T, ROW_B = 192, 240


def state_blocks(units):
    room = 4 * COARSE - 3 * units
    return [(k * room, min((k + 1) * room, 2 * units)) for k in range(3)]


def to_half_wire(out, value):
    high = value.astype(BF)
    out[0:ROWS] = high
    out[ROWS:] = (value - high.astype(F32))[ROWS - EXTRA :].astype(BF)


def from_half_wire(w):
    high = w[0:ROWS].astype(F32)
    last = high[ROWS - EXTRA :] + w[ROWS:].astype(F32)
    return jnp.concatenate([high[: ROWS - EXTRA], last], 0)


def to_wire(out, value):
    high = value.astype(BF)
    out[0:ROWS] = high
    out[ROWS:] = (value - high.astype(F32)).astype(BF)


def from_wire(w):
    return w[0:ROWS].astype(F32) + w[ROWS:].astype(F32)


def first_sum_kernel(bits, own, got, o_keep, o_send):
    for k in range(2):
        q = bits[0] * 2 + k
        o_keep[k] = own[q] + got[q]
        q = (1 - bits[0]) * 2 + k
        to_half_wire(o_send.at[k], own[q] + got[q])


def second_sum_kernel(bits, keep, got, o_keep, o_send):
    q = bits[1]
    o_keep[...] = keep[q] + from_half_wire(got[q])
    q = 1 - bits[1]
    to_half_wire(o_send, keep[q] + from_half_wire(got[q]))


def third_sum_kernel(bits, keep, got, o_keep, o_send):
    half = ROWS // 2
    total = keep[...] + from_half_wire(got[...])
    for b in range(2):

        @pl.when(bits[2] == b)
        def _(b=b):
            o_keep[...] = total[b * half : (b + 1) * half]
            eighth_wire(o_send, total[(1 - b) * half : (2 - b) * half])


def eighth_wire(out, value):
    half = ROWS // 2
    high = value.astype(BF).astype(F32)
    out[...] = jnp.concatenate([high, value - high], 0).astype(BF)


def fourth_sum_kernel(keep, got, o_send):
    half = ROWS // 2
    wide = got[...].astype(F32)
    eighth_wire(o_send, keep[...] + (wide[0:half] + wide[half:]))


def eighth_sum_kernel(one, two, o_send):
    half = ROWS // 2
    a, b = one[...].astype(F32), two[...].astype(F32)
    eighth_wire(o_send, (a[0:half] + a[half:]) + (b[0:half] + b[half:]))


def join_kernel(bits, one, two, o_send):
    half = ROWS // 2
    a, b = one[...].astype(F32), two[...].astype(F32)
    first = jnp.where(bits[2] == 0, a, b)
    second = jnp.where(bits[2] == 0, b, a)
    o_send[...] = jnp.concatenate([first[:half], second[:half], first[half:], second[half:]], 0).astype(BF)


def quarter_of(bits, k):
    one = bits[0] if k < 2 else 1 - bits[0]
    two = bits[1] if k % 2 == 0 else 1 - bits[1]
    return one * 2 + two


def shared_kernel(bits, w0, w1, w2, w3, out):
    for k, w in enumerate((w0, w1, w2, w3)):

        @pl.when(quarter_of(bits, k) == 3)
        def _(w=w):
            out[0:FINE] = w[COARSE:ROWS]
            out[FINE:] = w[ROWS + COARSE :]


def adam_kernel(bits, w0, w1, w2, w3, *refs):
    params, outs = refs[:18], refs[18:36]
    coarse, fine = refs[36:]
    for k, w in enumerate((w0, w1, w2, w3)):
        q = quarter_of(bits, k)
        value = from_wire(w[...])
        coarse[pl.ds(pl.multiple_of(q * COARSE, COARSE), COARSE)] = value[0:COARSE]
        fine[pl.ds(pl.multiple_of(q * FINE, FINE), FINE)] = value[COARSE:]
    units, gates = params[15].shape[1], params[3].shape[1]
    width = 2 * units

    def step(which, at, gradient):
        values = [params[3 * which + i][at] for i in range(3)]
        for i, v in enumerate(adam_step(*values, gradient)):
            outs[3 * which + i][at] = v

    every = (slice(None), slice(None))
    step(0, every, coarse[0:gates, 0 : 4 * width])
    for k, (first, last) in enumerate(state_blocks(units)):
        step(
            1, (slice(first, last), slice(0, 256)),
            coarse[gates : gates + last - first, k * 256 : (k + 1) * 256],
        )
    step(1, (slice(None), slice(256, gates)), coarse[0:width, 4 * width : 4 * width + gates - 256])
    step(2, every, fine[ROW_B : ROW_B + 2, 0:gates])
    step(3, 0, fine[0:units, 0 : 2 * width])
    step(3, 1, fine[0:units, 2 * width : 4 * width])
    step(3, 2, fine[units:width, 0 : 2 * width])
    for i in range(2):
        step(4, (slice(None), i), fine[units:width, (2 + i) * width : (3 + i) * width])
    quarter = units // 2
    for k in range(4):
        at = 2 * width + k * units
        step(5, (slice(k * quarter, (k + 1) * quarter), slice(None)), fine[ROW_T : ROW_T + quarter, at : at + units])


def shared_adam_kernel(meta, own, other, *refs):
    params, outs, o_loss = refs[:6], refs[6:12], refs[12]
    width = params[0].shape[0]
    quarter = width // 4

    def step(which, at, gradient):
        values = [params[3 * which + i][at] for i in range(3)]
        for i, v in enumerate(adam_step(*values, gradient)):
            outs[3 * which + i][at] = v

    def run(first, second):
        parts = [w[0:FINE].astype(F32) + w[FINE:].astype(F32) for w in (first, second)]
        for h in range(2):
            for k in range(2):
                at = (h * 2 + k) * quarter
                step(
                    0, (slice(at, at + quarter), slice(None)),
                    parts[h][0:quarter, k * width : (k + 1) * width],
                )
        row = ROW_B - 3 * FINE
        step(1, (slice(None), slice(None)), parts[0][row + 2 : row + 4, 0:width])
        o_loss[...] = jnp.broadcast_to(parts[0][row + 4 : row + 5, 0:128], o_loss.shape)

    @pl.when(meta[1] == 0)
    def _():
        run(own, other)

    @pl.when(meta[1] == 1)
    def _():
        run(other, own)


def memory_kernel(mem, fresh, src, wcount, out):
    units, rows = mem.shape
    pick = (lax.broadcasted_iota(jnp.int32, (rows, rows), 1) == src[...]).astype(BF)
    parts = split3(fresh[0:units])
    moved = nn(parts[0], pick) + nn(parts[1], pick) + nn(parts[2], pick)
    alive = (lax.broadcasted_iota(jnp.int32, (16, rows), 1) < wcount[0]).astype(BF)
    hit = nn(alive, pick)[0:1] > 0.5
    out[...] = jnp.where(hit, moved, mem[...])


def adam_step(master, moment, square, gradient):
    moment_new = BETA_ONE * moment + (1.0 - BETA_ONE) * gradient
    square_new = BETA_TWO * square + (1.0 - BETA_TWO) * gradient * gradient
    master_new = master - RATE * (moment_new / (1.0 - BETA_ONE**STEP)) / (
        jnp.sqrt(square_new / (1.0 - BETA_TWO**STEP)) + EPSILON
    )
    return (master_new, moment_new, square_new)


def axis_orders(n_row):
    bits = []
    step = PLANE
    while step < n_row:
        bits.append(step)
        step *= 2
    first = [1, 2] + bits
    second = bits[:2] + [1, 2] + bits[2:]
    return list(zip(first, second))


def flips(count, step):
    return [(i, i ^ step) for i in range(count)]


def per_device(
    n_row,
    memory, sources, dest_ids, neighbours, delta_t, nbr_delta, edge_feat, window_count,
    message_weight, message_weight_moment, message_weight_square,
    state_weight, state_weight_moment, state_weight_square,
    gate_bias, gate_bias_moment, gate_bias_square,
    time_param, time_param_moment, time_param_square,
    attend_weight, attend_weight_moment, attend_weight_square,
    dense_first, dense_first_moment, dense_first_square,
    dense_second, dense_second_moment, dense_second_square,
    target_weight, target_weight_moment, target_weight_square,
):
    rows, width = memory.shape
    units = width // 2
    events = rows // 2
    nbrs = neighbours.shape[1]
    planes = n_row // PLANE
    total_rows = n_row * rows
    head = lax.axis_index("head")
    row = lax.axis_index("row")
    meta = jnp.stack([row, head]).astype(jnp.int32)

    def own(x, axis):
        return lax.dynamic_slice_in_dim(x, head * events, events, axis)

    def swap(x):
        return lax.ppermute(x, "head", [(0, 1), (1, 0)])

    def hop(x, step):
        return lax.ppermute(x, "row", flips(n_row, step))

    bf = functools.partial(shape, dtype=BF)
    full = -(-(width + 4) // 16) * 16

    mem_t = memory.T
    block = vmem_call(block_kernel, bf(full, events), "ssvv", micros=1)(
        meta, window_count, mem_t, dest_ids[None]
    )
    cut = 128
    near_z = [hop(block[:cut], e * PLANE) for e in range(1, planes)]
    near_xy = [hop(block, d) for d in range(1, PLANE)]
    mw, aw, gb = message_weight.T, attend_weight.transpose(0, 2, 1), gate_bias
    packed = vmem_call(pack_weights_kernel, bf(WP_ROWS, WP_LANES), "vvvvvv", limit=VMEM_SMALL, micros=2)(
        mw, state_weight, aw, dense_first, dense_second, gb
    )
    line_a = jnp.stack(near_z)
    plane_b = jnp.stack([block[cut:]] + [p[cut:] for p in near_xy])
    line_a, plane_b = lax.optimization_barrier((line_a, plane_b))
    packed, _ = lax.optimization_barrier((packed, line_a))
    packed_o = swap(packed)
    far_a = tuple(hop(line_a, d) for d in range(1, PLANE))
    far_b = tuple(hop(plane_b, e * PLANE) for e in range(1, planes))
    delta, ndelta, edge, tcol, packed_o, _ = lax.optimization_barrier(
        (delta_t[None], nbr_delta.T, edge_feat.T, time_param.T, packed_o, plane_b)
    )
    code_shapes = (
        shape(2, PAD, events), bf(3 * width, events), shape(width, events),
        bf(width, nbrs * events), bf(width, nbrs * events),
    )
    srct, msg, sin_d, code_n, sin_n = vmem_call(codes_kernel, code_shapes, "svvvvvv", micros=9)(
        meta, mem_t, sources, delta, ndelta, tcol, edge
    )
    w_shapes = (
        bf(2, 3 * PAD, 256), bf(2, 3 * units, width), bf(2, PAD, 2 * PAD + width),
        bf(4 * PAD, 256), bf(4 * PAD, width), bf(2, width, 2 * PAD),
        bf(2, 2, PAD, width), bf(2, 2, width, PAD), bf(width, width), bf(width, width),
        bf(width, width), shape(2, 3 * PAD, events), shape(2, 3 * PAD, events),
    )
    w_md, w_mc, w_q, w_kvm, w_kvc, w_kvct, w_f, w_ft, w_d, w_dt, w_tt, gin0, gst = vmem_call(weights_kernel, w_shapes, "svvvv", micros=6)(
        meta, packed, packed_o, target_weight, msg
    )

    far_a, far_b, _ = lax.optimization_barrier((far_a, far_b, w_md))
    block, line_a, near_xy, _ = lax.optimization_barrier((block, line_a, near_xy, srct))
    own_piece = (block, swap(block))
    z_pieces = (line_a, swap(line_a))
    xy_pieces = (tuple(near_xy), swap(jnp.stack(near_xy)))
    far_a = (far_a, tuple(swap(p) for p in far_a))
    far_b = (far_b, tuple(swap(p) for p in far_b))

    index = jnp.concatenate([own(neighbours.T, 1).reshape(-1), own(dest_ids, 0)])
    use_table = total_rows <= TABLE_ROWS_MAX
    lookups = (nbrs + 1) * events
    if use_table:
        gathered = tcol
    else:
        parts = {}
        for k in range(2):
            parts[0, 0, k] = own_piece[k]
            for e in range(1, planes):
                parts[e, 0, k] = jnp.concatenate([z_pieces[k][e - 1], far_b[k][e - 1][0]], 0)
            for d in range(1, PLANE):
                parts[0, d, k] = xy_pieces[k][d - 1]
                for e in range(1, planes):
                    parts[e, d, k] = jnp.concatenate([far_a[k][d - 1][e - 1], far_b[k][e - 1][d]], 0)
        table = jnp.stack([parts[e, d, k].T for e in range(planes) for d in range(PLANE) for k in range(2)])
        half = (index % rows) // events
        gathered = table[((index // rows) ^ row) * 2 + (half ^ head), index % events]
        gathered = jnp.pad(gathered, ((0, 0), (0, 256 - full)))
    hi_rows = total_rows // COLS
    wide_cols = 4 * events
    groups = total_rows // wide_cols
    late = (
        srct, msg, sin_d, w_md, w_mc, w_q, w_kvm, w_kvct, w_f, w_ft, w_d, w_dt, gin0, gst, code_n, w_kvc, sin_n,
    )
    n_copies = 2 * (1 + (planes - 1) + (PLANE - 1) * planes + (planes - 1) * PLANE) + len(late) + 16
    scratch = [
        pltpu.SemaphoreType.DMA((n_copies,)),
        pltpu.VMEM((groups, full, wide_cols), BF),
        tuple(pltpu.VMEM(x.shape, x.dtype) for x in late),
        pltpu.VMEM((2, 4 * COARSE, LANES), F32),
        pltpu.VMEM((2, 4 * FINE, LANES), F32),
        pltpu.VMEM((lookups if use_table else 16, 256), BF),
        pltpu.VMEM((2 * PAD + width, events), F32),
        pltpu.VMEM((width, events), F32),
        pltpu.VMEM((groups if use_table else 1, full, wide_cols), BF),
        pltpu.VMEM((hi_rows, COLS), F32),
        pltpu.VMEM((8, 128), F32),
        pltpu.VMEM((8, wide_cols), F32),
        pltpu.VMEM((16, events), F32),
        pltpu.VMEM((3, 16, events), F32),
        pltpu.VMEM((2, PAD, events), F32),
        pltpu.VMEM((2, 4, PAD, events), F32),
        pltpu.VMEM((full, events), F32),
        pltpu.VMEM((2, PAD * 2, events), F32),
    ]
    spaces = [
        "s", "s", "s", ["a", "a"], ["a", "a"], [["a"] * (PLANE - 1), "a"],
        [["a"] * (PLANE - 1)] * 2, [["a"] * (planes - 1)] * 2, ["a"] * len(late),
    ] + ["v"] * 5
    fresh, pack_own, pack_other, live = vmem_call(
        functools.partial(step_kernel, planes, use_table),
        (
            shape(2, PAD, events), shape(4, ROWS, LANES), shape(4, ROWS, LANES), shape(8, 128),
        ),
        spaces,
        scratch,
        VMEM_LIMIT if use_table else VMEM_WHOLE,
        micros=40,
        in_place=(shape(4, ROWS, LANES),),
    )(
        meta, 2 * index, window_count, own_piece, z_pieces, xy_pieces, far_a, far_b, late,
        delta, ndelta, tcol, w_tt, gathered,
    )

    fresh_own = lax.dynamic_index_in_dim(fresh, head, 0, False)
    fresh_sent = swap(lax.dynamic_index_in_dim(fresh, 1 - head, 0, False))
    both = jnp.where(
        head == 0,
        jnp.concatenate([fresh_own, fresh_sent], 1),
        jnp.concatenate([fresh_sent, fresh_own], 1),
    )
    base_cols = lax.dynamic_slice_in_dim(mem_t, head * units, units, 0)
    new_memory = vmem_call(memory_kernel, shape(units, rows), "vvvs", limit=VMEM_SMALL, micros=3)(
        base_cols, both, sources.reshape(rows, 1), window_count
    ).T

    orders = axis_orders(n_row)

    def joint_hop(x, steps):
        pairs = [(2 * i + c, 2 * (i ^ steps[c]) + c) for i in range(n_row) for c in range(2)]
        return lax.ppermute(x, ("row", "head"), pairs)

    bits = jnp.stack(
        [jnp.where(head == 0, (row // steps[0]) % 2, (row // steps[1]) % 2) for steps in orders[:3]]
    ).astype(jnp.int32)
    wire = bf(2 * ROWS, LANES)
    keep, send = vmem_call(
        first_sum_kernel, (shape(2, ROWS, LANES), bf(2, ROWS + EXTRA, LANES)), "svv", limit=VMEM_SMALL, micros=1
    )(bits, pack_own, swap(pack_other))
    keep, send = vmem_call(
        second_sum_kernel, (shape(ROWS, LANES), bf(ROWS + EXTRA, LANES)), "svv", limit=VMEM_SMALL, micros=1
    )(bits, keep, joint_hop(send, orders[0]))
    keep, send = vmem_call(
        third_sum_kernel, (shape(ROWS // 2, LANES), bf(ROWS, LANES)), "svv", limit=VMEM_SMALL, micros=1
    )(bits, keep, joint_hop(send, orders[1]))
    eighth = bf(ROWS, LANES)
    part = vmem_call(fourth_sum_kernel, eighth, "vv", limit=VMEM_SMALL, micros=1)(
        keep, joint_hop(send, orders[2])
    )
    for steps in orders[3:]:
        part = vmem_call(eighth_sum_kernel, eighth, "vv", limit=VMEM_SMALL, micros=1)(
            part, joint_hop(part, steps)
        )
    total = vmem_call(join_kernel, wire, "svv", limit=VMEM_SMALL, micros=1)(
        bits, part, joint_hop(part, orders[2])
    )
    second_q = joint_hop(total, orders[1])
    first_q = joint_hop(total, orders[0])
    last_q = joint_hop(second_q, orders[0])
    quarters = (total, second_q, first_q, last_q)
    shared = vmem_call(shared_kernel, bf(2 * FINE, LANES), "svvvv", limit=VMEM_SMALL, micros=1)(bits, *quarters)
    shared_o = swap(shared)

    def turned(x):
        return x.transpose(0, 2, 1)

    def middle(x):
        return x.transpose(1, 0, 2)

    views = (lambda x: x.T, lambda x: x, lambda x: x, turned, middle, lambda x: x)
    params = (
        message_weight, message_weight_moment, message_weight_square,
        state_weight, state_weight_moment, state_weight_square,
        gate_bias, gate_bias_moment, gate_bias_square,
        attend_weight, attend_weight_moment, attend_weight_square,
        dense_first, dense_first_moment, dense_first_square,
        dense_second, dense_second_moment, dense_second_square,
    )
    params = [views[i // 3](p) for i, p in enumerate(params)]
    stepped = vmem_call(
        adam_kernel, tuple(shape(*p.shape) for p in params), "svvvv" + "v" * 18,
        [pltpu.VMEM((4 * COARSE, LANES), F32), pltpu.VMEM((4 * FINE, LANES), F32)], limit=VMEM_ADAM, micros=4,
    )(bits, *quarters, *params)
    back = (lambda x: x.T, lambda x: x, lambda x: x, turned, middle, lambda x: x)
    stepped = [back[i // 3](p) for i, p in enumerate(stepped)]
    rest = (
        target_weight, target_weight_moment, target_weight_square,
        time_param, time_param_moment, time_param_square,
    )
    *others, loss = vmem_call(
        shared_adam_kernel, tuple(shape(*p.shape) for p in rest) + (shape(8, 128),), "svv" + "v" * 6, limit=VMEM_SMALL, micros=2
    )(meta, shared, shared_o, *rest)
    return (
        new_memory, loss[0, 0], live[0, 0], *stepped[:9], *others[3:], *stepped[9:], *others[:3],
    )


def solution(mesh):
    cols = P(None, "head")
    third = P(None, None, "head")
    middle = P(None, "head", None)
    by_row = P("row", None)
    in_specs = (
        (by_row, by_row, P("row"), by_row, P("row"), by_row, by_row, P("row"))
        + (cols,) * 9 + (P(),) * 3 + (third,) * 3 + (middle,) * 3 + (cols,) * 3 + (P(),) * 3
    )
    out_specs = (
        (P("row", "head"), P(), P())
        + (cols,) * 9 + (P(),) * 3 + (third,) * 3 + (middle,) * 3 + (cols,) * 3 + (P(),) * 3
    )
    return jax.shard_map(
        functools.partial(per_device, mesh.shape["row"]),
        mesh=mesh, in_specs=in_specs, out_specs=out_specs, check_vma=False,
    )
```

```python
import functools
import math

import jax
import jax.numpy as jnp
from jax import lax
from jax.experimental import pallas as pl
from jax.experimental.pallas import tpu as pltpu
from jax.sharding import PartitionSpec as P

STEP = 10
LOGIT_SCALE = 0.25
BETA_ONE = 0.9
BETA_TWO = 0.999
RATE = 0.05
EPSILON = 1e-08
BF = jnp.bfloat16
F32 = jnp.float32
PLANE = 4
PAD = 88
LO_BASE = 256
COLS = 128
SAFE_LOGIT = 40.0
VMEM_LIMIT = 58 * 2**20
VMEM_WHOLE = 62 * 2**20
VMEM_SMALL = 12 * 2**20
VMEM_ADAM = 24 * 2**20
TABLE_ROWS_MAX = 16384


def nn(a, b):
    return jnp.dot(a, b, preferred_element_type=F32)


def nt(a, b):
    return lax.dot_general(a, b, (((1,), (1,)), ((), ())), preferred_element_type=F32)


def tn(a, b):
    return lax.dot_general(a, b, (((0,), (0,)), ((), ())), preferred_element_type=F32)


def sigmoid(x):
    return 0.5 * jnp.tanh(0.5 * x) + 0.5


def split3(x):
    first = x.astype(BF)
    rest = x - first.astype(F32)
    second = rest.astype(BF)
    third = (rest - second.astype(F32)).astype(BF)
    return first, second, third


def sin_cos(x):
    turns = jnp.floor(x * (1.0 / math.pi) + 0.5)
    r = ((x - turns * 3.140625) - turns * 0.0009679794311523438) + turns * 3.2584135922775204e-07
    sign = 1.0 - 2.0 * (turns - 2.0 * jnp.floor(turns * 0.5))
    r2 = r * r
    s = SIN[4]
    for k in (3, 2, 1, 0):
        s = s * r2 + SIN[k]
    c = COS[5]
    for k in (4, 3, 2, 1, 0):
        c = c * r2 + COS[k]
    return sign * (r * s), sign * c


SIN = (
    0.9999999956301436,
    -0.16666657831257647,
    0.008333047252581481,
    -0.00019808792312667284,
    2.6045791061554316e-06,
)
COS = (
    0.9999999997746029,
    -0.49999999344091517,
    0.0416666357232742,
    -0.0013888354556677485,
    2.4759808628775167e-05,
    -2.604520000579671e-07,
)


def vmem_call(kernel, out_shape, in_spaces, scratch=(), limit=VMEM_LIMIT, micros=0, in_place=()):
    spaces = {"s": pltpu.SMEM, "v": pltpu.VMEM, "a": pl.ANY}

    def spec(item):
        if isinstance(item, list):
            return tuple(spec(i) for i in item)
        return pl.BlockSpec(memory_space=spaces[item])

    return pl.pallas_call(
        kernel,
        out_shape=out_shape,
        in_specs=[spec(item) for item in in_spaces],
        out_specs=jax.tree.map(
            lambda x: pl.BlockSpec(memory_space=pl.ANY if x in in_place else pltpu.VMEM), out_shape
        ),
        scratch_shapes=list(scratch),
        compiler_params=pltpu.CompilerParams(vmem_limit_bytes=limit),
        cost_estimate=pl.CostEstimate(
            flops=micros * 10**9, bytes_accessed=micros * 10**6, transcendentals=0
        ),
    )


def shape(*dims, dtype=F32):
    return jax.ShapeDtypeStruct(dims, dtype)


def block_kernel(meta, wcount, mem, ids, out):
    width = mem.shape[0]
    events = out.shape[1]
    cols = pl.ds(pl.multiple_of(meta[1] * events, events), events)
    own = ids[:, cols]
    line = lax.broadcasted_iota(jnp.int32, (8, events), 0)
    small = jnp.where(line == 4, own // LO_BASE, own % LO_BASE)
    small = jnp.where(line == 6, wcount[0] // LO_BASE, small)
    small = jnp.where(line == 7, wcount[0] % LO_BASE, small).astype(F32)
    value = mem[:, cols]
    last = jnp.concatenate([value[width - 4 :], small[4:]], 0)
    out[...] = jnp.concatenate([value[: width - 4], last], 0).astype(BF)


def codes_kernel(meta, mem, src, delta, ndelta, tcol, edge, srct, msg, sin_d, code_n, sin_n):
    rows = mem.shape[1]
    events = srct.shape[2]
    nbrs = ndelta.shape[0]
    own = pl.ds(pl.multiple_of(meta[1] * events, events), events)
    pick = (lax.broadcasted_iota(jnp.int32, (rows, events), 0) == src[:, own]).astype(BF)
    parts = split3(mem[...])
    source = nn(parts[0], pick) + nn(parts[1], pick) + nn(parts[2], pick)
    units = source.shape[0] // 2
    fill = jnp.zeros((PAD - units, events), F32)
    for h in range(2):
        srct[h] = jnp.concatenate([source[h * units : (h + 1) * units], fill], 0)
    freq, phase = tcol[:, 0:1], tcol[:, 1:2]
    sin_v, cos_v = sin_cos(delta[:, own] * freq + phase)
    sin_d[...] = sin_v
    msg[...] = jnp.concatenate([source, cos_v, edge[:, own].astype(F32)], 0).astype(BF)

    def body(j, carry):
        cols = pl.ds(pl.multiple_of(j * events, events), events)
        s, c = sin_cos(ndelta[pl.ds(j, 1), own] * freq + phase)
        code_n[:, cols] = c.astype(BF)
        sin_n[:, cols] = s.astype(BF)
        return carry

    lax.fori_loop(0, nbrs, body, 0)


WP_QK, WP_VF, WP_SD, WP_B = 272, 368, 464, 736
WP_ROWS, WP_LANES = 752, 768


def pack_weights_kernel(mw, sw, aw, df, ds, gb, out):
    width, units = ds.shape
    out[0 : 3 * units, 0 : 4 * width] = mw[...].astype(BF)
    out[WP_QK : WP_QK + units, 0 : 4 * width] = jnp.concatenate([aw[0], aw[1]], 1).astype(BF)
    out[WP_VF : WP_VF + units, 0 : 4 * width] = jnp.concatenate([aw[2], df[0], df[1]], 1).astype(BF)
    out[WP_SD : WP_SD + 3 * units, 0:width] = sw[...].T.astype(BF)
    out[WP_SD : WP_SD + width, 256 : 256 + units] = ds[...].astype(BF)
    out[WP_SD : WP_SD + units, 384 : 384 + width] = ds[...].T.astype(BF)
    parts = split3(gb[...])
    small = jnp.concatenate([p.astype(F32) for p in parts] + [jnp.zeros((10, gb.shape[1]), F32)], 0)
    out[WP_B : WP_B + 16, 0 : 3 * units] = small.astype(BF)


def weights_kernel(
    meta, own, other, tw, msg,
    o_md, o_mc, o_q, o_kvm, o_kvc, o_kvct, o_f, o_ft, o_d, o_dt, o_tt, o_gin, o_gst,
):
    width = tw.shape[0]
    units = width // 2
    gates = 3 * units

    def rows_padded(x):
        zero = jnp.zeros((PAD - units, x.shape[1]), F32)
        parts = []
        for k in range(x.shape[0] // units):
            parts += [x[k * units : (k + 1) * units], zero]
        return jnp.concatenate(parts, 0)

    def put(h, w):
        mw = w[0:gates, 0 : 4 * width].astype(F32)
        o_mc[h] = mw[:, 2 * width : 3 * width].astype(BF)
        mw = rows_padded(mw)
        o_md[h] = jnp.concatenate(
            [mw[:, width : 2 * width], jnp.zeros((3 * PAD, 256 - width), F32)], 1
        ).astype(BF)
        rest = jnp.concatenate([mw[:, :width], mw[:, 2 * width :]], 1).astype(BF)
        small = w[WP_B : WP_B + 16, 0:gates].astype(F32)
        bias = (small[0:2] + small[2:4]) + small[4:6]
        bias = jnp.concatenate([bias, jnp.zeros((6, gates), F32)], 0).T
        bias = rows_padded(bias)
        state = rows_padded(w[WP_SD : WP_SD + gates, 0:width].astype(F32)).astype(BF)
        o_gin[h] = nn(rest, msg[...]) + bias[:, 0:1]
        o_gst[h] = nn(state, msg[0:width]) + bias[:, 1:2]
        query = rows_padded(w[WP_QK : WP_QK + units, 0 : 2 * width].astype(F32))
        zero = jnp.zeros((PAD, PAD - units), F32)
        o_q[h] = jnp.concatenate(
            [query[:, :units], zero, query[:, units:width], zero, query[:, width:]], 1
        ).astype(BF)
        key = w[WP_QK : WP_QK + units, 2 * width : 4 * width].astype(F32)
        value = w[WP_VF : WP_VF + units, 0 : 2 * width].astype(F32)
        pair = rows_padded(jnp.concatenate([key, value], 0))
        wide = jnp.concatenate([pair[:, :width], jnp.zeros((2 * PAD, 256 - width), F32)], 1)
        rows = pl.ds(pl.multiple_of(h * 2 * PAD, 2 * PAD), 2 * PAD)
        o_kvm[rows] = wide.astype(BF)
        code = pair[:, width:]
        o_kvc[rows] = code.astype(BF)
        o_kvct[h] = code.T.astype(BF)
        for i in range(2):
            dense = w[WP_VF : WP_VF + units, (2 + i) * width : (3 + i) * width].astype(F32)
            dense = rows_padded(dense)
            o_f[i, h] = dense.astype(BF)
            o_ft[i, h] = dense.T.astype(BF)

    def second(one, two):
        o_d[...] = jnp.concatenate(
            [w[WP_SD : WP_SD + width, 256 : 256 + units].astype(F32) for w in (one, two)], 1
        ).astype(BF)
        o_dt[...] = jnp.concatenate(
            [w[WP_SD : WP_SD + units, 384 : 384 + width].astype(F32) for w in (one, two)], 0
        ).astype(BF)

    @pl.when(meta[1] == 0)
    def _():
        second(own, other)

    @pl.when(meta[1] == 1)
    def _():
        second(other, own)

    put(meta[1], own)
    put(1 - meta[1], other)
    o_tt[...] = tw[...].T.astype(BF)


def step_kernel(
    planes, use_table,
    meta, idx, wcount, own_piece, z_pieces, xy_pieces, far_a, far_b, late_in,
    delta_all, ndelta_all, tcol, w_tt, gathered_in,
    o_fresh, o_own, o_other, o_live,
    sems, mem_all, late, coarse, fine, near, qin, emb, keyt, count, stat, norm,
    scores, probs, fresh_s, gates, acc_m, tgrad,
):
    (
        srct, msg, sin_d, w_md, w_mc, w_q, w_kvm, w_kvct, w_f, w_ft, w_d, w_dt, gin0, gst,
        code_n, w_kvc, sin_n,
    ) = late
    width, events = sin_d.shape
    units = width // 2
    nbrs = ndelta_all.shape[0]
    groups, full, wide_cols = mem_all.shape
    per_group = wide_cols // events
    lookups = (nbrs + 1) * events
    scale = 1.0 / math.sqrt(units)
    row_pos, head = meta[0], meta[1]
    hi_rows = count.shape[0]
    own_cols = pl.ds(pl.multiple_of(head * events, events), events)

    copies = []

    def start(src, dst):
        copy = pltpu.make_async_copy(src, dst, sems.at[len(copies)])
        copy.start()
        copies.append(copy)

    def bring(src, row, half, first, last):
        lanes = pl.ds(pl.multiple_of((lax.rem(row, 2) * 2 + half) * events, events), events)
        start(src, mem_all.at[lax.div(row, 2), pl.ds(first, last - first), lanes])

    cut = z_pieces[0].shape[1]
    first_copy = []
    for r in range(groups):
        first_copy.append(len(copies))
        for e, d in (divmod(2 * r, PLANE), divmod(2 * r + 1, PLANE)):
            row = row_pos ^ (e * PLANE + d)
            for k in range(2):
                half = head ^ k
                if e == 0 and d == 0:
                    bring(own_piece[k], row, half, 0, full)
                elif e == 0:
                    bring(xy_pieces[0][d - 1] if k == 0 else xy_pieces[1].at[d - 1], row, half, 0, full)
                else:
                    bring(z_pieces[k].at[e - 1] if d == 0 else far_a[k][d - 1].at[e - 1], row, half, 0, cut)
                    bring(far_b[k][e - 1].at[d], row, half, cut, full)
    n_memory = len(copies)
    first_copy.append(n_memory)
    for src, dst in zip(late_in, late):
        copies.append(pltpu.make_async_copy(src, dst, sems.at[len(copies)]))
    n_late = len(copies)

    def start_late():
        for copy in copies[n_memory:n_late]:
            copy.start()

    def group_here(r):
        for copy in copies[first_copy[r] : first_copy[r + 1]]:
            copy.wait()
        return lax.div(row_pos, 2) ^ r

    def each_group(work):
        if groups <= 8:
            for r in range(groups):
                g = group_here(r)
                if r == groups - 1:
                    start_late()
                work(g)
        else:
            for r in range(groups):
                group_here(r)
            start_late()
            lax.fori_loop(0, groups, lambda g, s: (work(g), s)[1], 0)

    count[...] = jnp.zeros_like(count)
    norm[...] = jnp.zeros_like(norm)
    stat[...] = jnp.zeros_like(stat)
    target_t = w_tt[...]

    def keys_of(g):
        return nn(target_t, mem_all[g, 0:width]).astype(BF)

    def per_group_rows(g, table):
        x = mem_all[g]
        wide = x.astype(F32)
        keys = keys_of(g)
        if use_table:
            keyt[g, 0:width] = keys
        keys = keys.astype(F32)
        norm[0:1] = jnp.maximum(norm[0:1], jnp.sum(keys * keys, 0, keepdims=True))
        ids = (wide[width : width + 1] * LO_BASE + wide[width + 1 : width + 2]).astype(jnp.int32)
        hot = []
        for size, part in ((hi_rows, ids // COLS), (COLS, ids % COLS)):
            place = lax.broadcasted_iota(jnp.int32, (size, wide_cols), 0).astype(F32)
            hot.append(jnp.where(place == part.astype(F32), 1.0, 0.0).astype(BF))
        count[...] += nt(hot[0], hot[1])
        here = wide[width + 2 : width + 3] * LO_BASE + wide[width + 3 : width + 4]
        for k in range(0, per_group, 2):
            stat[0:1, :] += here[:, k * events : k * events + 128]
        if table is not None:
            turned = wide.T
            base = pl.multiple_of(g * 2 * wide_cols, 2 * wide_cols)
            table[pl.ds(base, wide_cols, stride=2), :] = turned[:, :128]
            table[pl.ds(base + 1, wide_cols, stride=2), :] = jnp.concatenate(
                [turned[:, 128:], jnp.zeros((wide_cols, 256 - full), F32)], 1
            )

    def gather_rows(table, gathered):
        each_group(lambda g: per_group_rows(g, table))
        unroll = 32

        def body(i, carry):
            for u in range(unroll):
                k = i * unroll + u
                gathered[pl.ds(pl.multiple_of(2 * k, 2), 2), :] = table[
                    pl.ds(pl.multiple_of(idx[k], 2), 2), :
                ]
            return carry

        lax.fori_loop(0, lookups // unroll, body, 0)
        for j in range(nbrs + 1):
            low = gathered[pl.ds(2 * j * events, events, stride=2), :]
            high = gathered[pl.ds(2 * j * events + 1, events, stride=2), :]
            near[pl.ds(j * events, events), :] = jnp.concatenate([low, high], 1).astype(BF)

    if use_table:
        pl.run_scoped(
            gather_rows,
            pltpu.VMEM((2 * groups * wide_cols, 128), F32),
            pltpu.VMEM((2 * lookups, 128), F32),
        )
    else:
        each_group(lambda g: per_group_rows(g, None))
        near = gathered_in

    def count_lines(g, keys):
        at = g * (wide_cols // COLS)
        line = jnp.concatenate([count[pl.ds(at + k, 1), :] for k in range(wide_cols // COLS)], 1)
        line = jnp.where(line > 0.5, jnp.log(jnp.maximum(line, 1.0)), -1e30)
        parts = split3(line)
        place = lax.broadcasted_iota(jnp.int32, (16, wide_cols), 0)
        first = full - 16
        tail = jnp.where(place >= width - first, 0.0, keys.astype(F32))
        for k in range(3):
            tail = jnp.where(place == width - first + k, parts[k].astype(F32), tail)
        return tail.astype(BF)

    if use_table:

        def add_lines(g, carry):
            keyt[g, full - 16 : full] = count_lines(g, keyt[g, full - 16 : full])
            return carry

        lax.fori_loop(0, groups, add_lines, 0)

    def keys_with_lines(g):
        if use_table:
            return keyt[g]
        keys = jnp.concatenate([keys_of(g).astype(F32), jnp.zeros((full - width, wide_cols), F32)], 0)
        keys = keys.astype(BF)
        return jnp.concatenate([keys[: full - 16], count_lines(g, keys[full - 16 :])], 0)

    live_rows = stat[0:1, 0:1]

    def rest(kvt, pair):
        for copy in copies[n_memory : n_late - 3]:
            copy.wait()
        dest = near[pl.ds(nbrs * events, events), :]
        dest_t = dest.astype(F32).T[:width]
        dest_key = nn(target_t, dest_t.astype(BF)).astype(BF)
        for h in range(2):
            gate_in = gin0[h] + nt(w_md[h], dest)
            gate_state = gst[h]
            reset = sigmoid(gate_in[:PAD] + gate_state[:PAD])
            update = sigmoid(gate_in[PAD : 2 * PAD] + gate_state[PAD : 2 * PAD])
            state_c = gate_state[2 * PAD :]
            candidate = jnp.tanh(gate_in[2 * PAD :] + reset * state_c)
            for k, v in enumerate((reset, update, candidate, state_c)):
                gates[h, k] = v
            fresh = (1.0 - update) * candidate + update * srct[h]
            o_fresh[h] = fresh
            qin[h * PAD : (h + 1) * PAD] = fresh
        zero_sin, zero_cos = sin_cos(tcol[...])
        qin[2 * PAD :] = jnp.broadcast_to(zero_cos[:, 1:2], (width, events))
        query_in = qin[...].astype(BF)
        copies[n_late - 3].wait()
        copies[n_late - 2].wait()

        def project(j, carry):
            cols = pl.ds(pl.multiple_of(j * events, events), events)
            kvt[:, cols] = nt(w_kvm[...], near[cols, :]) + nn(w_kvc[...], code_n[:, cols])
            return carry

        lax.fori_loop(0, nbrs, project, 0)
        attended_low = []
        for h in range(2):
            key_at, value_at = h * 2 * PAD, h * 2 * PAD + PAD
            queries = nn(w_q[h], query_in)
            fresh_s[h] = queries
            for j in range(nbrs):
                cols = pl.ds(j * events, events)
                scores[j : j + 1] = (
                    jnp.sum(queries * kvt[key_at : key_at + PAD, cols], 0, keepdims=True) * scale
                )
            score = scores[0:nbrs]
            grown = jnp.exp(score - jnp.max(score, 0, keepdims=True))
            prob = grown / jnp.sum(grown, 0, keepdims=True)
            probs[h, 0:nbrs] = prob
            total = jnp.zeros((PAD, events), F32)
            for j in range(nbrs):
                cols = pl.ds(j * events, events)
                total = total + prob[j : j + 1] * kvt[value_at : value_at + PAD, cols]
            attended_low.append(total.astype(BF))
        fresh_lows = [qin[h * PAD : (h + 1) * PAD].astype(BF) for h in range(2)]
        hidden = (nn(w_ft[0, 0], attended_low[0]) + nn(w_ft[0, 1], attended_low[1])) + (
            nn(w_ft[1, 0], fresh_lows[0]) + nn(w_ft[1, 1], fresh_lows[1])
        )
        sigmoid_h = sigmoid(hidden)
        mixed_low = (hidden * sigmoid_h).astype(BF)
        emb[...] = nn(w_dt[...], mixed_low)
        emb_low = emb[...].astype(BF)
        ones_line = (lax.broadcasted_iota(jnp.int32, (full - width, events), 0) < 3).astype(F32)
        emb_aug = jnp.concatenate([LOGIT_SCALE * emb_low.astype(F32), ones_line], 0)
        emb_rows = emb_aug.T.astype(BF)
        emb_norm = jnp.max(jnp.sum(emb[...] * emb[...], 0, keepdims=True))
        bound = LOGIT_SCALE * LOGIT_SCALE * emb_norm * jnp.max(norm[0:1])
        own_logit = LOGIT_SCALE * jnp.sum(
            emb_low.astype(F32) * dest_key.astype(F32), 0, keepdims=True
        )

        def soft_section(acc, top, total):
            total[...] = jnp.zeros_like(total)
            acc[...] = jnp.zeros_like(acc)
            small = bound < SAFE_LOGIT * SAFE_LOGIT

            @pl.when(small)
            def _():
                top[...] = jnp.zeros_like(top)

                def body(g, carry):
                    grown = jnp.exp(nn(emb_rows, keys_with_lines(g)))
                    lanes = grown[:, 0:128]
                    for k in range(1, wide_cols // 128):
                        lanes = lanes + grown[:, k * 128 : (k + 1) * 128]
                    total[...] += lanes
                    acc[...] += nt(grown.astype(BF), mem_all[g])
                    return carry

                lax.fori_loop(0, groups, body, 0)
                total[...] = jnp.broadcast_to(jnp.sum(total[...], 1, keepdims=True), total.shape)

            @pl.when(jnp.logical_not(small))
            def _():
                top[...] = jnp.full_like(top, -1e30)

                def body(g, carry):
                    logits = nn(emb_rows, keys_with_lines(g))
                    old = top[:, 0:1]
                    new = jnp.maximum(old, jnp.max(logits, 1, keepdims=True))
                    grown = jnp.exp(logits - new)
                    fade = jnp.exp(old - new)
                    total[...] = total[...] * fade + jnp.sum(grown, 1, keepdims=True)
                    top[...] = jnp.broadcast_to(new, top.shape)
                    acc[...] = acc[...] * fade + nt(grown.astype(BF), mem_all[g])
                    return carry

                lax.fori_loop(0, groups, body, 0)

            acc_m[...] = (acc[...] / total[:, 0:1]).T
            probs[2] = jnp.broadcast_to(top[:, 0:1] + jnp.log(total[:, 0:1]), (events, 128)).T[:16]

        pl.run_scoped(
            soft_section,
            pltpu.VMEM((events, full), F32),
            pltpu.VMEM((events, 128), F32),
            pltpu.VMEM((events, 128), F32),
        )
        log_total = probs[2, 0:1]
        position = lax.broadcasted_iota(jnp.int32, (1, events), 1) + head * events
        live = (position < wcount[0]).astype(F32)
        loss = jnp.sum((log_total - own_logit) * live, 1, keepdims=True)
        weight = live / live_rows
        own_prob = jnp.exp(own_logit - log_total)
        own_grad = ((own_prob - 1.0) * weight).astype(BF).astype(F32) - own_prob * weight
        mean_mem = acc_m[:width]
        spread = weight * mean_mem + own_grad * dest_t
        parts = split3(spread)
        target_grad = LOGIT_SCALE * (nt(parts[0], emb_low) + nt(parts[1], emb_low) + nt(parts[2], emb_low))
        parts = split3(mean_mem)
        mean_key = nn(target_t, parts[0]) + nn(target_t, parts[1]) + nn(target_t, parts[2])
        emb_grad = LOGIT_SCALE * (weight * mean_key + own_grad * dest_key.astype(F32))

        coarse[...] = jnp.zeros_like(coarse)
        fine[...] = jnp.zeros_like(fine)
        blocks = state_blocks(units)
        quarter = units // 2

        def slot(h):
            return h ^ head

        emb_grad_low = emb_grad.astype(BF)
        mixed_grad = nn(w_d[...], emb_grad_low)
        second = nt(mixed_low, emb_grad_low)
        hidden_grad = (mixed_grad * sigmoid_h * (1.0 + hidden * (1.0 - sigmoid_h))).astype(BF)
        for h in range(2):
            place = slot(h)
            for i, v in enumerate((attended_low[h], fresh_lows[h])):
                fine[place, units:width, (2 + i) * width : (3 + i) * width] = nt(v, hidden_grad)[:units]
            for k in range(2):
                fine[place, ROW_T : ROW_T + quarter, k * width : (k + 1) * width] = target_grad[
                    h * units + k * quarter : h * units + (k + 1) * quarter
                ]
            for k in range(4):
                at = 2 * width + k * units
                fine[place, ROW_T : ROW_T + quarter, at : at + units] = second[
                    k * quarter : (k + 1) * quarter, h * units : (h + 1) * units
                ]

        copies[n_late - 1].wait()
        tgrad[...] = jnp.zeros_like(tgrad)
        query_lows = []
        prob_terms = []
        att_grads = []
        for h in range(2):
            value_at = h * 2 * PAD + PAD
            att_grad = nn(w_f[0, h], hidden_grad)
            prob = probs[h, 0:nbrs]
            for j in range(nbrs):
                cols = pl.ds(j * events, events)
                scores[j : j + 1] = jnp.sum(
                    att_grad * kvt[value_at : value_at + PAD, cols], 0, keepdims=True
                )
            prob_grad = scores[0:nbrs]
            prob_terms.append(prob * (prob_grad - jnp.sum(prob * prob_grad, 0, keepdims=True)))
            att_grads.append(att_grad)
            total = jnp.zeros((PAD, events), F32)
            key_at = h * 2 * PAD
            for j in range(nbrs):
                cols = pl.ds(j * events, events)
                total = total + prob_terms[h][j : j + 1] * kvt[key_at : key_at + PAD, cols]
            query_lows.append((total * scale).astype(BF))
        for j in range(nbrs):
            cols = pl.ds(j * events, events)
            pieces = []
            for h in range(2):
                pieces += [
                    (prob_terms[h][j : j + 1] * scale) * fresh_s[h], probs[h, j : j + 1] * att_grads[h],
                ]
            pair_j = jnp.concatenate(pieces, 0).astype(BF)
            pair[:, cols] = pair_j
            code_grad = nn(w_kvct[0], pair_j[: 2 * PAD]) + nn(w_kvct[1], pair_j[2 * PAD :])
            slope = sin_n[:, cols].astype(F32) * code_grad
            tgrad[1, :width] -= slope
            tgrad[0, :width] -= slope * ndelta_all[j : j + 1, own_cols]
        near_grad = nn(pair[...], near[pl.ds(0, nbrs * events), :])
        code_wgrad = nt(pair[...], code_n[...])
        for h in range(2):
            place = slot(h)
            base = h * 2 * PAD
            query_grad = nt(query_lows[h], query_in)
            fine[place, 0:units, 0:units] = query_grad[:units, 0:units]
            fine[place, 0:units, units:width] = query_grad[:units, PAD : PAD + units]
            fine[place, 0:units, width : 2 * width] = query_grad[:units, 2 * PAD :]
            for k, (row, lane) in enumerate(((0, 2 * width), (units, 0))):
                at = base + k * PAD
                fine[place, row : row + units, lane : lane + width] = near_grad[
                    at : at + units, :width
                ]
                fine[place, row : row + units, lane + width : lane + 2 * width] = code_wgrad[
                    at : at + units
                ]
        query_in_grad = tn(w_q[0], query_lows[0]) + tn(w_q[1], query_lows[1])
        zero_term = zero_sin[:, 1:2] * query_in_grad[2 * PAD :]
        tgrad[1, :width] -= zero_term

        def send_fine(k):
            start(fine.at[0, pl.ds(k * FINE, FINE)], o_own.at[k, pl.ds(COARSE, FINE)])

        for k in range(3):
            send_fine(k)

        code_dt_grad = jnp.zeros((width, events), F32)
        ones = jnp.ones((8, events), BF)
        for h in range(2):
            place = slot(h)
            reset, update, candidate, state_c = (gates[h, k] for k in range(4))
            fresh_grad = nn(w_f[1, h], hidden_grad) + query_in_grad[h * PAD : (h + 1) * PAD]
            own_state = srct[h]
            candidate_pre = fresh_grad * (1.0 - update) * (1.0 - candidate * candidate)
            update_pre = fresh_grad * (own_state - candidate) * update * (1.0 - update)
            reset_pre = candidate_pre * state_c * reset * (1.0 - reset)
            last_pre = candidate_pre * reset
            shared = [reset_pre[:units], update_pre[:units]]
            in_grad = jnp.concatenate(shared + [candidate_pre[:units]], 0).astype(BF)
            state_grad = jnp.concatenate(shared + [last_pre[:units]], 0).astype(BF)
            gate_rows = 3 * units
            coarse[place, 0:gate_rows, width : 2 * width] = nn(in_grad, dest)[:, :width]
            rest_grad = nt(in_grad, msg[...])
            coarse[place, 0:gate_rows, 0:width] = rest_grad[:, :width]
            coarse[place, 0:gate_rows, 2 * width : 4 * width] = rest_grad[:, width:]
            state_w = nt(msg[0:width], state_grad)
            coarse[place, 0:width, 4 * width : 4 * width + gate_rows - 256] = state_w[:, 256:]
            for k, (first, last) in enumerate(blocks):
                coarse[place, gate_rows : gate_rows + last - first, k * 256 : (k + 1) * 256] = state_w[
                    first:last, 0:256
                ]
            fine[place, ROW_B : ROW_B + 1, 0:gate_rows] = nt(ones, in_grad)[0:1]
            fine[place, ROW_B + 1 : ROW_B + 2, 0:gate_rows] = nt(ones, state_grad)[0:1]
            code_dt_grad = code_dt_grad + tn(w_mc[h], in_grad)
        slope = sin_d[...] * code_dt_grad
        tgrad[1, :width] -= slope
        tgrad[0, :width] -= slope * delta_all[:, own_cols]
        ones_f = jnp.ones((8, events), F32)
        for i in range(2):
            line = lax.dot_general(
                ones_f, tgrad[i, :width], (((1,), (1,)), ((), ())),
                precision=lax.Precision.HIGHEST, preferred_element_type=F32,
            )[0:1]
            for place in range(2):
                fine[place, ROW_B + 2 + i : ROW_B + 3 + i, 0:width] = line
        for place in range(2):
            fine[place, ROW_B + 4 : ROW_B + 5, 0:128] = jnp.broadcast_to(loss, (1, 128))
        o_live[...] = jnp.broadcast_to(stat[0:1, :], o_live.shape)
        send_fine(3)
        for k in range(4):
            start(coarse.at[0, pl.ds(k * COARSE, COARSE)], o_own.at[k, pl.ds(0, COARSE)])
        for k in range(4):
            rows_c, rows_f = pl.ds(k * COARSE, COARSE), pl.ds(k * FINE, FINE)
            to_half_wire(o_other.at[k], jnp.concatenate([coarse[1, rows_c], fine[1, rows_f]], 0))
        for copy in copies[n_late:]:
            copy.wait()

    pl.run_scoped(
        rest,
        pltpu.VMEM((4 * PAD, nbrs * events), F32),
        pltpu.VMEM((4 * PAD, nbrs * events), BF),
    )


COARSE, FINE, LANES = 80, 64, 768
ROWS = COARSE + FINE
EXTRA = 16
ROW_T, ROW_B = 192, 240


def state_blocks(units):
    room = 4 * COARSE - 3 * units
    return [(k * room, min((k + 1) * room, 2 * units)) for k in range(3)]


def to_half_wire(out, value):
    high = value.astype(BF)
    out[0:ROWS] = high
    out[ROWS:] = (value - high.astype(F32))[ROWS - EXTRA :].astype(BF)


def from_half_wire(w):
    high = w[0:ROWS].astype(F32)
    last = high[ROWS - EXTRA :] + w[ROWS:].astype(F32)
    return jnp.concatenate([high[: ROWS - EXTRA], last], 0)


def to_wire(out, value):
    high = value.astype(BF)
    out[0:ROWS] = high
    out[ROWS:] = (value - high.astype(F32)).astype(BF)


def from_wire(w):
    return w[0:ROWS].astype(F32) + w[ROWS:].astype(F32)


def first_sum_kernel(bits, own, got, o_keep, o_send):
    for k in range(2):
        q = bits[0] * 2 + k
        o_keep[k] = own[q] + from_half_wire(got[q])
        q = (1 - bits[0]) * 2 + k
        to_half_wire(o_send.at[k], own[q] + from_half_wire(got[q]))


def second_sum_kernel(bits, keep, got, o_keep, o_send):
    q = bits[1]
    o_keep[...] = keep[q] + from_half_wire(got[q])
    q = 1 - bits[1]
    to_half_wire(o_send, keep[q] + from_half_wire(got[q]))


def third_sum_kernel(bits, keep, got, o_keep, o_send):
    half = ROWS // 2
    total = keep[...] + from_half_wire(got[...])
    for b in range(2):

        @pl.when(bits[2] == b)
        def _(b=b):
            o_keep[...] = total[b * half : (b + 1) * half]
            eighth_wire(o_send, total[(1 - b) * half : (2 - b) * half])


def eighth_wire(out, value):
    half = ROWS // 2
    high = value.astype(BF).astype(F32)
    out[...] = jnp.concatenate([high, value - high], 0).astype(BF)


def fourth_sum_kernel(keep, got, o_send):
    half = ROWS // 2
    wide = got[...].astype(F32)
    eighth_wire(o_send, keep[...] + (wide[0:half] + wide[half:]))


def eighth_sum_kernel(one, two, o_send):
    half = ROWS // 2
    a, b = one[...].astype(F32), two[...].astype(F32)
    eighth_wire(o_send, (a[0:half] + a[half:]) + (b[0:half] + b[half:]))


def join_kernel(bits, one, two, o_send):
    half = ROWS // 2
    a, b = one[...].astype(F32), two[...].astype(F32)
    first = jnp.where(bits[2] == 0, a, b)
    second = jnp.where(bits[2] == 0, b, a)
    o_send[...] = jnp.concatenate([first[:half], second[:half], first[half:], second[half:]], 0).astype(BF)


def quarter_of(bits, k):
    one = bits[0] if k < 2 else 1 - bits[0]
    two = bits[1] if k % 2 == 0 else 1 - bits[1]
    return one * 2 + two


def shared_kernel(bits, w0, w1, w2, w3, out):
    for k, w in enumerate((w0, w1, w2, w3)):

        @pl.when(quarter_of(bits, k) == 3)
        def _(w=w):
            out[0:FINE] = w[COARSE:ROWS]
            out[FINE:] = w[ROWS + COARSE :]


def adam_kernel(bits, w0, w1, w2, w3, *refs):
    params, outs = refs[:18], refs[18:36]
    coarse, fine = refs[36:]
    for k, w in enumerate((w0, w1, w2, w3)):
        q = quarter_of(bits, k)
        value = from_wire(w[...])
        coarse[pl.ds(pl.multiple_of(q * COARSE, COARSE), COARSE)] = value[0:COARSE]
        fine[pl.ds(pl.multiple_of(q * FINE, FINE), FINE)] = value[COARSE:]
    units, gates = params[15].shape[1], params[3].shape[1]
    width = 2 * units

    def step(which, at, gradient):
        values = [params[3 * which + i][at] for i in range(3)]
        for i, v in enumerate(adam_step(*values, gradient)):
            outs[3 * which + i][at] = v

    every = (slice(None), slice(None))
    step(0, every, coarse[0:gates, 0 : 4 * width])
    for k, (first, last) in enumerate(state_blocks(units)):
        step(
            1, (slice(first, last), slice(0, 256)),
            coarse[gates : gates + last - first, k * 256 : (k + 1) * 256],
        )
    step(1, (slice(None), slice(256, gates)), coarse[0:width, 4 * width : 4 * width + gates - 256])
    step(2, every, fine[ROW_B : ROW_B + 2, 0:gates])
    step(3, 0, fine[0:units, 0 : 2 * width])
    step(3, 1, fine[0:units, 2 * width : 4 * width])
    step(3, 2, fine[units:width, 0 : 2 * width])
    for i in range(2):
        step(4, (slice(None), i), fine[units:width, (2 + i) * width : (3 + i) * width])
    quarter = units // 2
    for k in range(4):
        at = 2 * width + k * units
        step(5, (slice(k * quarter, (k + 1) * quarter), slice(None)), fine[ROW_T : ROW_T + quarter, at : at + units])


def shared_adam_kernel(meta, own, other, *refs):
    params, outs, o_loss = refs[:6], refs[6:12], refs[12]
    width = params[0].shape[0]
    quarter = width // 4

    def step(which, at, gradient):
        values = [params[3 * which + i][at] for i in range(3)]
        for i, v in enumerate(adam_step(*values, gradient)):
            outs[3 * which + i][at] = v

    def run(first, second):
        parts = [w[0:FINE].astype(F32) + w[FINE:].astype(F32) for w in (first, second)]
        for h in range(2):
            for k in range(2):
                at = (h * 2 + k) * quarter
                step(
                    0, (slice(at, at + quarter), slice(None)),
                    parts[h][0:quarter, k * width : (k + 1) * width],
                )
        row = ROW_B - 3 * FINE
        step(1, (slice(None), slice(None)), parts[0][row + 2 : row + 4, 0:width])
        o_loss[...] = jnp.broadcast_to(parts[0][row + 4 : row + 5, 0:128], o_loss.shape)

    @pl.when(meta[1] == 0)
    def _():
        run(own, other)

    @pl.when(meta[1] == 1)
    def _():
        run(other, own)


def memory_kernel(mem, fresh, src, wcount, out):
    units, rows = mem.shape
    pick = (lax.broadcasted_iota(jnp.int32, (rows, rows), 1) == src[...]).astype(BF)
    parts = split3(fresh[0:units])
    moved = nn(parts[0], pick) + nn(parts[1], pick) + nn(parts[2], pick)
    alive = (lax.broadcasted_iota(jnp.int32, (16, rows), 1) < wcount[0]).astype(BF)
    hit = nn(alive, pick)[0:1] > 0.5
    out[...] = jnp.where(hit, moved, mem[...])


def adam_step(master, moment, square, gradient):
    moment_new = BETA_ONE * moment + (1.0 - BETA_ONE) * gradient
    square_new = BETA_TWO * square + (1.0 - BETA_TWO) * gradient * gradient
    master_new = master - RATE * (moment_new / (1.0 - BETA_ONE**STEP)) / (
        jnp.sqrt(square_new / (1.0 - BETA_TWO**STEP)) + EPSILON
    )
    return (master_new, moment_new, square_new)


def axis_orders(n_row):
    bits = []
    step = PLANE
    while step < n_row:
        bits.append(step)
        step *= 2
    first = [1, 2] + bits
    second = bits[:2] + [1, 2] + bits[2:]
    return list(zip(first, second))


def flips(count, step):
    return [(i, i ^ step) for i in range(count)]


def per_device(
    n_row,
    memory, sources, dest_ids, neighbours, delta_t, nbr_delta, edge_feat, window_count,
    message_weight, message_weight_moment, message_weight_square,
    state_weight, state_weight_moment, state_weight_square,
    gate_bias, gate_bias_moment, gate_bias_square,
    time_param, time_param_moment, time_param_square,
    attend_weight, attend_weight_moment, attend_weight_square,
    dense_first, dense_first_moment, dense_first_square,
    dense_second, dense_second_moment, dense_second_square,
    target_weight, target_weight_moment, target_weight_square,
):
    rows, width = memory.shape
    units = width // 2
    events = rows // 2
    nbrs = neighbours.shape[1]
    planes = n_row // PLANE
    total_rows = n_row * rows
    head = lax.axis_index("head")
    row = lax.axis_index("row")
    meta = jnp.stack([row, head]).astype(jnp.int32)

    def own(x, axis):
        return lax.dynamic_slice_in_dim(x, head * events, events, axis)

    def swap(x):
        return lax.ppermute(x, "head", [(0, 1), (1, 0)])

    def hop(x, step):
        return lax.ppermute(x, "row", flips(n_row, step))

    bf = functools.partial(shape, dtype=BF)
    full = -(-(width + 4) // 16) * 16

    mem_t = memory.T
    block = vmem_call(block_kernel, bf(full, events), "ssvv", micros=1)(
        meta, window_count, mem_t, dest_ids[None]
    )
    cut = 128
    near_z = [hop(block[:cut], e * PLANE) for e in range(1, planes)]
    near_xy = [hop(block, d) for d in range(1, PLANE)]
    mw, aw, gb = message_weight.T, attend_weight.transpose(0, 2, 1), gate_bias
    packed = vmem_call(pack_weights_kernel, bf(WP_ROWS, WP_LANES), "vvvvvv", limit=VMEM_SMALL, micros=2)(
        mw, state_weight, aw, dense_first, dense_second, gb
    )
    line_a = jnp.stack(near_z)
    plane_b = jnp.stack([block[cut:]] + [p[cut:] for p in near_xy])
    line_a, plane_b = lax.optimization_barrier((line_a, plane_b))
    packed, _ = lax.optimization_barrier((packed, line_a))
    packed_o = swap(packed)
    far_a = tuple(hop(line_a, d) for d in range(1, PLANE))
    far_b = tuple(hop(plane_b, e * PLANE) for e in range(1, planes))
    delta, ndelta, edge, tcol, packed_o, _ = lax.optimization_barrier(
        (delta_t[None], nbr_delta.T, edge_feat.T, time_param.T, packed_o, plane_b)
    )
    code_shapes = (
        shape(2, PAD, events), bf(3 * width, events), shape(width, events),
        bf(width, nbrs * events), bf(width, nbrs * events),
    )
    srct, msg, sin_d, code_n, sin_n = vmem_call(codes_kernel, code_shapes, "svvvvvv", micros=9)(
        meta, mem_t, sources, delta, ndelta, tcol, edge
    )
    w_shapes = (
        bf(2, 3 * PAD, 256), bf(2, 3 * units, width), bf(2, PAD, 2 * PAD + width),
        bf(4 * PAD, 256), bf(4 * PAD, width), bf(2, width, 2 * PAD),
        bf(2, 2, PAD, width), bf(2, 2, width, PAD), bf(width, width), bf(width, width),
        bf(width, width), shape(2, 3 * PAD, events), shape(2, 3 * PAD, events),
    )
    w_md, w_mc, w_q, w_kvm, w_kvc, w_kvct, w_f, w_ft, w_d, w_dt, w_tt, gin0, gst = vmem_call(weights_kernel, w_shapes, "svvvv", micros=6)(
        meta, packed, packed_o, target_weight, msg
    )

    far_a, far_b, _ = lax.optimization_barrier((far_a, far_b, w_md))
    block, line_a, near_xy, _ = lax.optimization_barrier((block, line_a, near_xy, srct))
    own_piece = (block, swap(block))
    z_pieces = (line_a, swap(line_a))
    xy_pieces = (tuple(near_xy), swap(jnp.stack(near_xy)))
    far_a = (far_a, tuple(swap(p) for p in far_a))
    far_b = (far_b, tuple(swap(p) for p in far_b))

    index = jnp.concatenate([own(neighbours.T, 1).reshape(-1), own(dest_ids, 0)])
    use_table = total_rows <= TABLE_ROWS_MAX
    lookups = (nbrs + 1) * events
    if use_table:
        gathered = tcol
    else:
        parts = {}
        for k in range(2):
            parts[0, 0, k] = own_piece[k]
            for e in range(1, planes):
                parts[e, 0, k] = jnp.concatenate([z_pieces[k][e - 1], far_b[k][e - 1][0]], 0)
            for d in range(1, PLANE):
                parts[0, d, k] = xy_pieces[k][d - 1]
                for e in range(1, planes):
                    parts[e, d, k] = jnp.concatenate([far_a[k][d - 1][e - 1], far_b[k][e - 1][d]], 0)
        table = jnp.stack([parts[e, d, k].T for e in range(planes) for d in range(PLANE) for k in range(2)])
        half = (index % rows) // events
        gathered = table[((index // rows) ^ row) * 2 + (half ^ head), index % events]
        gathered = jnp.pad(gathered, ((0, 0), (0, 256 - full)))
    hi_rows = total_rows // COLS
    wide_cols = 4 * events
    groups = total_rows // wide_cols
    late = (
        srct, msg, sin_d, w_md, w_mc, w_q, w_kvm, w_kvct, w_f, w_ft, w_d, w_dt, gin0, gst, code_n, w_kvc, sin_n,
    )
    n_copies = 2 * (1 + (planes - 1) + (PLANE - 1) * planes + (planes - 1) * PLANE) + len(late) + 8
    scratch = [
        pltpu.SemaphoreType.DMA((n_copies,)),
        pltpu.VMEM((groups, full, wide_cols), BF),
        tuple(pltpu.VMEM(x.shape, x.dtype) for x in late),
        pltpu.VMEM((2, 4 * COARSE, LANES), F32),
        pltpu.VMEM((2, 4 * FINE, LANES), F32),
        pltpu.VMEM((lookups if use_table else 16, 256), BF),
        pltpu.VMEM((2 * PAD + width, events), F32),
        pltpu.VMEM((width, events), F32),
        pltpu.VMEM((groups if use_table else 1, full, wide_cols), BF),
        pltpu.VMEM((hi_rows, COLS), F32),
        pltpu.VMEM((8, 128), F32),
        pltpu.VMEM((8, wide_cols), F32),
        pltpu.VMEM((16, events), F32),
        pltpu.VMEM((3, 16, events), F32),
        pltpu.VMEM((2, PAD, events), F32),
        pltpu.VMEM((2, 4, PAD, events), F32),
        pltpu.VMEM((full, events), F32),
        pltpu.VMEM((2, PAD * 2, events), F32),
    ]
    spaces = [
        "s", "s", "s", ["a", "a"], ["a", "a"], [["a"] * (PLANE - 1), "a"],
        [["a"] * (PLANE - 1)] * 2, [["a"] * (planes - 1)] * 2, ["a"] * len(late),
    ] + ["v"] * 5
    fresh, pack_own, pack_other, live = vmem_call(
        functools.partial(step_kernel, planes, use_table),
        (
            shape(2, PAD, events), shape(4, ROWS, LANES), bf(4, ROWS + EXTRA, LANES), shape(8, 128),
        ),
        spaces,
        scratch,
        VMEM_LIMIT if use_table else VMEM_WHOLE,
        micros=40,
        in_place=(shape(4, ROWS, LANES),),
    )(
        meta, 2 * index, window_count, own_piece, z_pieces, xy_pieces, far_a, far_b, late,
        delta, ndelta, tcol, w_tt, gathered,
    )

    fresh_own = lax.dynamic_index_in_dim(fresh, head, 0, False)
    fresh_sent = swap(lax.dynamic_index_in_dim(fresh, 1 - head, 0, False))
    both = jnp.where(
        head == 0,
        jnp.concatenate([fresh_own, fresh_sent], 1),
        jnp.concatenate([fresh_sent, fresh_own], 1),
    )
    base_cols = lax.dynamic_slice_in_dim(mem_t, head * units, units, 0)
    new_memory = vmem_call(memory_kernel, shape(units, rows), "vvvs", limit=VMEM_SMALL, micros=3)(
        base_cols, both, sources.reshape(rows, 1), window_count
    ).T

    orders = axis_orders(n_row)

    def joint_hop(x, steps):
        pairs = [(2 * i + c, 2 * (i ^ steps[c]) + c) for i in range(n_row) for c in range(2)]
        return lax.ppermute(x, ("row", "head"), pairs)

    bits = jnp.stack(
        [jnp.where(head == 0, (row // steps[0]) % 2, (row // steps[1]) % 2) for steps in orders[:3]]
    ).astype(jnp.int32)
    wire = bf(2 * ROWS, LANES)
    keep, send = vmem_call(
        first_sum_kernel, (shape(2, ROWS, LANES), bf(2, ROWS + EXTRA, LANES)), "svv", limit=VMEM_SMALL, micros=1
    )(bits, pack_own, swap(pack_other))
    keep, send = vmem_call(
        second_sum_kernel, (shape(ROWS, LANES), bf(ROWS + EXTRA, LANES)), "svv", limit=VMEM_SMALL, micros=1
    )(bits, keep, joint_hop(send, orders[0]))
    keep, send = vmem_call(
        third_sum_kernel, (shape(ROWS // 2, LANES), bf(ROWS, LANES)), "svv", limit=VMEM_SMALL, micros=1
    )(bits, keep, joint_hop(send, orders[1]))
    eighth = bf(ROWS, LANES)
    part = vmem_call(fourth_sum_kernel, eighth, "vv", limit=VMEM_SMALL, micros=1)(
        keep, joint_hop(send, orders[2])
    )
    for steps in orders[3:]:
        part = vmem_call(eighth_sum_kernel, eighth, "vv", limit=VMEM_SMALL, micros=1)(
            part, joint_hop(part, steps)
        )
    total = vmem_call(join_kernel, wire, "svv", limit=VMEM_SMALL, micros=1)(
        bits, part, joint_hop(part, orders[2])
    )
    second_q = joint_hop(total, orders[1])
    first_q = joint_hop(total, orders[0])
    last_q = joint_hop(second_q, orders[0])
    quarters = (total, second_q, first_q, last_q)
    shared = vmem_call(shared_kernel, bf(2 * FINE, LANES), "svvvv", limit=VMEM_SMALL, micros=1)(bits, *quarters)
    shared_o = swap(shared)

    def turned(x):
        return x.transpose(0, 2, 1)

    def middle(x):
        return x.transpose(1, 0, 2)

    views = (lambda x: x.T, lambda x: x, lambda x: x, turned, middle, lambda x: x)
    params = (
        message_weight, message_weight_moment, message_weight_square,
        state_weight, state_weight_moment, state_weight_square,
        gate_bias, gate_bias_moment, gate_bias_square,
        attend_weight, attend_weight_moment, attend_weight_square,
        dense_first, dense_first_moment, dense_first_square,
        dense_second, dense_second_moment, dense_second_square,
    )
    params = [views[i // 3](p) for i, p in enumerate(params)]
    stepped = vmem_call(
        adam_kernel, tuple(shape(*p.shape) for p in params), "svvvv" + "v" * 18,
        [pltpu.VMEM((4 * COARSE, LANES), F32), pltpu.VMEM((4 * FINE, LANES), F32)], limit=VMEM_ADAM, micros=4,
    )(bits, *quarters, *params)
    back = (lambda x: x.T, lambda x: x, lambda x: x, turned, middle, lambda x: x)
    stepped = [back[i // 3](p) for i, p in enumerate(stepped)]
    rest = (
        target_weight, target_weight_moment, target_weight_square,
        time_param, time_param_moment, time_param_square,
    )
    *others, loss = vmem_call(
        shared_adam_kernel, tuple(shape(*p.shape) for p in rest) + (shape(8, 128),), "svv" + "v" * 6, limit=VMEM_SMALL, micros=2
    )(meta, shared, shared_o, *rest)
    return (
        new_memory, loss[0, 0], live[0, 0], *stepped[:9], *others[3:], *stepped[9:], *others[:3],
    )


def solution(mesh):
    cols = P(None, "head")
    third = P(None, None, "head")
    middle = P(None, "head", None)
    by_row = P("row", None)
    in_specs = (
        (by_row, by_row, P("row"), by_row, P("row"), by_row, by_row, P("row"))
        + (cols,) * 9 + (P(),) * 3 + (third,) * 3 + (middle,) * 3 + (cols,) * 3 + (P(),) * 3
    )
    out_specs = (
        (P("row", "head"), P(), P())
        + (cols,) * 9 + (P(),) * 3 + (third,) * 3 + (middle,) * 3 + (cols,) * 3 + (P(),) * 3
    )
    return jax.shard_map(
        functools.partial(per_device, mesh.shape["row"]),
        mesh=mesh, in_specs=in_specs, out_specs=out_specs, check_vma=False,
    )
```
